32 devices in a mesh: dp: 4 (over y, core), ep: 2 (over x), seq: 4 (over z).
Axes of the slice: x: 2, y: 2, z: 4, core: 2. Of those that a mesh axis runs over, the one named last changes fastest.
Arguments:
- enc_input: bfloat16 [16, 1024, 512], P(('dp', 'ep'), 'seq'), may hold values from -6 to 6
- dec_input: bfloat16 [16, 1024, 512], P(('dp', 'ep'), 'seq'), may hold values from -6 to 6
- enc_segments: int32 [16, 1024], P(('dp', 'ep')), may hold values from 0 to 3, as said below
- dec_segments: int32 [16, 1024], P(('dp', 'ep')), may hold values from 0 to 3, as said below
- routes: int32 [3, 16, 1024, 2], P(None, ('dp', 'ep'), 'seq'), may hold values from 0 to 7, all different within a row
- enc_out_grad: bfloat16 [16, 1024, 512], P(('dp', 'ep'), 'seq'), may hold values from -6 to 6
- dec_out_grad: bfloat16 [16, 1024, 512], P(('dp', 'ep'), 'seq'), may hold values from -6 to 6
- enc_gains: bfloat16 [2, 512], replicated, may hold values from 0.5 to 1.5
- enc_biases: bfloat16 [2, 512], replicated, may hold values from -2 to 2
- dec_gains: bfloat16 [3, 512], replicated, may hold values from 0.5 to 1.5
- dec_biases: bfloat16 [3, 512], replicated, may hold values from -2 to 2
- kv_weights: bfloat16 [3, 512, 128], replicated, may hold values from -0.25 to 0.25
- router_weights: bfloat16 [3, 512, 8], replicated, may hold values from -0.1875 to 0.1875
- expert_weights: bfloat16 [3, 8, 512, 128], P(None, 'ep'), may hold values from -0.87 to 0.87
- ffn_in: bfloat16 [2, 512, 2048], replicated, may hold values from -0.25 to 0.25
- ffn_in_bias: bfloat16 [2, 2048], replicated, may hold values from -2 to 2
- ffn_out: bfloat16 [2, 2048, 512], replicated, may hold values from -0.125 to 0.125
- ffn_out_bias: bfloat16 [2, 512], replicated, may hold values from -2 to 2
Outputs:
- enc_output: bfloat16 [16, 1024, 512], P(('dp', 'ep'), 'seq')
- dec_output: bfloat16 [16, 1024, 512], P(('dp', 'ep'), 'seq')
- enc_input_grad: float32 [16, 1024, 512], P(('dp', 'ep'), 'seq')
- dec_input_grad: float32 [16, 1024, 512], P(('dp', 'ep'), 'seq')
- enc_gains_grad: float32 [2, 512], replicated
- enc_biases_grad: float32 [2, 512], replicated
- dec_gains_grad: float32 [3, 512], replicated
- dec_biases_grad: float32 [3, 512], replicated
- kv_weights_grad: float32 [3, 512, 128], replicated
- router_weights_grad: float32 [3, 512, 8], replicated
- expert_weights_grad: float32 [3, 8, 512, 128], P(None, 'ep')
- ffn_in_grad: float32 [2, 512, 2048], replicated
- ffn_in_bias_grad: float32 [2, 2048], replicated
- ffn_out_grad: float32 [2, 2048, 512], replicated
- ffn_out_bias_grad: float32 [2, 512], replicated
The draws below stay inside these ranges and needn't reach their ends.
Inputs may be any that keep to these rules, and one draw needn't show every extreme that they name: `enc_segments`: each row's document numbers never fall and take every value; one document of each row covers more than three quarters of the row. `dec_segments`: each row's document numbers never fall and take every value; one document of each row covers more than three quarters of the row.
All inputs are finite; a program needn't handle non-finite values.
Results may differ from the reference program's by a relative error of at most 0.024.
Values may be sent and summed in bfloat16 or wider, within the bound.
No kernel may reach another device: no remote copies, remote signals or barrier semaphores. Data moves between devices by JAX's collectives and lax.ppermute only.
A program may use at most 192 MiB of HBM per device.

```python
from functools import partial
import jax
import jax.numpy as jnp
from jax import lax

D = 512
FF = 2048
EXPERTS = 8
HD = 64
TOP = 2
ROW_LEN = 1024
SEGS = 4
ROWS_DEV = 2
SPAN = 256
ROWS = 16
CAP = 128
N_SEQ = 4


def segment_numbers(key):
    long_key, length_key = jax.random.split(key)
    longest = jax.random.randint(long_key, (ROWS, 1), 0, SEGS)
    short = jax.random.randint(length_key, (ROWS, SEGS), 1, ROW_LEN // (4 * SEGS) + 1)
    index = jnp.arange(SEGS, dtype=jnp.int32)[None, :]
    short = jnp.where(index == longest, 0, short)
    lengths = jnp.where(index == longest, ROW_LEN - jnp.sum(short, 1, keepdims=True), short)
    ends = jnp.cumsum(lengths, 1)
    places = jnp.arange(ROW_LEN, dtype=jnp.int32)
    return jnp.sum((places[None, :, None] >= ends[:, None, :]).astype(jnp.int32), -1).astype(jnp.int32)


def draw_enc_segments(key, part):
    key = jax.random.fold_in(key, 11)
    return segment_numbers(key)


def draw_dec_segments(key, part):
    key = jax.random.fold_in(key, 12)
    return segment_numbers(key)


def draw_expert_weights(key, part):
    key = jax.random.fold_in(key, 13)
    values = jax.random.uniform(key, (3, EXPERTS, D, 2 * HD), jnp.float32, -1.7320508, 1.7320508)
    column = jnp.arange(2 * HD)
    scale = jnp.where(column < HD, D ** (-0.5), 0.5)
    return (values * scale).astype(jnp.bfloat16)


def shard_levels(key, extent, pieces, least, top_value):
    def one(position, blocks):
        draws = jax.random.uniform(jax.random.fold_in(jax.random.fold_in(key, 6), position), (blocks,), jnp.float32, least / len(pieces), top_value / len(pieces))
        return jnp.repeat(jnp.exp(draws), extent[position] // blocks).reshape((-1,) + (1,) * (len(extent) - position - 1))

    level = one(*pieces[0])
    for cut in pieces[1:]:
        level = level * one(*cut)
    return level


def choose_distinct(own_key, rows, number_of, top, lift):
    order = jax.random.permutation(jax.random.fold_in(own_key, 1), number_of)
    favour = order
    for power in range(3):
        favour = favour * favour // number_of
    favour = favour * lift // number_of
    lots = jax.random.randint(jax.random.fold_in(own_key, 2), (rows, number_of), 0, 4096) + favour
    sure = jax.random.permutation(jax.random.fold_in(own_key, 3), rows)[jnp.arange(number_of) % rows]
    lots = jnp.where(jnp.arange(rows)[:, None] == sure[None, :], 1 << 14, lots)
    priority = lots * number_of + jnp.arange(number_of)
    return lax.top_k(priority.astype(jnp.int32), top)[1].astype(jnp.int32)


def normal_values(stream_key, extent, spread, bound, pieces=(), kind=jnp.bfloat16):
    values = jax.random.normal(stream_key, extent, jnp.float32) * spread
    if len(pieces) > 0:
        values = shard_levels(stream_key, extent, pieces, -0.22, 0.18) * values
    return jnp.clip(values, min=-bound, max=bound).astype(kind)


def setup_inputs(seed: int = 0) -> dict:
    streams_of = jax.random.split(jax.random.key(seed), 19)
    enc_input = normal_values(streams_of[0], (ROWS, ROW_LEN, D), 1.0, 6.0, ((0, 8), (1, 4)))
    dec_input = normal_values(streams_of[1], (ROWS, ROW_LEN, D), 1.0, 6.0, ((0, 8), (1, 4)))
    enc_segments = draw_enc_segments(jax.random.fold_in(streams_of[18], 71), 0)
    dec_segments = draw_dec_segments(jax.random.fold_in(streams_of[18], 71), 0)
    routes = choose_distinct(streams_of[4], 3 * ROWS * ROW_LEN, EXPERTS, TOP, 4096).reshape((3, ROWS, ROW_LEN, TOP))
    enc_out_grad = normal_values(streams_of[5], (ROWS, ROW_LEN, D), 1.0, 6.0, ((0, 8), (1, 4)))
    dec_out_grad = normal_values(streams_of[6], (ROWS, ROW_LEN, D), 1.0, 6.0, ((0, 8), (1, 4)))
    enc_gains = jnp.clip(1.0 + 0.1 * jax.random.normal(streams_of[7], (2, D), jnp.float32), 0.5, 1.5).astype(jnp.bfloat16)
    enc_biases = normal_values(streams_of[8], (2, D), 0.3, 2.0)
    dec_gains = jnp.clip(1.0 + 0.1 * jax.random.normal(streams_of[9], (3, D), jnp.float32), 0.5, 1.5).astype(jnp.bfloat16)
    dec_biases = normal_values(streams_of[10], (3, D), 0.3, 2.0)
    kv_weights = normal_values(streams_of[11], (3, D, 2 * HD), D ** -0.5, 0.25)
    router_weights = normal_values(streams_of[12], (3, D, EXPERTS), (0.75 * D ** -0.5), 0.1875)
    expert_weights = draw_expert_weights(jax.random.fold_in(streams_of[18], 71), 0)
    ffn_in = normal_values(streams_of[14], (2, D, FF), D ** -0.5, 0.25)
    ffn_in_bias = normal_values(streams_of[15], (2, FF), 0.3, 2.0)
    ffn_out = normal_values(streams_of[16], (2, FF, D), FF ** -0.5, 0.125)
    ffn_out_bias = normal_values(streams_of[17], (2, D), 0.3, 2.0)
    return dict(enc_input=enc_input, dec_input=dec_input, enc_segments=enc_segments, dec_segments=dec_segments, routes=routes, enc_out_grad=enc_out_grad, dec_out_grad=dec_out_grad, enc_gains=enc_gains, enc_biases=enc_biases, dec_gains=dec_gains, dec_biases=dec_biases, kv_weights=kv_weights, router_weights=router_weights, expert_weights=expert_weights, ffn_in=ffn_in, ffn_in_bias=ffn_in_bias, ffn_out=ffn_out, ffn_out_bias=ffn_out_bias)


EPS = 1e-05
SCALE = 0.125
NEG = -1e+30
HIGH = lax.Precision.HIGHEST

@jax.custom_vjp
def low(v):
    return lax.optimization_barrier(v.astype(jnp.bfloat16)).astype(jnp.float32)

@jax.custom_vjp
def low_back(v):
    return v

def low_keep(v):
    return (low(v), None)

def low_pass(kept, grad):
    return (grad,)

def back_keep(v):
    return (v, None)

def back_low(kept, grad):
    return (low(grad),)
low.defvjp(low_keep, low_pass)
low_back.defvjp(back_keep, back_low)

def layer_norm(hidden, gain, bias):
    mean_part = lax.optimization_barrier(jnp.mean(hidden, -1, keepdims=True))
    centred = hidden - mean_part
    var_part = lax.optimization_barrier(jnp.mean(centred * centred, -1, keepdims=True))
    return centred * lax.rsqrt(var_part + EPS) * gain + bias

def project(values, weight):
    return jnp.einsum('rld,de->rle', values, weight, precision=HIGH)

def feed_forward(normed, w_in, b_in, w_out, b_out):
    inner = low_back(project(low(normed), w_in) + b_in)
    active = low(jax.nn.gelu(inner, approximate=False))
    return low_back(project(active, w_out) + b_out)

def attend(queries, key_value, query_seg, key_seg, causal):
    key_part = key_value[:, :HD]
    value_part = key_value[:, HD:]
    scores = low_back(jnp.einsum('qjh,kh->qjk', queries, key_part, precision=HIGH) * SCALE)
    allowed = query_seg[:, None] == key_seg[None, :]
    if causal:
        places = jnp.arange(ROW_LEN, dtype=jnp.int32)
        allowed = allowed & (places[:, None] >= places[None, :])
    scores = jnp.where(allowed[:, None, :], scores, NEG)
    probs = low(jax.nn.softmax(scores, axis=-1))
    return jnp.einsum('qjk,kh->qjh', probs, value_part, precision=HIGH)

def kept_pairs(route_ids):
    groups = ROWS // ROWS_DEV
    order = route_ids.reshape(groups, ROWS_DEV, N_SEQ, SPAN, TOP).transpose(0, 2, 1, 3, 4)
    order = order.reshape(groups * N_SEQ, ROWS_DEV * SPAN * TOP)
    onehot = (order[..., None] == jnp.arange(EXPERTS, dtype=jnp.int32)).astype(jnp.int32)
    ranks = lax.optimization_barrier(jnp.sum(jnp.cumsum(onehot, 1) * onehot, -1)) - 1
    kept = (ranks < CAP).astype(jnp.float32)
    kept = kept.reshape(groups, N_SEQ, ROWS_DEV, SPAN, TOP).transpose(0, 2, 1, 3, 4)
    return kept.reshape(ROWS, ROW_LEN, TOP)

def mixture(normed, source, query_seg, key_seg, route_ids, kept, kv_weight, router_weight, expert_weight, causal):
    key_value = low_back(low(project(source, kv_weight)))
    logits = low_back(project(normed, router_weight))
    gates = jax.nn.softmax(jnp.take_along_axis(logits, route_ids, -1), axis=-1)
    masks = [(route_ids == expert).astype(jnp.float32)[..., None] for expert in range(EXPERTS)]
    queries = jnp.zeros(route_ids.shape + (HD,), jnp.float32)
    for expert in range(EXPERTS):
        queries = queries + masks[expert] * project(normed, expert_weight[expert, :, :HD])[:, :, None, :]
    queries = low_back(low(queries))
    attend_one = jax.checkpoint(partial(attend, causal=causal))

    def per_row(items):
        return attend_one(items[0], items[1], items[2], items[3])
    mixed = lax.map(per_row, (queries, key_value, query_seg, key_seg))
    mixed = low_back(low(mixed))
    returned = jnp.zeros(route_ids.shape + (D,), jnp.float32)
    for expert in range(EXPERTS):
        returned = returned + jnp.einsum('rljh,dh->rljd', mixed * masks[expert], expert_weight[expert, :, HD:], precision=HIGH)
    returned = low_back(low(returned))
    return lax.optimization_barrier(jnp.sum((kept * gates)[..., None] * returned, 2))

def layers(enc_in, dec_in, enc_gains, enc_biases, dec_gains, dec_biases, kv_weights, router_weights, expert_weights, ffn_in, ffn_in_bias, ffn_out, ffn_out_bias, enc_seg, dec_seg, routes, keeps):
    normed = low(layer_norm(enc_in, enc_gains[0], enc_biases[0]))
    hidden = enc_in + mixture(normed, normed, enc_seg, enc_seg, routes[0], keeps[0], kv_weights[0], router_weights[0], expert_weights[0], False)
    hidden = hidden + feed_forward(layer_norm(hidden, enc_gains[1], enc_biases[1]), ffn_in[0], ffn_in_bias[0], ffn_out[0], ffn_out_bias[0])
    memory = low(hidden)
    normed = low(layer_norm(dec_in, dec_gains[0], dec_biases[0]))
    decoded = dec_in + mixture(normed, normed, dec_seg, dec_seg, routes[1], keeps[1], kv_weights[1], router_weights[1], expert_weights[1], True)
    normed = low(layer_norm(decoded, dec_gains[1], dec_biases[1]))
    decoded = decoded + mixture(normed, memory, dec_seg, enc_seg, routes[2], keeps[2], kv_weights[2], router_weights[2], expert_weights[2], False)
    decoded = decoded + feed_forward(layer_norm(decoded, dec_gains[2], dec_biases[2]), ffn_in[1], ffn_in_bias[1], ffn_out[1], ffn_out_bias[1])
    return (hidden, decoded)

def reference(enc_input, dec_input, enc_segments, dec_segments, routes, enc_out_grad, dec_out_grad, enc_gains, enc_biases, dec_gains, dec_biases, kv_weights, router_weights, expert_weights, ffn_in, ffn_in_bias, ffn_out, ffn_out_bias):
    keeps = jnp.stack([kept_pairs(routes[block]) for block in range(3)])
    floats = tuple((value.astype(jnp.float32) for value in (enc_input, dec_input, enc_gains, enc_biases, dec_gains, dec_biases, kv_weights, router_weights, expert_weights, ffn_in, ffn_in_bias, ffn_out, ffn_out_bias)))

    def forward(*values):
        return layers(*values, enc_segments, dec_segments, routes, keeps)
    outputs, pull = jax.vjp(forward, *floats)
    grads = pull((enc_out_grad.astype(jnp.float32), dec_out_grad.astype(jnp.float32)))
    return (outputs[0].astype(jnp.bfloat16), outputs[1].astype(jnp.bfloat16), grads[0], grads[1], grads[2], grads[3], grads[4], grads[5], grads[6], grads[7], grads[8], grads[9], grads[10], grads[11], grads[12])
```

```python
from functools import partial

import jax
import jax.numpy as jnp
from jax import lax
from jax.experimental import pallas as pl
from jax.experimental.pallas import tpu as pltpu
from jax.sharding import PartitionSpec as P

EXPERTS = 8
HD = 64
TOP = 2
PAIR = 2 * HD

EPS = 1e-05
SCALE = 0.125
NEG = -1e30
F32 = jnp.float32
BF16 = jnp.bfloat16
SQRT_HALF = 0.7071067811865476
INV_SQRT_2PI = 0.3989422804014327
VMEM_LIMIT = 20 * 1024 * 1024

ROUTE = 0
LOCAL_ROUTE = 6
KEY_SEG = 12


def mm(left, right):
    return lax.dot_general(left, right, (((1,), (0,)), ((), ())), preferred_element_type=F32)


def mm_nt(left, right):
    return lax.dot_general(left, right, (((1,), (1,)), ((), ())), preferred_element_type=F32)


def mm_tn(left, right):
    return lax.dot_general(left, right, (((0,), (0,)), ((), ())), preferred_element_type=F32)


def iota(shape, dim):
    return lax.broadcasted_iota(jnp.int32, shape, dim)


def standardize(hidden):
    centred = hidden - jnp.mean(hidden, -1, keepdims=True)
    inverse = lax.rsqrt(jnp.mean(centred * centred, -1, keepdims=True) + EPS)
    return centred * inverse, inverse


def norm(hidden, gain, bias):
    return standardize(hidden)[0] * gain + bias


def norm_back(hidden, gain, upstream):
    unit, inverse = standardize(hidden)
    grad_gain = jnp.sum(upstream * unit, 0, keepdims=True)
    grad_bias = jnp.sum(upstream, 0, keepdims=True)
    scaled = upstream * gain
    centred = scaled - jnp.mean(scaled, -1, keepdims=True)
    projected = jnp.mean(scaled * unit, -1, keepdims=True)
    return inverse * (centred - unit * projected), grad_gain, grad_bias


def widened(router):
    full = router.astype(F32)
    return jnp.concatenate([full, jnp.zeros((PAIR - full.shape[0], full.shape[1]), F32)], 0).astype(BF16)


def row_of(ref, index):
    return ref[...].astype(F32)[index : index + 1]


class Order:
    last = None

    @classmethod
    def start(cls):
        cls.last = None

    @classmethod
    def run(cls, kernel, args):
        args = [operand(arg) for arg in args]
        if cls.last is not None:
            args[0], _ = lax.optimization_barrier((args[0], cls.last))
        outs = kernel(*args)
        cls.last = outs[0]
        return outs


class Layer:
    def __init__(self, array, index):
        self.array, self.index = array, index
        self.shape = array.shape[1:]

    def spec(self):
        index, rest = self.index, len(self.shape)
        return pl.BlockSpec((None,) + self.shape, lambda *_: (index,) + (0,) * rest)


class Rows:
    def __init__(self, array, rows, index):
        self.array, self.index = array, index
        self.shape = (rows, array.shape[1])

    def spec(self):
        index = self.index
        return pl.BlockSpec(self.shape, lambda *_: (index, 0))


def operand(arg):
    return arg.array if isinstance(arg, (Layer, Rows)) else arg


def whole(arg):
    if isinstance(arg, (Layer, Rows)):
        return arg.spec()
    rest = len(arg.shape)
    return pl.BlockSpec(arg.shape, lambda *_: (0,) * rest)


TIMES = {
    "norm_kv": 0.7, "prepare": 0.3, "queries": 2.0, "norm_queries": 2.3, "attend": 3.4, "ffn_forward": 6.2,
    "ffn_both": 12.0, "attend_back": 5.0, "expert_back": 3.4, "ffn_back": 8.5, "self_finish": 2.0,
    "place_first": 3.5, "place_second": 3.5, "unpack_small": 1.0,
}
PACE = 1.0


def cost(name):
    micros = TIMES.get(name, 0.4) * PACE
    return pl.CostEstimate(flops=int(micros * 1e9), bytes_accessed=int(micros * 3e6), transcendentals=0)


def call(body, outs, args, scratch=(), limit=14 * 1024 * 1024, name=None):
    shapes = [jax.ShapeDtypeStruct(s, d) for s, d in outs]
    kernel = pl.pallas_call(
        body,
        grid=(1,),
        out_shape=tuple(shapes),
        in_specs=[whole(arg) for arg in args],
        out_specs=tuple(whole(out) for out in shapes),
        scratch_shapes=list(scratch),
        cost_estimate=cost(name),
        compiler_params=pltpu.CompilerParams(vmem_limit_bytes=limit),
        name=name,
    )
    return Order.run(kernel, args)


def prepare(routes, enc_seg, dec_seg, n_ep, n_seq, per):
    subs, rows, _, span = routes.shape
    tokens = rows * span
    used = 2 * subs * TOP + 2 * n_seq

    def body(r_ref, e_ref, d_ref, meta_ref, rows_ref):
        base = lax.axis_index("ep") * per
        me = lax.axis_index("seq")
        lines = []
        for flip in (False, True):
            for sub in range(subs):
                for j in range(TOP):
                    line = jnp.concatenate([r_ref[sub, r, j : j + 1, :] for r in range(rows)], 1)
                    lines.append(line ^ base if flip else line)
        queries = []
        for ref in (e_ref, d_ref):
            for d in range(n_seq):
                at = pl.multiple_of((me ^ d) * span, span)
                block = ref[:, pl.ds(at, span)]
                lines.append(jnp.concatenate([block[r : r + 1] for r in range(rows)], 1))
                if d == 0:
                    queries.append(jnp.concatenate([block] * TOP, 1))
        rows_ref[...] = jnp.concatenate(queries, 0)
        lines = [line.astype(F32) for line in lines]
        lines.append(jnp.zeros((PAIR - used, tokens), F32))
        meta_ref[...] = jnp.concatenate(lines, 0).T.astype(jnp.int32)

    return call(
        body,
        [((tokens, PAIR), jnp.int32), ((2 * rows, TOP * span), jnp.int32)],
        (routes, enc_seg, dec_seg),
        name="prepare",
    )


def norm_kv(hidden, gains, biases, kv_weights, layer, index, expert_weights, copied):
    tokens, width = hidden.shape
    stack = gains.shape[0]

    def body(h_ref, g_ref, b_ref, w_ref, e_ref, n_ref, kv_ref, *rest):
        e_outs = rest[: len(copied)]
        h_in, g_in, b_in, w_in, sems = rest[len(copied) :]
        pairs = [(h_ref, h_in), (g_ref, g_in), (b_ref, b_in), (w_ref.at[index], w_in)]
        pairs += [(e_ref.at[k], out) for k, out in zip(copied, e_outs)]
        moves = [pltpu.make_async_copy(*pair, sems.at[i]) for i, pair in enumerate(pairs)]
        for move in moves:
            move.start()
        for move in moves[:3]:
            move.wait()
        normed = norm(h_in[...].astype(F32), row_of(g_in, layer), row_of(b_in, layer)).astype(BF16)
        n_ref[...] = normed
        moves[3].wait()
        kv_ref[...] = mm(normed, w_in[...]).astype(BF16)
        for move in moves[4:]:
            move.wait()

    held = pl.BlockSpec(memory_space=pltpu.HBM)
    outs = [((tokens, width), BF16), ((tokens, PAIR), BF16)] + [(expert_weights.shape[1:], BF16)] * len(copied)
    shapes = [jax.ShapeDtypeStruct(*out) for out in outs]
    kernel = pl.pallas_call(
        body,
        out_shape=tuple(shapes),
        in_specs=[held] * 5,
        out_specs=tuple(pl.BlockSpec(memory_space=pltpu.VMEM) for _ in shapes),
        scratch_shapes=[
            pltpu.VMEM((tokens, width), BF16), pltpu.VMEM((stack, width), BF16), pltpu.VMEM((stack, width), BF16),
            pltpu.VMEM(kv_weights.shape[1:], BF16), pltpu.SemaphoreType.DMA((4 + len(copied),)),
        ],
        cost_estimate=cost("norm_kv"),
        compiler_params=pltpu.CompilerParams(vmem_limit_bytes=VMEM_LIMIT),
        name="norm_kv",
    )
    return Order.run(kernel, [hidden, gains, biases, kv_weights, expert_weights])


def query_part(normed, weights, router, meta_ref, sub, q_ref, aux_ref):
    tokens = normed.shape[0]
    per = weights[0].shape[0]
    lane = iota((tokens, PAIR), 1)
    local = [meta_ref[:, LOCAL_ROUTE + TOP * sub + j : LOCAL_ROUTE + TOP * sub + j + 1] for j in range(TOP)]
    route = [meta_ref[:, ROUTE + TOP * sub + j : ROUTE + TOP * sub + j + 1] for j in range(TOP)]
    picked = [jnp.zeros((tokens, PAIR), F32) for _ in range(TOP)]
    for expert in range(EXPERTS):
        every = mm(normed, weights[expert // per][expert % per])
        picked = [jnp.where(local[j] == expert, every, picked[j]) for j in range(TOP)]
    for j in range(TOP):
        rounded = picked[j].astype(BF16).astype(F32) * SCALE
        q_ref[j] = jnp.where(lane < HD, rounded, 0.0).astype(BF16)
    logits = mm_nt(normed, widened(router))
    hit = [lane == route[j] for j in range(TOP)]
    chosen = [jnp.sum(jnp.where(hit[j], logits, 0.0), -1, keepdims=True) for j in range(TOP)]
    top = jnp.maximum(chosen[0], chosen[1])
    raised = [jnp.exp(value - top) for value in chosen]
    total = raised[0] + raised[1]
    count = jnp.where(hit[0] | hit[1], 1.0, 0.0).astype(BF16)
    before = (iota((tokens, tokens), 0) > iota((tokens, tokens), 1)).astype(F32).astype(BF16)
    ranks = mm(before, count)
    capacity = tokens * TOP // EXPERTS
    aux = jnp.zeros((tokens, PAIR), F32)
    for j in range(TOP):
        rank = jnp.sum(jnp.where(hit[j], ranks, 0.0), -1, keepdims=True)
        kept = jnp.where(rank < capacity, 1.0, 0.0)
        aux = jnp.where(lane == j, raised[j] / total, aux)
        aux = jnp.where(lane == TOP + j, kept, aux)
    aux_ref[...] = aux


def queries(normed, weights, router, meta, sub):
    tokens, width = normed.shape
    count = len(weights)

    def body(*refs):
        n_ref, w_refs = refs[0], refs[1 : 1 + count]
        r_ref, meta_ref, q_ref, aux_ref = refs[1 + count :]
        query_part(n_ref[...], w_refs, r_ref[...], meta_ref, sub, q_ref, aux_ref)

    return call(
        body,
        [((TOP, tokens, PAIR), BF16), ((tokens, PAIR), F32)],
        (normed, *weights, router, meta),
        name="queries",
    )


def norm_queries(hidden, gains, biases, layer, weights, router, meta, sub):
    tokens, width = hidden.shape
    count = len(weights)

    def body(*refs):
        h_ref, g_ref, b_ref, w_refs = refs[0], refs[1], refs[2], refs[3 : 3 + count]
        r_ref, meta_ref, n_ref, q_ref, aux_ref = refs[3 + count :]
        normed = norm(h_ref[...], row_of(g_ref, layer), row_of(b_ref, layer)).astype(BF16)
        n_ref[...] = normed
        query_part(normed, w_refs, r_ref[...], meta_ref, sub, q_ref, aux_ref)

    return call(
        body,
        [((tokens, width), BF16), ((TOP, tokens, PAIR), BF16), ((tokens, PAIR), F32)],
        (hidden, gains, biases, *weights, router, meta),
        name="norm_queries",
    )


def allowed_block(meta_ref, q_row, place, rows, column, causal):
    allowed = meta_ref[rows, column : column + 1] == q_row
    if causal:
        span, wide = rows.stop - rows.start, q_row.shape[1]
        me = lax.axis_index("seq")
        key = iota((span, wide), 0) + ((me ^ place) - me) * span
        query = lax.rem(iota((1, wide), 1), span)
        allowed = allowed & (query >= key)
    return allowed


def mixed_slots(mixed, aux, meta_ref, sub):
    scaled = [mixed[j] * (aux[:, j : j + 1] * aux[:, TOP + j : TOP + j + 1]) for j in range(TOP)]
    local = [meta_ref[:, LOCAL_ROUTE + TOP * sub + j : LOCAL_ROUTE + TOP * sub + j + 1] for j in range(TOP)]

    def of(expert):
        part = jnp.where(local[1] == expert, scaled[1], 0.0)
        return jnp.where(local[0] == expert, scaled[0], part).astype(BF16)

    return of


def attend(hidden, query, aux, key_values, weights, meta, q_rows, sub, q_base, k_base, causal):
    tokens, width = hidden.shape
    rows = q_rows.shape[0] // 2
    span = tokens // rows
    wide = TOP * span
    blocks, owners = len(key_values), len(weights)
    per = weights[0].shape[0]

    def body(*refs):
        h_ref, q_ref, aux_ref = refs[:3]
        kv_refs = refs[3 : 3 + blocks]
        w_refs = refs[3 + blocks : 3 + blocks + owners]
        meta_ref, qr_ref, o_ref, lse_ref, out_ref, s_ref = refs[3 + blocks + owners :]
        lane = iota((wide, PAIR), 1)
        for r in range(rows):
            here = slice(r * span, (r + 1) * span)
            q_row = qr_ref[q_base * rows + r : q_base * rows + r + 1, :]
            q_all = jnp.concatenate([q_ref[j, here] for j in range(TOP)], 0)
            top = jnp.full((1, wide), NEG, F32)
            for d in range(blocks):
                scores = mm_nt(kv_refs[d][here], q_all)
                allowed = allowed_block(
                    meta_ref, q_row, d, here, KEY_SEG + k_base * blocks + d, causal
                )
                scores = jnp.where(allowed, scores, NEG)
                s_ref[d * span : (d + 1) * span] = scores
                top = jnp.maximum(top, jnp.max(scores, 0, keepdims=True))
            total = jnp.zeros((1, wide), F32)
            mixed = jnp.zeros((PAIR, wide), F32)
            for d in range(blocks):
                probs = jnp.exp(s_ref[d * span : (d + 1) * span] - top)
                total = total + jnp.sum(probs, 0, keepdims=True)
                mixed = mixed + mm_tn(kv_refs[d][here], probs.astype(BF16))
            lse_ref[r : r + 1] = top + jnp.log(total)
            mixed = jnp.where(lane < HD, 0.0, (mixed / total).T).astype(BF16)
            for j in range(TOP):
                o_ref[j, here] = mixed[j * span : (j + 1) * span]
        slot = mixed_slots([o_ref[j].astype(F32) for j in range(TOP)], aux_ref[...], meta_ref, sub)
        result = h_ref[...].astype(F32)
        for expert in range(0, EXPERTS, 2):
            part = jnp.concatenate([slot(expert), slot(expert + 1)], 1)
            weight = jnp.concatenate([w_refs[e // per][e % per] for e in (expert, expert + 1)], 1)
            result = result + mm_nt(part, weight)
        out_ref[...] = result

    args = (hidden, query, aux, *key_values, *weights, meta, q_rows)
    return call(
        body,
        [((TOP, tokens, PAIR), BF16), ((rows, wide), F32), ((tokens, width), F32)],
        args,
        scratch=[pltpu.VMEM((blocks * span, wide), F32)],
        name="attend",
    )


def attend_back(upstream, mixed, query, aux, lse, key_values, weights, meta, q_rows, sub, q_base, k_base, causal):
    tokens, width = upstream.shape
    rows = q_rows.shape[0] // 2
    span = tokens // rows
    wide = TOP * span
    blocks, owners = len(key_values), len(weights)
    per = weights[0].shape[0]

    def body(*refs):
        up_ref, o_ref, q_ref, aux_ref, lse_ref = refs[:5]
        kv_refs = refs[5 : 5 + blocks]
        w_refs = refs[5 + blocks : 5 + blocks + owners]
        meta_ref, qr_ref = refs[5 + blocks + owners : 7 + blocks + owners]
        dkv_refs = refs[7 + blocks + owners : 7 + 2 * blocks + owners]
        dq_ref, dlog_ref, do_ref = refs[7 + 2 * blocks + owners :]
        rounded = up_ref[...].astype(BF16)
        lane = iota((tokens, PAIR), 1)
        local = [meta_ref[:, LOCAL_ROUTE + TOP * sub + j : LOCAL_ROUTE + TOP * sub + j + 1] for j in range(TOP)]
        route = [meta_ref[:, ROUTE + TOP * sub + j : ROUTE + TOP * sub + j + 1] for j in range(TOP)]
        picked = [jnp.zeros((tokens, PAIR), F32) for _ in range(TOP)]
        for expert in range(EXPERTS):
            every = mm(rounded, w_refs[expert // per][expert % per])
            picked = [jnp.where(local[j] == expert, every, picked[j]) for j in range(TOP)]
        aux = aux_ref[...]
        gate = [aux[:, j : j + 1] for j in range(TOP)]
        kept = [aux[:, TOP + j : TOP + j + 1] for j in range(TOP)]
        grad_gate = [
            kept[j] * jnp.sum(picked[j] * o_ref[j].astype(F32), -1, keepdims=True) for j in range(TOP)
        ]
        inner = gate[0] * grad_gate[0] + gate[1] * grad_gate[1]
        dlog = jnp.zeros((tokens, PAIR), F32)
        for j in range(TOP):
            dlog = jnp.where(lane == route[j], gate[j] * (grad_gate[j] - inner), dlog)
            do_ref[j] = jnp.where(lane < HD, 0.0, picked[j] * (gate[j] * kept[j])).astype(BF16)
        dlog_ref[...] = dlog.astype(BF16)
        lane = iota((wide, PAIR), 1)
        for r in range(rows):
            here = slice(r * span, (r + 1) * span)
            q_row = qr_ref[q_base * rows + r : q_base * rows + r + 1, :]
            q_all = jnp.concatenate([q_ref[j, here] for j in range(TOP)], 0)
            do_all = jnp.concatenate([do_ref[j, here] for j in range(TOP)], 0)
            log_total = lse_ref[r : r + 1]
            inner = jnp.zeros((1, wide), F32)
            probs, grads = [], []
            for d in range(blocks):
                scores = mm_nt(kv_refs[d][here], q_all)
                allowed = allowed_block(
                    meta_ref, q_row, d, here, KEY_SEG + k_base * blocks + d, causal
                )
                prob = jnp.exp(jnp.where(allowed, scores, NEG) - log_total)
                grad = mm_nt(kv_refs[d][here], do_all)
                inner = inner + jnp.sum(prob * grad, 0, keepdims=True)
                probs.append(prob)
                grads.append(grad)
            grad_query = jnp.zeros((PAIR, wide), F32)
            for d in range(blocks):
                grad_score = (probs[d] * (grads[d] - inner)).astype(BF16)
                grad_query = grad_query + mm_tn(kv_refs[d][here], grad_score)
                grad_kv = mm(probs[d].astype(BF16), do_all) + mm(grad_score, q_all)
                dkv_refs[d][here] = grad_kv.astype(BF16)
            grad_query = jnp.where(lane < HD, grad_query.T * SCALE, 0.0).astype(BF16)
            for j in range(TOP):
                dq_ref[j, here] = grad_query[j * span : (j + 1) * span]

    args = (upstream, mixed, query, aux, lse, *key_values, *weights, meta, q_rows)
    outs = call(
        body,
        [((tokens, PAIR), BF16)] * blocks + [((TOP, tokens, PAIR), BF16), ((tokens, PAIR), BF16)],
        args,
        scratch=[pltpu.VMEM((TOP, tokens, PAIR), BF16)],
        name="attend_back",
    )
    return outs[:blocks], outs[blocks], outs[blocks + 1]


def expert_back(upstream, normed, mixed, aux, dq, dlog, weights, router, meta, sub, hidden=None, gains=None, layer=0):
    tokens, width = upstream.shape
    owners = len(weights)
    per = weights[0].shape[0]
    finish = hidden is not None

    def body(*refs):
        up_ref, n_ref, o_ref, aux_ref, dq_ref, dlog_ref = refs[:6]
        w_refs = refs[6 : 6 + owners]
        r_ref, meta_ref = refs[6 + owners : 8 + owners]
        at = 8 + owners
        if finish:
            h_ref, g_ref = refs[at : at + 2]
            at += 2
        own_ref, send_ref, dr_ref, dn_ref = refs[at : at + 4]
        low_core = lax.axis_index("core") == 0
        half = width // 2
        slot = mixed_slots([o_ref[j].astype(F32) for j in range(TOP)], aux_ref[...], meta_ref, sub)
        local = [meta_ref[:, LOCAL_ROUTE + TOP * sub + j : LOCAL_ROUTE + TOP * sub + j + 1] for j in range(TOP)]
        grads = [dq_ref[j].astype(F32) * aux_ref[:, TOP + j : TOP + j + 1] for j in range(TOP)]

        def query_slot(expert):
            part = jnp.where(local[1] == expert, grads[1], 0.0)
            return jnp.where(local[0] == expert, grads[0], part).astype(BF16)

        normed_t = n_ref[...].T
        up_t = up_ref[...].astype(BF16).T
        total = mm(dlog_ref[...], widened(r_ref[...]))
        for expert in range(0, EXPERTS, 2):
            both = (expert, expert + 1)
            part = jnp.concatenate([query_slot(e) for e in both], 1)
            weight = jnp.concatenate([w_refs[e // per][e % per] for e in both], 1)
            total = total + mm_nt(part, weight)
            result = jnp.concatenate([slot(e) for e in both], 1)
            grad = (mm(normed_t, part) + mm(up_t, result)).astype(BF16)
            for k, e in enumerate(both):
                low, high = [grad[at : at + half, k * PAIR : (k + 1) * PAIR] for at in (0, half)]
                place = slice(e * half, (e + 1) * half)
                own_ref[place] = jnp.where(low_core, low, high)
                send_ref[place] = jnp.where(low_core, high, low)
        dr_ref[...] = mm_tn(dlog_ref[...], n_ref[...])[:EXPERTS]
        if finish:
            back, grad_gain, grad_bias = norm_back(h_ref[...].astype(F32), row_of(g_ref, layer), total)
            dn_ref[...] = up_ref[...] + back
            refs[at + 4][...] = jnp.concatenate([grad_gain, grad_bias], 0)
        else:
            dn_ref[...] = total

    outs = [((EXPERTS * width // 2, PAIR), BF16)] * 2 + [((EXPERTS, width), F32), ((tokens, width), F32)]
    args = (upstream, normed, mixed, aux, dq, dlog, *weights, router, meta)
    if finish:
        outs = outs + [((2, width), F32)]
        args = args + (hidden, gains)
    return call(body, outs, args, name="expert_back")


def self_finish(upstream, grad_normed, grad_kvs, normed, kv_weight, hidden, gains, layer):
    tokens, width = upstream.shape
    blocks = len(grad_kvs)

    def body(*refs):
        up_ref, dn_ref = refs[:2]
        kv_refs = refs[2 : 2 + blocks]
        n_ref, w_ref, h_ref, g_ref, out_ref, dw_ref, small_ref = refs[2 + blocks :]
        grad_kv = kv_refs[0][...].astype(F32)
        for ref in kv_refs[1:]:
            grad_kv = grad_kv + ref[...].astype(F32)
        grad_kv = grad_kv.astype(BF16)
        total = dn_ref[...] + mm_nt(grad_kv, w_ref[...])
        dw_ref[...] = mm_tn(n_ref[...], grad_kv)
        back, grad_gain, grad_bias = norm_back(h_ref[...].astype(F32), row_of(g_ref, layer), total)
        out_ref[...] = up_ref[...] + back
        small_ref[...] = jnp.concatenate([grad_gain, grad_bias], 0)

    return call(
        body,
        [((tokens, width), F32), ((width, PAIR), F32), ((2, width), F32)],
        (upstream, grad_normed, *grad_kvs, normed, kv_weight, hidden, gains),
        name="self_finish",
    )


def gelu_parts(inner):
    cdf = 0.5 * (1.0 + lax.erf(inner * SQRT_HALF))
    density = jnp.exp(-0.5 * inner * inner) * INV_SQRT_2PI
    return inner * cdf, cdf + inner * density


def ffn_call(body, tokens, width, hidden, tiles, ins, outs, scratch, name):
    tile = hidden // tiles
    kinds = {
        "full2": lambda s: pl.BlockSpec(s, lambda k: (0, 0)),
        "win": lambda s: pl.BlockSpec((1, width, tile), lambda k: (s, 0, k)),
        "bin": lambda s: pl.BlockSpec((2, tile), lambda k: (0, k)),
        "wout": lambda s: pl.BlockSpec((1, tile, width), lambda k: (s, k, 0)),
        "act": lambda s: pl.BlockSpec((tokens, tile), lambda k: (0, k)),
    }
    kernel = pl.pallas_call(
        body,
        grid=(tiles,),
        in_specs=[kinds[kind](s) for kind, s, _ in ins],
        out_specs=tuple(kinds[kind](shape) for kind, shape, _ in outs),
        out_shape=tuple(jax.ShapeDtypeStruct(shape, dtype) for _, shape, dtype in outs),
        scratch_shapes=scratch,
        cost_estimate=cost(name),
        compiler_params=pltpu.CompilerParams(vmem_limit_bytes=VMEM_LIMIT),
        name=name,
    )
    return Order.run(kernel, [a for _, _, a in ins])


def ffn_forward(hidden, gains, biases, norm_layer, w_in, b_in, w_out, b_out, layer, kv_weight, tiles):
    tokens, width = hidden.shape
    units = w_in.shape[2]

    def body(h_ref, g_ref, b_ref, wi_ref, bi_ref, wo_ref, bo_ref, kw_ref,
             n_out, z_ref, s_ref, mem_ref, kv_ref, n_ref, acc_ref):
        step = pl.program_id(0)

        @pl.when(step == 0)
        def _():
            normed = norm(h_ref[...], row_of(g_ref, norm_layer), row_of(b_ref, norm_layer)).astype(BF16)
            n_ref[...] = normed
            n_out[...] = normed
            acc_ref[...] = h_ref[...] + row_of(bo_ref, layer)

        inner = mm(n_ref[...], wi_ref[0]) + row_of(bi_ref, layer)
        active, slope = gelu_parts(inner)
        active = active.astype(BF16)
        z_ref[...] = active
        s_ref[...] = slope.astype(BF16)
        acc_ref[...] += mm(active, wo_ref[0])

        @pl.when(step == tiles - 1)
        def _():
            memory = acc_ref[...].astype(BF16)
            mem_ref[...] = memory
            kv_ref[...] = mm(memory, kw_ref[...]).astype(BF16)

    ins = [
        ("full2", hidden.shape, hidden), ("full2", gains.shape, gains), ("full2", biases.shape, biases),
        ("win", layer, w_in), ("bin", None, b_in), ("wout", layer, w_out), ("full2", b_out.shape, b_out),
        ("full2", kv_weight.shape, kv_weight),
    ]
    outs = [
        ("full2", (tokens, width), BF16), ("act", (tokens, units), BF16), ("act", (tokens, units), BF16),
        ("full2", (tokens, width), BF16), ("full2", (tokens, PAIR), BF16),
    ]
    scratch = [pltpu.VMEM((tokens, width), BF16), pltpu.VMEM((tokens, width), F32)]
    return ffn_call(body, tokens, width, units, tiles, ins, outs, scratch, "ffn_forward")


def grad_call(body, core, ins, outs, scratch, tiles, name):
    half = tiles // 2

    def unit(k, core_ref):
        far = jnp.where(k < half, 1 - core_ref[0], core_ref[0])
        return far * half + lax.rem(k, half)

    def spec(kind, shape):
        if kind == "w_in":
            layer, (width, tile) = shape
            return pl.BlockSpec((None, width, tile), lambda k, c: (layer, 0, unit(k, c)))
        if kind == "w_out":
            layer, (tile, width) = shape
            return pl.BlockSpec((None, tile, width), lambda k, c: (layer, unit(k, c), 0))
        if kind == "units":
            rows, tile = shape
            return pl.BlockSpec((rows, tile), lambda k, c: (0, unit(k, c)))
        if kind == "send":
            return pl.BlockSpec((1,) + shape[1:], lambda k, c: (jnp.minimum(k, half - 1), 0, 0, 0))
        if kind == "own":
            return pl.BlockSpec((1,) + shape[1:], lambda k, c: (jnp.maximum(k - half, 0), 0, 0, 0))
        rest = len(shape)
        return pl.BlockSpec(shape, lambda k, c: (0,) * rest)

    in_specs = [whole(a) if kind == "full" else spec(kind, shape) for kind, shape, a in ins]
    kernel = pl.pallas_call(
        body,
        grid_spec=pltpu.PrefetchScalarGridSpec(
            num_scalar_prefetch=1,
            grid=(tiles,),
            in_specs=in_specs,
            out_specs=tuple(spec(kind, shape) for kind, shape, _, _ in outs),
            scratch_shapes=scratch,
        ),
        out_shape=tuple(jax.ShapeDtypeStruct(full, dtype) for _, _, full, dtype in outs),
        cost_estimate=cost(name),
        compiler_params=pltpu.CompilerParams(vmem_limit_bytes=VMEM_LIMIT),
        name=name,
    )
    return Order.run(kernel, [core] + [a for _, _, a in ins])


def store_grads(step, half, send_ref, own_ref, grad_in, grad_out):
    @pl.when(step < half)
    def _():
        send_ref[0, 0] = grad_in
        send_ref[0, 1] = grad_out

    @pl.when(step >= half)
    def _():
        own_ref[0, 0] = grad_in
        own_ref[0, 1] = grad_out


def ffn_both(core, hidden, upstream, gains, biases, norm_layer, w_in, b_in, w_out, b_out, layer):
    tokens, width = hidden.shape
    units = w_in.shape[2]
    tile = width
    tiles = units // tile

    def body(_, h_ref, up_ref, g_ref, b_ref, wi_ref, bi_ref, wo_ref, bo_ref,
             out_ref, grad_ref, send_ref, own_ref, dbi_ref, small_ref, n_ref, nt_ref, acc_ref, dn_ref):
        step = pl.program_id(0)

        @pl.when(step == 0)
        def _():
            normed = norm(h_ref[...], row_of(g_ref, norm_layer), row_of(b_ref, norm_layer)).astype(BF16)
            n_ref[...] = normed
            nt_ref[...] = normed.T
            acc_ref[...] = h_ref[...] + row_of(bo_ref, layer)
            dn_ref[...] = jnp.zeros_like(dn_ref)

        inner = mm(n_ref[...], wi_ref[...]) + row_of(bi_ref, layer)
        active, slope = gelu_parts(inner)
        active = active.astype(BF16)
        acc_ref[...] += mm(active, wo_ref[...])
        up = up_ref[...]
        grad_out = mm_tn(active, up).astype(BF16)
        grad_inner = (slope * mm_nt(up, wo_ref[...])).astype(BF16)
        dbi_ref[...] = jnp.sum(grad_inner.astype(F32), 0, keepdims=True)
        store_grads(step, tiles // 2, send_ref, own_ref, mm(nt_ref[...], grad_inner).astype(BF16), grad_out)
        dn_ref[...] += mm_nt(grad_inner, wi_ref[...])

        @pl.when(step == tiles - 1)
        def _():
            out_ref[...] = acc_ref[...].astype(BF16)
            top = up_ref[...].astype(F32)
            back, grad_gain, grad_bias = norm_back(h_ref[...], row_of(g_ref, norm_layer), dn_ref[...])
            grad_ref[...] = top + back
            small_ref[...] = jnp.concatenate([grad_gain, grad_bias, jnp.sum(top, 0, keepdims=True)], 0)

    ins = [
        ("full", None, hidden), ("full", None, upstream), ("full", None, gains), ("full", None, biases),
        ("w_in", (layer, (width, tile)), w_in), ("units", (b_in.shape[0], tile), b_in),
        ("w_out", (layer, (tile, width)), w_out), ("full", None, b_out),
    ]
    half = (tiles // 2, 2, width, tile)
    outs = [
        ("all", (tokens, width), (tokens, width), BF16), ("all", (tokens, width), (tokens, width), F32),
        ("send", half, half, BF16), ("own", half, half, BF16),
        ("units", (1, tile), (1, units), F32), ("all", (3, width), (3, width), F32),
    ]
    scratch = [
        pltpu.VMEM((tokens, width), BF16), pltpu.VMEM((width, tokens), BF16),
        pltpu.VMEM((tokens, width), F32), pltpu.VMEM((tokens, width), F32),
    ]
    return grad_call(body, core, ins, outs, scratch, tiles, "ffn_both")


def ffn_back(core, upstream, grad_kvs, kv_weight, memory, hidden, normed, active, slope, gains, norm_layer, w_in, w_out, layer):
    tokens, width = hidden.shape
    units = w_in.shape[2]
    tile = width
    tiles = units // tile
    blocks = len(grad_kvs)

    def body(*refs):
        up_ref = refs[1]
        kv_refs = refs[2 : 2 + blocks]
        (kw_ref, mem_ref, h_ref, n_in, z_ref, s_ref, g_ref, wi_ref, wo_ref,
         grad_ref, dkw_ref, send_ref, own_ref, dbi_ref, small_ref, nt_ref, top_ref, dn_ref) = refs[2 + blocks :]
        step = pl.program_id(0)

        @pl.when(step == 0)
        def _():
            nt_ref[...] = n_in[...].T
            grad_kv = kv_refs[0][...].astype(F32)
            for ref in kv_refs[1:]:
                grad_kv = grad_kv + ref[...].astype(F32)
            grad_kv = grad_kv.astype(BF16)
            dkw_ref[...] = mm_tn(mem_ref[...], grad_kv)
            top = up_ref[...].astype(F32) + mm_nt(grad_kv, kw_ref[...])
            grad_ref[...] = top
            top_ref[...] = top.astype(BF16)
            dn_ref[...] = jnp.zeros_like(dn_ref)

        top = top_ref[...]
        grad_out = mm_tn(z_ref[...], top).astype(BF16)
        grad_inner = (s_ref[...].astype(F32) * mm_nt(top, wo_ref[...])).astype(BF16)
        dbi_ref[...] = jnp.sum(grad_inner.astype(F32), 0, keepdims=True)
        store_grads(step, tiles // 2, send_ref, own_ref, mm(nt_ref[...], grad_inner).astype(BF16), grad_out)
        dn_ref[...] += mm_nt(grad_inner, wi_ref[...])

        @pl.when(step == tiles - 1)
        def _():
            back, grad_gain, grad_bias = norm_back(h_ref[...], row_of(g_ref, norm_layer), dn_ref[...])
            grad_ref[...] += back
            grad_top = jnp.sum(top_ref[...].astype(F32), 0, keepdims=True)
            small_ref[...] = jnp.concatenate([grad_gain, grad_bias, grad_top], 0)

    ins = [("full", None, a) for a in (upstream, *grad_kvs, kv_weight, memory, hidden, normed)] + [
        ("units", (tokens, tile), active), ("units", (tokens, tile), slope), ("full", None, gains),
        ("w_in", (layer, (width, tile)), w_in), ("w_out", (layer, (tile, width)), w_out),
    ]
    half = (tiles // 2, 2, width, tile)
    outs = [
        ("all", (tokens, width), (tokens, width), F32), ("all", (width, PAIR), (width, PAIR), F32),
        ("send", half, half, BF16), ("own", half, half, BF16),
        ("units", (1, tile), (1, units), F32), ("all", (3, width), (3, width), F32),
    ]
    scratch = [
        pltpu.VMEM((width, tokens), BF16), pltpu.VMEM((tokens, width), BF16), pltpu.VMEM((tokens, width), F32),
    ]
    return grad_call(body, core, ins, outs, scratch, tiles, "ffn_back")


def digit_of(axis, count):
    if isinstance(axis, tuple):
        return (lax.axis_index(axis[0]) >> axis[1]) & (count - 1)
    return lax.axis_index(axis)


def swap(value, axis, size, mask):
    return lax.ppermute(value, axis, [(i, i ^ mask) for i in range(size)])


def every_block(value, axis, size):
    return [value] + [swap(value, axis, size, d) for d in range(1, size)]


def give_back(blocks, axis, size):
    return [blocks[0]] + [swap(blocks[d], axis, size, d) for d in range(1, size)]


def row_chunks(rows, most=256):
    return [(at, min(most, rows - at)) for at in range(0, rows, most)]


def fold(groups, merge=False, dtype=BF16, name="fold"):
    args, outs, places = [], [], []
    total = 0
    for addends, axis, count in groups:
        rows, columns = addends[0].shape
        places.append((len(args), total))
        args += list(addends)
        total += rows // count
        if not merge:
            outs += [((rows // count, columns), dtype)] * count
    if merge:
        outs = [((total, groups[0][0][0].shape[1]), dtype)] * groups[0][2]

    def body(*refs):
        out_refs = refs[len(args) :]
        at_out = 0
        for (addends, axis, count), (at, row) in zip(groups, places):
            ins = refs[at : at + len(addends)]
            rows = ins[0].shape[0] // count
            for d in range(count):
                for start, size in row_chunks(rows):
                    place = pl.ds(d * rows + start, size)
                    if axis is not None:
                        place = pl.ds(pl.multiple_of((digit_of(axis, count) ^ d) * rows + start, 16), size)
                    part = ins[0][place].astype(F32)
                    for ref in ins[1:]:
                        part = part + ref[place].astype(F32)
                    if merge:
                        out_refs[d][row + start : row + start + size] = part.astype(dtype)
                    else:
                        out_refs[at_out + d][start : start + size] = part.astype(dtype)
            at_out += count

    outs = call(body, outs, args, name=name)
    if merge:
        return list(outs)
    result, at = [], 0
    for _, _, count in groups:
        result.append(list(outs[at : at + count]))
        at += count
    return result


def unfold(groups, sizes=None, dtype=BF16, name="unfold"):
    args, outs = [], []
    for blocks, axis, count in groups:
        rows, columns = blocks[0].shape
        args += list(blocks)
        for size in sizes or [rows]:
            outs.append(((size * count, columns), dtype))

    def body(*refs):
        out_refs = refs[len(args) :]
        at = at_out = 0
        for blocks, axis, count in groups:
            ins = refs[at : at + count]
            at += count
            digit = digit_of(axis, count)
            for d in range(count):
                row = 0
                for k, size in enumerate(sizes or [ins[0].shape[0]]):
                    base = (digit ^ d) * size
                    for start, part in row_chunks(size):
                        place = pl.ds(pl.multiple_of(base + start, 16), part)
                        out_refs[at_out + k][place] = ins[d][row + start : row + start + part].astype(dtype)
                    row += size
            at_out += len(sizes or [1])

    return call(body, outs, args, name=name)


def place_grads(core, own, other, layer, shapes, before, name):
    pieces = [*own, *other]
    half = len(own)
    _, _, width, tile = own[0].shape

    def body(*refs):
        parts = refs[1 : 1 + 2 * half]
        in_ref, out_ref = refs[-2:]
        for k in range(2 * half):

            @pl.when(pl.program_id(0) == k)
            def _():
                in_ref[...] = parts[k][0].astype(F32)
                out_ref[...] = parts[k][1].astype(F32)

    def unit(k, core_ref):
        near = jnp.where(k < half, core_ref[0], 1 - core_ref[0])
        return near * half + lax.rem(k, half)

    kernel = pl.pallas_call(
        body,
        grid_spec=pltpu.PrefetchScalarGridSpec(
            num_scalar_prefetch=1,
            grid=(2 * half,),
            in_specs=[pl.BlockSpec((None, 2, width, tile), lambda k, c: (0, 0, 0, 0)) for _ in pieces]
            + [pl.BlockSpec(memory_space=pl.ANY) for _ in before],
            out_specs=(
                pl.BlockSpec((None, width, tile), lambda k, c: (layer, 0, unit(k, c))),
                pl.BlockSpec((None, tile, width), lambda k, c: (layer, unit(k, c), 0)),
            ),
        ),
        out_shape=tuple(jax.ShapeDtypeStruct(shape, F32) for shape in shapes),
        input_output_aliases={1 + len(pieces) + i: i for i in range(len(before))},
        cost_estimate=cost(name),
        compiler_params=pltpu.CompilerParams(vmem_limit_bytes=VMEM_LIMIT),
        name=name,
    )
    return Order.run(kernel, [core, *pieces, *before])


def place_first(core, own, other, units):
    width = own[0].shape[2]
    return place_grads(core, own, other, 1, [(2, width, units), (2, units, width)], [], "place_first")


def place_second(core, own, other, grad_in, grad_out):
    return place_grads(core, own, other, 0, [grad_in.shape, grad_out.shape], [grad_in, grad_out], "place_second")


def place_experts(core_pairs, per, width):
    args = [part for own, other, _ in core_pairs for part in (own, other)]
    subs = sum(len(layers) for _, _, layers in core_pairs)
    half = width // 2

    def body(*refs):
        out_ref = refs[-1]
        core = lax.axis_index("core")
        for k, (_, _, layers) in enumerate(core_pairs):
            for place, ref in ((core, refs[2 * k]), (1 - core, refs[2 * k + 1])):
                for i, layer in enumerate(layers):
                    for expert in range(per):
                        at = (i * per + expert) * half
                        row = pl.multiple_of(place * half, half)
                        out_ref[layer, expert, pl.ds(row, half)] = ref[at : at + half].astype(F32)

    return call(body, [((subs, per, width, PAIR), F32)], args, name="place_experts")[0]


def lanes(count):
    return [slice(c * PAIR, (c + 1) * PAIR) for c in range(count)]


def pack_small(kvs, routers, rows, in_biases):
    args = [*kvs, *routers, *rows, *in_biases]
    width = kvs[0].shape[0]
    wide = width // PAIR
    units = in_biases[0].shape[1]
    used = len(kvs) * width + len(routers) * wide * EXPERTS + sum(r.shape[0] for r in rows) * wide
    used += len(in_biases) * (units // PAIR)
    total = used + -used % 1024

    def body(*refs):
        ins, outs, buffer = refs[: len(args)], refs[len(args) : -1], refs[-1]
        at = 0
        for ref in ins[: len(kvs)]:
            buffer[at : at + width] = ref[...]
            at += width
        ins = ins[len(kvs) :]
        for ref in ins[: len(routers)]:
            for lane in lanes(wide):
                buffer[at : at + EXPERTS] = ref[:, lane]
                at += EXPERTS
        for ref in ins[len(routers) :]:
            for row in range(ref.shape[0]):
                for lane in lanes(ref.shape[1] // PAIR):
                    buffer[at : at + 1] = ref[row : row + 1, lane]
                    at += 1
        buffer[at:] = jnp.zeros((total - at, PAIR), F32)
        share = total // 2
        digit = lax.axis_index("core")
        for d in range(2):
            outs[d][...] = buffer[pl.ds(pl.multiple_of((digit ^ d) * share, share), share)].astype(BF16)

    return call(
        body, [((total // 2, PAIR), BF16)] * 2, args, scratch=[pltpu.VMEM((total, PAIR), F32)], name="pack_small"
    )


def unpack_small(parts, counts, width, units):
    share = parts[0].shape[0]
    n_kv, n_router, picks, n_bias = counts
    wide = width // PAIR
    outs = [((n_kv, width, PAIR), F32), ((n_router, EXPERTS, width), F32)]
    outs += [((len(pick), width), F32) for pick in picks] + [((n_bias, units), F32)]
    n_rows = sum(len(pick) for pick in picks)

    def body(*refs):
        ins, outs, buffer = refs[:2], refs[2:-1], refs[-1]
        digit = lax.axis_index("core")
        for d in range(2):
            buffer[pl.ds(pl.multiple_of((digit ^ d) * share, share), share)] = ins[d][...].astype(F32)
        at = 0
        for i in range(n_kv):
            outs[0][i] = buffer[at : at + width]
            at += width
        for i in range(n_router):
            for lane in lanes(wide):
                outs[1][i, :, lane] = buffer[at : at + EXPERTS]
                at += EXPERTS
        for out, pick in zip(outs[2:-1], picks):
            for k, row in enumerate(pick):
                for c, lane in enumerate(lanes(wide)):
                    place = at + row * wide + c
                    out[k : k + 1, lane] = buffer[place : place + 1]
        at += n_rows * wide
        for i in range(n_bias):
            for lane in lanes(units // PAIR):
                outs[-1][i : i + 1, lane] = buffer[at : at + 1]
                at += 1

    return call(body, outs, parts, scratch=[pltpu.VMEM((2 * share, PAIR), F32)], name="unpack_small")


def after(value, *first):
    return lax.optimization_barrier((value, first))[0]


def shards(
    sizes, enc_input, dec_input, enc_segments, dec_segments, routes, enc_out_grad, dec_out_grad,
    enc_gains, enc_biases, dec_gains, dec_biases, kv_weights, router_weights, expert_weights,
    ffn_in, ffn_in_bias, ffn_out, ffn_out_bias,
):
    n_core, n_y, n_ep, n_seq = sizes["core"], sizes["y"], sizes["ep"], sizes["seq"]
    rows, span, width = enc_input.shape
    tokens = rows * span
    per = expert_weights.shape[1]
    units = ffn_in.shape[2]
    core = lax.axis_index("core").astype(jnp.int32).reshape(1)
    Order.start()

    flat = lambda a: a.reshape(tokens, a.shape[-1])
    enc_x, dec_x = flat(enc_input), flat(dec_input)
    enc_up, dec_up = flat(enc_out_grad), flat(dec_out_grad)
    kv_w = [Layer(kv_weights, i) for i in range(3)]
    router_t = router_weights.transpose(0, 2, 1)
    routers = [Layer(router_t, i) for i in range(3)]

    n_one, kv_one, w_send = norm_kv(enc_x, enc_gains, enc_biases, kv_weights, 0, 0, expert_weights, [0])
    w_enc = [Layer(expert_weights, 0)] + every_block(w_send, "ep", n_ep)[1:]
    kvs_one = every_block(kv_one, "seq", n_seq)
    n_three, kv_three, *w_sends = norm_kv(dec_x, dec_gains, dec_biases, kv_weights, 0, 1, expert_weights, [1, 2])
    meta, q_rows = prepare(routes.transpose(0, 1, 3, 2), enc_segments, dec_segments, n_ep, n_seq, per)
    q_one, aux_one = queries(n_one, w_enc, routers[0], meta, 0)
    w_got = every_block(after(w_sends[0], *w_enc[1:]), "ep", n_ep)
    w_dec = [Layer(expert_weights, 1)] + w_got[1:]
    w_cross = [Layer(expert_weights, 2)] + every_block(after(w_sends[1], *w_got[1:]), "ep", n_ep)[1:]
    o_one, lse_one, enc_mid = attend(
        enc_x, q_one, aux_one, kvs_one, w_enc, meta, q_rows, 0, 0, 0, False
    )
    kvs_three = every_block(after(kv_three, *kvs_one[1:]), "seq", n_seq)
    n_two, z_two, slope_two, memory, kv_mem = ffn_forward(
        enc_mid, enc_gains, enc_biases, 1, ffn_in, ffn_in_bias, ffn_out, ffn_out_bias, 0, kv_weights[2], 4
    )
    kvs_mem = every_block(kv_mem, "seq", n_seq)
    q_three, aux_three = queries(n_three, w_dec, routers[1], meta, 1)
    o_three, lse_three, dec_mid = attend(
        dec_x, q_three, aux_three, kvs_three, w_dec, meta, q_rows, 1, 1, 1, True
    )
    n_four, q_four, aux_four = norm_queries(dec_mid, dec_gains, dec_biases, 1, w_cross, routers[2], meta, 2)
    o_four, lse_four, dec_late = attend(
        dec_mid, q_four, aux_four, kvs_mem, w_cross, meta, q_rows, 2, 1, 0, False
    )

    other_core = lambda a: swap(a, "core", n_core, 1)
    two = lambda a: a.reshape(2, a.shape[0] // 2, a.shape[1])

    def first_parts(own, got, name):
        pairs = [[Layer(two(own), i), Layer(two(got), i)] for i in range(2)]
        a, b = fold([(pairs[0], "ep", n_ep), (pairs[1], "y", n_y)], name=name)
        return give_back(a, "ep", n_ep), give_back(b, "y", n_y)

    def second_parts(a, b, name):
        a, b = fold([(a, "y", n_y), (b, "ep", n_ep)], name=name)
        return give_back(a, "y", n_y), give_back(b, "ep", n_ep)

    near, far = (("seq", 0), 2), (("seq", 1), n_seq // 2)

    def near_swap(blocks):
        return [blocks[0], swap(blocks[1], "seq", n_seq, 1)]

    def far_swap(blocks):
        return [blocks[0]] + [swap(blocks[d], "seq", n_seq, 2 * d) for d in range(1, far[1])]

    def z_near(groups, name):
        return near_swap(fold([(addends, *near) for addends in groups], merge=True, name=name))

    def z_far(parts, name):
        return far_swap(fold([(parts, *far)], name=name)[0])

    def z_all(parts, name):
        ((done,),) = fold([(parts, None, 1)], name=name)
        return far_swap([done] * far[1])

    def z_back(parts, name):
        (done,) = unfold([(parts, *far)], name=name)
        return near_swap([done] * 2)

    def back_second(parts, name):
        share = parts[0].shape[0] // 2
        a, b = unfold([(parts, *near)], [share, share], name=name)
        return every_block(a, "y", n_y), every_block(b, "ep", n_ep)

    def back_first(a, b, name):
        a, b = unfold([(a, "y", n_y), (b, "ep", n_ep)], name=name)
        return every_block(a, "ep", n_ep), every_block(b, "y", n_y)

    def back_core(a, b, name):
        parts = unfold([(a, "ep", n_ep), (b, "y", n_y)], name=name)
        return list(parts), [other_core(part) for part in parts]

    dec_out, grad_late, dec_send, dec_own, dbi_dec, small_dec = ffn_both(
        core, dec_late, dec_up, dec_gains, dec_biases, 2, ffn_in, ffn_in_bias, ffn_out, ffn_out_bias, 1
    )
    half = (dec_own.shape[0] * 2 * width, dec_own.shape[3])
    dec_got = other_core(dec_send.reshape(half))
    dkv_mem, dq_four, dlog_four = attend_back(
        grad_late, o_four, q_four, aux_four, lse_four, kvs_mem, w_cross, meta, q_rows, 2, 1, 0, False
    )
    dkv_mem = give_back(dkv_mem, "seq", n_seq)
    dec_a, dec_b = first_parts(dec_own.reshape(half), dec_got, "dec_first")
    cross_own, cross_send, dr_cross, grad_mid, small_cross = expert_back(
        grad_late, n_four, o_four, aux_four, dq_four, dlog_four, w_cross, routers[2], meta, 2,
        dec_mid, dec_gains, 1
    )
    cross_got = other_core(cross_send)
    dkv_three, dq_three, dlog_three = attend_back(
        grad_mid, o_three, q_three, aux_three, lse_three, kvs_three, w_dec, meta, q_rows, 1, 1, 1, True
    )
    dkv_three = give_back(dkv_three, "seq", n_seq)
    dec_a, dec_b = second_parts(dec_a, dec_b, "dec_second")
    grad_enc, dkw_cross, enc_send, enc_own, dbi_enc, small_enc = ffn_back(
        core, enc_up, dkv_mem, kv_w[2], memory, enc_mid, n_two, z_two, slope_two, enc_gains, 1,
        ffn_in, ffn_out, 0,
    )
    enc_got = other_core(enc_send.reshape(half))
    dkv_one, dq_one, dlog_one = attend_back(
        grad_enc, o_one, q_one, aux_one, lse_one, kvs_one, w_enc, meta, q_rows, 0, 0, 0, False
    )
    dkv_one = give_back(dkv_one, "seq", n_seq)
    enc_a, enc_b = first_parts(enc_own.reshape(half), enc_got, "enc_first")
    dec_parts = z_near([dec_a, dec_b], "dec_near")
    enc_own_x, enc_send_x, dr_enc, dn_one = expert_back(
        grad_enc, n_one, o_one, aux_one, dq_one, dlog_one, w_enc, routers[0], meta, 0
    )
    enc_got_x = other_core(enc_send_x)
    dec_own_x, dec_send_x, dr_dec, dn_three = expert_back(
        grad_mid, n_three, o_three, aux_three, dq_three, dlog_three, w_dec, routers[1], meta, 1
    )
    dec_got_x = other_core(dec_send_x)
    dec_grad, dkw_dec, small_three = self_finish(
        grad_mid, dn_three, dkv_three, n_three, kv_w[1], dec_x, dec_gains, 0
    )
    dec_parts = z_far(dec_parts, "dec_far")
    x_one = fold([([cross_own, cross_got], None, n_ep), ([dec_own_x, dec_got_x], None, n_ep)], True, name="x_one")
    x_one = give_back(x_one, "ep", n_ep)
    enc_grad, dkw_enc, small_one = self_finish(
        grad_enc, dn_one, dkv_one, n_one, kv_w[0], enc_x, enc_gains, 0
    )
    small_own, small_send = pack_small(
        [dkw_enc, dkw_dec, dkw_cross], [dr_enc, dr_dec, dr_cross],
        [small_one, small_enc, small_three, small_cross, small_dec], [dbi_enc, dbi_dec],
    )
    small_got = other_core(small_send)
    enc_a, enc_b = second_parts(enc_a, enc_b, "enc_second")
    dec_parts = z_all(dec_parts, "dec_all")
    x_two = fold([([enc_own_x, enc_got_x], None, n_ep), ([small_own, small_got], "ep", n_ep)], True, name="x_two")
    x_two = give_back(x_two, "ep", n_ep)
    enc_parts = z_near([enc_a, enc_b], "enc_near")
    dec_parts = z_back(dec_parts, "dec_back_far")
    enc_parts = z_far(enc_parts, "enc_far")
    n_small = small_own.shape[0] // n_ep
    n_enc = x_two[0].shape[0] - n_small
    x_parts = fold([
        (x_one, "y", n_y), ([Rows(part, n_enc, 0) for part in x_two], "y", n_y),
        ([Rows(part, n_small, n_enc // n_small) for part in x_two], "y", n_y),
    ], True, name="x_y")
    x_parts = give_back(x_parts, "y", n_y)
    enc_parts = z_all(enc_parts, "enc_all")
    dec_a, dec_b = back_second(dec_parts, "dec_back_near")
    x_parts = z_near([x_parts], "x_near")
    enc_parts = z_back(enc_parts, "enc_back_far")
    dec_a, dec_b = back_first(dec_a, dec_b, "dec_back_second")
    x_parts = z_far(x_parts, "x_far")
    enc_a, enc_b = back_second(enc_parts, "enc_back_near")
    x_parts = z_all(x_parts, "x_all")
    dec_ab, dec_other = back_core(dec_a, dec_b, "dec_back_first")
    enc_a, enc_b = back_first(enc_a, enc_b, "enc_back_second")
    x_parts = z_back(x_parts, "x_back_far")
    pieces = lambda parts: [part.reshape((-1, 2, width) + dec_own.shape[3:]) for part in parts]
    grad_in, grad_out = place_first(core, pieces(dec_ab), pieces(dec_other), units)
    (x_part,) = unfold([(x_parts, *near)], name="x_back_near")
    x_parts = every_block(x_part, "y", n_y)
    enc_ab, enc_other = back_core(enc_a, enc_b, "enc_back_first")
    x_one, x_two, small_part = unfold(
        [(x_parts, "y", n_y)], [2 * n_enc // n_y, n_enc // n_y, n_small // n_y], name="x_back_y"
    )
    small_parts = every_block(small_part, "ep", n_ep)
    x_one_other, x_two_other = other_core(x_one), other_core(x_two)
    grad_in, grad_out = place_second(core, pieces(enc_ab), pieces(enc_other), grad_in, grad_out)
    (small_half,) = unfold([(small_parts, "ep", n_ep)], name="small_back_x")
    small_parts = every_block(small_half, "core", n_core)
    experts = place_experts([(x_one, x_one_other, (2, 1)), (x_two, x_two_other, (0,))], per, width)
    picks = [[0, 2], [1, 3], [5, 7, 9], [6, 8, 10], [4, 11]]
    kv_grad, router_grad, enc_gain, enc_bias, dec_gain, dec_bias, out_bias, in_bias = unpack_small(
        small_parts, (3, 3, picks, 2), width, units
    )
    shape = enc_input.shape
    return (
        memory.reshape(shape), dec_out.reshape(shape), enc_grad.reshape(shape), dec_grad.reshape(shape),
        enc_gain, enc_bias, dec_gain, dec_bias, kv_grad, router_grad.transpose(0, 2, 1), experts,
        grad_in, in_bias, grad_out, out_bias,
    )


def solution(mesh):
    sizes = dict(mesh.shape)
    n_dp, n_ep, n_seq = sizes["dp"], sizes["ep"], sizes["seq"]
    split = jax.sharding.Mesh(mesh.devices.reshape(n_dp // 2, 2, n_ep, n_seq), ("y", "core", "ep", "seq"))
    batch = ("y", "core", "ep")
    tokens = P(batch, "seq", None)
    rows = P(batch, None)
    experts = P(None, "ep", None, None)
    return jax.shard_map(
        partial(shards, dict(split.shape)),
        mesh=split,
        in_specs=(
            tokens, tokens, rows, rows, P(None, batch, "seq", None), tokens, tokens,
            P(), P(), P(), P(), P(), P(), experts, P(), P(), P(), P(),
        ),
        out_specs=(
            tokens, tokens, tokens, tokens, P(), P(), P(), P(), P(), P(), experts, P(), P(), P(), P(),
        ),
        check_vma=False,
    )
```

```python
from functools import partial

import jax
import jax.numpy as jnp
from jax import lax
from jax.experimental import pallas as pl
from jax.experimental.pallas import tpu as pltpu
from jax.sharding import PartitionSpec as P

EXPERTS = 8
HD = 64
TOP = 2
PAIR = 2 * HD

EPS = 1e-05
SCALE = 0.125
NEG = -1e30
F32 = jnp.float32
BF16 = jnp.bfloat16
SQRT_HALF = 0.7071067811865476
INV_SQRT_2PI = 0.3989422804014327
VMEM_LIMIT = 20 * 1024 * 1024

ROUTE = 0
LOCAL_ROUTE = 6
KEY_SEG = 12


def mm(left, right):
    return lax.dot_general(left, right, (((1,), (0,)), ((), ())), preferred_element_type=F32)


def mm_nt(left, right):
    return lax.dot_general(left, right, (((1,), (1,)), ((), ())), preferred_element_type=F32)


def mm_tn(left, right):
    return lax.dot_general(left, right, (((0,), (0,)), ((), ())), preferred_element_type=F32)


def iota(shape, dim):
    return lax.broadcasted_iota(jnp.int32, shape, dim)


def standardize(hidden):
    centred = hidden - jnp.mean(hidden, -1, keepdims=True)
    inverse = lax.rsqrt(jnp.mean(centred * centred, -1, keepdims=True) + EPS)
    return centred * inverse, inverse


def norm(hidden, gain, bias):
    return standardize(hidden)[0] * gain + bias


def norm_back(hidden, gain, upstream):
    unit, inverse = standardize(hidden)
    grad_gain = jnp.sum(upstream * unit, 0, keepdims=True)
    grad_bias = jnp.sum(upstream, 0, keepdims=True)
    scaled = upstream * gain
    centred = scaled - jnp.mean(scaled, -1, keepdims=True)
    projected = jnp.mean(scaled * unit, -1, keepdims=True)
    return inverse * (centred - unit * projected), grad_gain, grad_bias


def widened(router):
    full = router.astype(F32)
    return jnp.concatenate([full, jnp.zeros((PAIR - full.shape[0], full.shape[1]), F32)], 0).astype(BF16)


def row_of(ref, index):
    return ref[...].astype(F32)[index : index + 1]


class Order:
    last = None
    share = 1.0

    @classmethod
    def start(cls):
        cls.last = None
        cls.share = 1.0

    @classmethod
    def run(cls, kernel, args):
        args = [operand(arg) for arg in args]
        if cls.last is not None:
            args[0], _ = lax.optimization_barrier((args[0], cls.last))
        outs = kernel(*args)
        cls.last = outs[0]
        return outs


class Layer:
    def __init__(self, array, index):
        self.array, self.index = array, index
        self.shape = array.shape[1:]

    def spec(self):
        index, rest = self.index, len(self.shape)
        return pl.BlockSpec((None,) + self.shape, lambda *_: (index,) + (0,) * rest)


class Rows:
    def __init__(self, array, rows, index):
        self.array, self.index = array, index
        self.shape = (rows, array.shape[1])

    def spec(self):
        index = self.index
        return pl.BlockSpec(self.shape, lambda *_: (index, 0))


def operand(arg):
    return arg.array if isinstance(arg, (Layer, Rows)) else arg


def whole(arg):
    if isinstance(arg, (Layer, Rows)):
        return arg.spec()
    rest = len(arg.shape)
    return pl.BlockSpec(arg.shape, lambda *_: (0,) * rest)


TIMES = {
    "norm_kv": 0.7, "prepare": 0.3, "queries": 2.0, "norm_queries": 2.3, "attend": 3.4, "ffn_forward": 6.2,
    "ffn_both": 12.0, "attend_back": 5.0, "expert_back": 3.4, "ffn_back": 8.5, "self_finish": 2.0,
    "place_first": 3.5, "place_second": 3.5, "unpack_small": 1.0,
}
PACE = 1.0
LATER = 4.0
FOLD = 0.4
LIGHT = 0.05
ROOMY = 60 * 1024 * 1024


def cost(name):
    first = ("norm_kv", "prepare", "queries", "norm_queries", "attend", "ffn_forward", "ffn_both")
    micros = TIMES.get(name, FOLD) * (PACE if name in first else LATER)
    micros *= Order.share
    return pl.CostEstimate(flops=int(micros * 1e9), bytes_accessed=int(micros * 3e6), transcendentals=0)


def call(body, outs, args, scratch=(), limit=14 * 1024 * 1024, name=None):
    shapes = [jax.ShapeDtypeStruct(s, d) for s, d in outs]
    kernel = pl.pallas_call(
        body,
        grid=(1,),
        out_shape=tuple(shapes),
        in_specs=[whole(arg) for arg in args],
        out_specs=tuple(whole(out) for out in shapes),
        scratch_shapes=list(scratch),
        cost_estimate=cost(name),
        compiler_params=pltpu.CompilerParams(vmem_limit_bytes=limit),
        name=name,
    )
    return Order.run(kernel, args)


def prepare(routes, enc_seg, dec_seg, n_ep, n_seq, per):
    subs, rows, _, span = routes.shape
    tokens = rows * span
    used = 2 * subs * TOP + 2 * n_seq

    def body(r_ref, e_ref, d_ref, meta_ref, rows_ref):
        base = lax.axis_index("ep") * per
        me = lax.axis_index("seq")
        lines = []
        for flip in (False, True):
            for sub in range(subs):
                for j in range(TOP):
                    line = jnp.concatenate([r_ref[sub, r, j : j + 1, :] for r in range(rows)], 1)
                    lines.append(line ^ base if flip else line)
        queries = []
        for ref in (e_ref, d_ref):
            for d in range(n_seq):
                at = pl.multiple_of((me ^ d) * span, span)
                block = ref[:, pl.ds(at, span)]
                lines.append(jnp.concatenate([block[r : r + 1] for r in range(rows)], 1))
                if d == 0:
                    queries.append(jnp.concatenate([block] * TOP, 1))
        rows_ref[...] = jnp.concatenate(queries, 0)
        lines = [line.astype(F32) for line in lines]
        lines.append(jnp.zeros((PAIR - used, tokens), F32))
        meta_ref[...] = jnp.concatenate(lines, 0).T.astype(jnp.int32)

    return call(
        body,
        [((tokens, PAIR), jnp.int32), ((2 * rows, TOP * span), jnp.int32)],
        (routes, enc_seg, dec_seg),
        name="prepare",
    )


def norm_kv(hidden, gains, biases, kv_weights, layer, index, expert_weights, copied):
    tokens, width = hidden.shape
    stack = gains.shape[0]

    def body(h_ref, g_ref, b_ref, w_ref, e_ref, n_ref, kv_ref, *rest):
        e_outs = rest[: len(copied)]
        h_in, g_in, b_in, w_in, sems = rest[len(copied) :]
        pairs = [(h_ref, h_in), (g_ref, g_in), (b_ref, b_in), (w_ref.at[index], w_in)]
        pairs += [(e_ref.at[k], out) for k, out in zip(copied, e_outs)]
        moves = [pltpu.make_async_copy(*pair, sems.at[i]) for i, pair in enumerate(pairs)]
        for move in moves:
            move.start()
        for move in moves[:3]:
            move.wait()
        normed = norm(h_in[...].astype(F32), row_of(g_in, layer), row_of(b_in, layer)).astype(BF16)
        n_ref[...] = normed
        moves[3].wait()
        kv_ref[...] = mm(normed, w_in[...]).astype(BF16)
        for move in moves[4:]:
            move.wait()

    held = pl.BlockSpec(memory_space=pltpu.HBM)
    outs = [((tokens, width), BF16), ((tokens, PAIR), BF16)] + [(expert_weights.shape[1:], BF16)] * len(copied)
    shapes = [jax.ShapeDtypeStruct(*out) for out in outs]
    kernel = pl.pallas_call(
        body,
        out_shape=tuple(shapes),
        in_specs=[held] * 5,
        out_specs=tuple(pl.BlockSpec(memory_space=pltpu.VMEM) for _ in shapes),
        scratch_shapes=[
            pltpu.VMEM((tokens, width), BF16), pltpu.VMEM((stack, width), BF16), pltpu.VMEM((stack, width), BF16),
            pltpu.VMEM(kv_weights.shape[1:], BF16), pltpu.SemaphoreType.DMA((4 + len(copied),)),
        ],
        cost_estimate=cost("norm_kv"),
        compiler_params=pltpu.CompilerParams(vmem_limit_bytes=ROOMY),
        name="norm_kv",
    )
    return Order.run(kernel, [hidden, gains, biases, kv_weights, expert_weights])


def query_part(normed, weights, router, meta_ref, sub, q_ref, aux_ref):
    tokens = normed.shape[0]
    per = weights[0].shape[0]
    lane = iota((tokens, PAIR), 1)
    local = [meta_ref[:, LOCAL_ROUTE + TOP * sub + j : LOCAL_ROUTE + TOP * sub + j + 1] for j in range(TOP)]
    route = [meta_ref[:, ROUTE + TOP * sub + j : ROUTE + TOP * sub + j + 1] for j in range(TOP)]
    picked = [jnp.zeros((tokens, PAIR), F32) for _ in range(TOP)]
    for expert in range(EXPERTS):
        every = mm(normed, weights[expert // per][expert % per])
        picked = [jnp.where(local[j] == expert, every, picked[j]) for j in range(TOP)]
    for j in range(TOP):
        rounded = picked[j].astype(BF16).astype(F32) * SCALE
        q_ref[j] = jnp.where(lane < HD, rounded, 0.0).astype(BF16)
    logits = mm_nt(normed, widened(router))
    hit = [lane == route[j] for j in range(TOP)]
    chosen = [jnp.sum(jnp.where(hit[j], logits, 0.0), -1, keepdims=True) for j in range(TOP)]
    top = jnp.maximum(chosen[0], chosen[1])
    raised = [jnp.exp(value - top) for value in chosen]
    total = raised[0] + raised[1]
    count = jnp.where(hit[0] | hit[1], 1.0, 0.0).astype(BF16)
    before = (iota((tokens, tokens), 0) > iota((tokens, tokens), 1)).astype(F32).astype(BF16)
    ranks = mm(before, count)
    capacity = tokens * TOP // EXPERTS
    aux = jnp.zeros((tokens, PAIR), F32)
    for j in range(TOP):
        rank = jnp.sum(jnp.where(hit[j], ranks, 0.0), -1, keepdims=True)
        kept = jnp.where(rank < capacity, 1.0, 0.0)
        aux = jnp.where(lane == j, raised[j] / total, aux)
        aux = jnp.where(lane == TOP + j, kept, aux)
    aux_ref[...] = aux


def queries(normed, weights, router, meta, sub):
    tokens, width = normed.shape
    count = len(weights)

    def body(*refs):
        n_ref, w_refs = refs[0], refs[1 : 1 + count]
        r_ref, meta_ref, q_ref, aux_ref = refs[1 + count :]
        query_part(n_ref[...], w_refs, r_ref[...], meta_ref, sub, q_ref, aux_ref)

    return call(
        body,
        [((TOP, tokens, PAIR), BF16), ((tokens, PAIR), F32)],
        (normed, *weights, router, meta),
        name="queries",
    )


def norm_queries(hidden, gains, biases, layer, weights, router, meta, sub):
    tokens, width = hidden.shape
    count = len(weights)

    def body(*refs):
        h_ref, g_ref, b_ref, w_refs = refs[0], refs[1], refs[2], refs[3 : 3 + count]
        r_ref, meta_ref, n_ref, q_ref, aux_ref = refs[3 + count :]
        normed = norm(h_ref[...], row_of(g_ref, layer), row_of(b_ref, layer)).astype(BF16)
        n_ref[...] = normed
        query_part(normed, w_refs, r_ref[...], meta_ref, sub, q_ref, aux_ref)

    return call(
        body,
        [((tokens, width), BF16), ((TOP, tokens, PAIR), BF16), ((tokens, PAIR), F32)],
        (hidden, gains, biases, *weights, router, meta),
        name="norm_queries",
    )


def allowed_block(meta_ref, q_row, place, rows, column, causal):
    allowed = meta_ref[rows, column : column + 1] == q_row
    if causal:
        span, wide = rows.stop - rows.start, q_row.shape[1]
        me = lax.axis_index("seq")
        key = iota((span, wide), 0) + ((me ^ place) - me) * span
        query = lax.rem(iota((1, wide), 1), span)
        allowed = allowed & (query >= key)
    return allowed


def mixed_slots(mixed, aux, meta_ref, sub):
    scaled = [mixed[j] * (aux[:, j : j + 1] * aux[:, TOP + j : TOP + j + 1]) for j in range(TOP)]
    local = [meta_ref[:, LOCAL_ROUTE + TOP * sub + j : LOCAL_ROUTE + TOP * sub + j + 1] for j in range(TOP)]

    def of(expert):
        part = jnp.where(local[1] == expert, scaled[1], 0.0)
        return jnp.where(local[0] == expert, scaled[0], part).astype(BF16)

    return of


def attend(hidden, query, aux, key_values, weights, meta, q_rows, sub, q_base, k_base, causal):
    tokens, width = hidden.shape
    rows = q_rows.shape[0] // 2
    span = tokens // rows
    wide = TOP * span
    blocks, owners = len(key_values), len(weights)
    per = weights[0].shape[0]

    def body(*refs):
        h_ref, q_ref, aux_ref = refs[:3]
        kv_refs = refs[3 : 3 + blocks]
        w_refs = refs[3 + blocks : 3 + blocks + owners]
        meta_ref, qr_ref, o_ref, lse_ref, out_ref, s_ref = refs[3 + blocks + owners :]
        lane = iota((wide, PAIR), 1)
        for r in range(rows):
            here = slice(r * span, (r + 1) * span)
            q_row = qr_ref[q_base * rows + r : q_base * rows + r + 1, :]
            q_all = jnp.concatenate([q_ref[j, here] for j in range(TOP)], 0)
            top = jnp.full((1, wide), NEG, F32)
            for d in range(blocks):
                scores = mm_nt(kv_refs[d][here], q_all)
                allowed = allowed_block(
                    meta_ref, q_row, d, here, KEY_SEG + k_base * blocks + d, causal
                )
                scores = jnp.where(allowed, scores, NEG)
                s_ref[d * span : (d + 1) * span] = scores
                top = jnp.maximum(top, jnp.max(scores, 0, keepdims=True))
            total = jnp.zeros((1, wide), F32)
            mixed = jnp.zeros((PAIR, wide), F32)
            for d in range(blocks):
                probs = jnp.exp(s_ref[d * span : (d + 1) * span] - top)
                total = total + jnp.sum(probs, 0, keepdims=True)
                mixed = mixed + mm_tn(kv_refs[d][here], probs.astype(BF16))
            lse_ref[r : r + 1] = top + jnp.log(total)
            mixed = jnp.where(lane < HD, 0.0, (mixed / total).T).astype(BF16)
            for j in range(TOP):
                o_ref[j, here] = mixed[j * span : (j + 1) * span]
        slot = mixed_slots([o_ref[j].astype(F32) for j in range(TOP)], aux_ref[...], meta_ref, sub)
        result = h_ref[...].astype(F32)
        for expert in range(0, EXPERTS, 2):
            part = jnp.concatenate([slot(expert), slot(expert + 1)], 1)
            weight = jnp.concatenate([w_refs[e // per][e % per] for e in (expert, expert + 1)], 1)
            result = result + mm_nt(part, weight)
        out_ref[...] = result

    args = (hidden, query, aux, *key_values, *weights, meta, q_rows)
    return call(
        body,
        [((TOP, tokens, PAIR), BF16), ((rows, wide), F32), ((tokens, width), F32)],
        args,
        scratch=[pltpu.VMEM((blocks * span, wide), F32)],
        name="attend",
    )


def attend_back(upstream, mixed, query, aux, lse, key_values, weights, meta, q_rows, sub, q_base, k_base, causal):
    tokens, width = upstream.shape
    rows = q_rows.shape[0] // 2
    span = tokens // rows
    wide = TOP * span
    blocks, owners = len(key_values), len(weights)
    per = weights[0].shape[0]

    def body(*refs):
        up_ref, o_ref, q_ref, aux_ref, lse_ref = refs[:5]
        kv_refs = refs[5 : 5 + blocks]
        w_refs = refs[5 + blocks : 5 + blocks + owners]
        meta_ref, qr_ref = refs[5 + blocks + owners : 7 + blocks + owners]
        keep_ref, near_ref, dq_ref, dlog_ref, do_ref = refs[7 + blocks + owners :]
        rounded = up_ref[...].astype(BF16)
        lane = iota((tokens, PAIR), 1)
        local = [meta_ref[:, LOCAL_ROUTE + TOP * sub + j : LOCAL_ROUTE + TOP * sub + j + 1] for j in range(TOP)]
        route = [meta_ref[:, ROUTE + TOP * sub + j : ROUTE + TOP * sub + j + 1] for j in range(TOP)]
        picked = [jnp.zeros((tokens, PAIR), F32) for _ in range(TOP)]
        for expert in range(EXPERTS):
            every = mm(rounded, w_refs[expert // per][expert % per])
            picked = [jnp.where(local[j] == expert, every, picked[j]) for j in range(TOP)]
        aux = aux_ref[...]
        gate = [aux[:, j : j + 1] for j in range(TOP)]
        kept = [aux[:, TOP + j : TOP + j + 1] for j in range(TOP)]
        grad_gate = [
            kept[j] * jnp.sum(picked[j] * o_ref[j].astype(F32), -1, keepdims=True) for j in range(TOP)
        ]
        inner = gate[0] * grad_gate[0] + gate[1] * grad_gate[1]
        dlog = jnp.zeros((tokens, PAIR), F32)
        for j in range(TOP):
            dlog = jnp.where(lane == route[j], gate[j] * (grad_gate[j] - inner), dlog)
            do_ref[j] = jnp.where(lane < HD, 0.0, picked[j] * (gate[j] * kept[j])).astype(BF16)
        dlog_ref[...] = dlog.astype(BF16)
        lane = iota((wide, PAIR), 1)
        for r in range(rows):
            here = slice(r * span, (r + 1) * span)
            q_row = qr_ref[q_base * rows + r : q_base * rows + r + 1, :]
            q_all = jnp.concatenate([q_ref[j, here] for j in range(TOP)], 0)
            do_all = jnp.concatenate([do_ref[j, here] for j in range(TOP)], 0)
            log_total = lse_ref[r : r + 1]
            inner = jnp.zeros((1, wide), F32)
            probs, grads = [], []
            for d in range(blocks):
                scores = mm_nt(kv_refs[d][here], q_all)
                allowed = allowed_block(
                    meta_ref, q_row, d, here, KEY_SEG + k_base * blocks + d, causal
                )
                prob = jnp.exp(jnp.where(allowed, scores, NEG) - log_total)
                grad = mm_nt(kv_refs[d][here], do_all)
                inner = inner + jnp.sum(prob * grad, 0, keepdims=True)
                probs.append(prob)
                grads.append(grad)
            grad_query = jnp.zeros((PAIR, wide), F32)
            for d in range(blocks):
                grad_score = (probs[d] * (grads[d] - inner)).astype(BF16)
                grad_query = grad_query + mm_tn(kv_refs[d][here], grad_score)
                grad_kv = mm(probs[d].astype(BF16), do_all) + mm(grad_score, q_all)
                place = slice(d // 2 * tokens + r * span, d // 2 * tokens + (r + 1) * span)
                (near_ref if d % 2 else keep_ref)[place] = grad_kv.astype(BF16)
            grad_query = jnp.where(lane < HD, grad_query.T * SCALE, 0.0).astype(BF16)
            for j in range(TOP):
                dq_ref[j, here] = grad_query[j * span : (j + 1) * span]

    args = (upstream, mixed, query, aux, lse, *key_values, *weights, meta, q_rows)
    return call(
        body,
        [((blocks // 2 * tokens, PAIR), BF16)] * 2 + [((TOP, tokens, PAIR), BF16), ((tokens, PAIR), BF16)],
        args,
        scratch=[pltpu.VMEM((TOP, tokens, PAIR), BF16)],
        name="attend_back",
    )


def expert_back(upstream, normed, mixed, aux, dq, dlog, weights, router, meta, sub, hidden=None, gains=None, layer=0):
    tokens, width = upstream.shape
    owners = len(weights)
    per = weights[0].shape[0]
    finish = hidden is not None

    def body(*refs):
        up_ref, n_ref, o_ref, aux_ref, dq_ref, dlog_ref = refs[:6]
        w_refs = refs[6 : 6 + owners]
        r_ref, meta_ref = refs[6 + owners : 8 + owners]
        at = 8 + owners
        if finish:
            h_ref, g_ref = refs[at : at + 2]
            at += 2
        own_ref, send_ref, dr_ref, dn_ref = refs[at : at + 4]
        low_core = lax.axis_index("core") == 0
        half = width // 2
        slot = mixed_slots([o_ref[j].astype(F32) for j in range(TOP)], aux_ref[...], meta_ref, sub)
        local = [meta_ref[:, LOCAL_ROUTE + TOP * sub + j : LOCAL_ROUTE + TOP * sub + j + 1] for j in range(TOP)]
        grads = [dq_ref[j].astype(F32) * aux_ref[:, TOP + j : TOP + j + 1] for j in range(TOP)]

        def query_slot(expert):
            part = jnp.where(local[1] == expert, grads[1], 0.0)
            return jnp.where(local[0] == expert, grads[0], part).astype(BF16)

        normed_t = n_ref[...].T
        up_t = up_ref[...].astype(BF16).T
        total = mm(dlog_ref[...], widened(r_ref[...]))
        for expert in range(0, EXPERTS, 2):
            both = (expert, expert + 1)
            part = jnp.concatenate([query_slot(e) for e in both], 1)
            weight = jnp.concatenate([w_refs[e // per][e % per] for e in both], 1)
            total = total + mm_nt(part, weight)
            result = jnp.concatenate([slot(e) for e in both], 1)
            grad = (mm(normed_t, part) + mm(up_t, result)).astype(BF16)
            for k, e in enumerate(both):
                low, high = [grad[at : at + half, k * PAIR : (k + 1) * PAIR] for at in (0, half)]
                place = slice(e * half, (e + 1) * half)
                own_ref[place] = jnp.where(low_core, low, high)
                send_ref[place] = jnp.where(low_core, high, low)
        dr_ref[...] = mm_tn(dlog_ref[...], n_ref[...])[:EXPERTS]
        if finish:
            back, grad_gain, grad_bias = norm_back(h_ref[...].astype(F32), row_of(g_ref, layer), total)
            dn_ref[...] = up_ref[...] + back
            refs[at + 4][...] = jnp.concatenate([grad_gain, grad_bias], 0)
        else:
            dn_ref[...] = total

    outs = [((EXPERTS * width // 2, PAIR), BF16)] * 2 + [((EXPERTS, width), F32), ((tokens, width), F32)]
    args = (upstream, normed, mixed, aux, dq, dlog, *weights, router, meta)
    if finish:
        outs = outs + [((2, width), F32)]
        args = args + (hidden, gains)
    return call(body, outs, args, name="expert_back")


def added(refs):
    total = refs[0][...].astype(F32)
    for ref in refs[1:]:
        total = total + ref[...].astype(F32)
    return total.astype(BF16)


def self_finish(upstream, grad_normed, grad_kvs, normed, kv_weight, hidden, gains, layer):
    tokens, width = upstream.shape

    def body(up_ref, dn_ref, *refs):
        n_ref, w_ref, h_ref, g_ref, out_ref, dw_ref, small_ref = refs[len(grad_kvs) :]
        grad_kv = added(refs[: len(grad_kvs)])
        total = dn_ref[...] + mm_nt(grad_kv, w_ref[...])
        dw_ref[...] = mm_tn(n_ref[...], grad_kv)
        back, grad_gain, grad_bias = norm_back(h_ref[...].astype(F32), row_of(g_ref, layer), total)
        out_ref[...] = up_ref[...] + back
        small_ref[...] = jnp.concatenate([grad_gain, grad_bias], 0)

    return call(
        body,
        [((tokens, width), F32), ((width, PAIR), F32), ((2, width), F32)],
        (upstream, grad_normed, *grad_kvs, normed, kv_weight, hidden, gains),
        name="self_finish",
    )


def gelu_parts(inner):
    cdf = 0.5 * (1.0 + lax.erf(inner * SQRT_HALF))
    density = jnp.exp(-0.5 * inner * inner) * INV_SQRT_2PI
    return inner * cdf, cdf + inner * density


def ffn_call(body, tokens, width, hidden, tiles, ins, outs, scratch, name):
    tile = hidden // tiles
    kinds = {
        "full2": lambda s: pl.BlockSpec(s, lambda k: (0, 0)),
        "win": lambda s: pl.BlockSpec((1, width, tile), lambda k: (s, 0, k)),
        "bin": lambda s: pl.BlockSpec((2, tile), lambda k: (0, k)),
        "wout": lambda s: pl.BlockSpec((1, tile, width), lambda k: (s, k, 0)),
        "act": lambda s: pl.BlockSpec((tokens, tile), lambda k: (0, k)),
    }
    kernel = pl.pallas_call(
        body,
        grid=(tiles,),
        in_specs=[kinds[kind](s) for kind, s, _ in ins],
        out_specs=tuple(kinds[kind](shape) for kind, shape, _ in outs),
        out_shape=tuple(jax.ShapeDtypeStruct(shape, dtype) for _, shape, dtype in outs),
        scratch_shapes=scratch,
        cost_estimate=cost(name),
        compiler_params=pltpu.CompilerParams(vmem_limit_bytes=VMEM_LIMIT),
        name=name,
    )
    return Order.run(kernel, [a for _, _, a in ins])


def ffn_forward(hidden, gains, biases, norm_layer, w_in, b_in, w_out, b_out, layer, kv_weight, tiles):
    tokens, width = hidden.shape
    units = w_in.shape[2]

    def body(h_ref, g_ref, b_ref, wi_ref, bi_ref, wo_ref, bo_ref, kw_ref,
             n_out, z_ref, s_ref, mem_ref, kv_ref, n_ref, acc_ref):
        step = pl.program_id(0)

        @pl.when(step == 0)
        def _():
            normed = norm(h_ref[...], row_of(g_ref, norm_layer), row_of(b_ref, norm_layer)).astype(BF16)
            n_ref[...] = normed
            n_out[...] = normed
            acc_ref[...] = h_ref[...] + row_of(bo_ref, layer)

        inner = mm(n_ref[...], wi_ref[0]) + row_of(bi_ref, layer)
        active, slope = gelu_parts(inner)
        active = active.astype(BF16)
        z_ref[...] = active
        s_ref[...] = slope.astype(BF16)
        acc_ref[...] += mm(active, wo_ref[0])

        @pl.when(step == tiles - 1)
        def _():
            memory = acc_ref[...].astype(BF16)
            mem_ref[...] = memory
            kv_ref[...] = mm(memory, kw_ref[...]).astype(BF16)

    ins = [
        ("full2", hidden.shape, hidden), ("full2", gains.shape, gains), ("full2", biases.shape, biases),
        ("win", layer, w_in), ("bin", None, b_in), ("wout", layer, w_out), ("full2", b_out.shape, b_out),
        ("full2", kv_weight.shape, kv_weight),
    ]
    outs = [
        ("full2", (tokens, width), BF16), ("act", (tokens, units), BF16), ("act", (tokens, units), BF16),
        ("full2", (tokens, width), BF16), ("full2", (tokens, PAIR), BF16),
    ]
    scratch = [pltpu.VMEM((tokens, width), BF16), pltpu.VMEM((tokens, width), F32)]
    return ffn_call(body, tokens, width, units, tiles, ins, outs, scratch, "ffn_forward")


def grad_call(body, core, ins, outs, scratch, tiles, name):
    half = tiles // 2

    def unit(k, core_ref):
        far = jnp.where(k < half, 1 - core_ref[0], core_ref[0])
        return far * half + lax.rem(k, half)

    def spec(kind, shape):
        if kind == "w_in":
            layer, (width, tile) = shape
            return pl.BlockSpec((None, width, tile), lambda k, c: (layer, 0, unit(k, c)))
        if kind == "w_out":
            layer, (tile, width) = shape
            return pl.BlockSpec((None, tile, width), lambda k, c: (layer, unit(k, c), 0))
        if kind == "units":
            rows, tile = shape
            return pl.BlockSpec((rows, tile), lambda k, c: (0, unit(k, c)))
        if kind == "send":
            return pl.BlockSpec((1,) + shape[1:], lambda k, c: (jnp.minimum(k, half - 1), 0, 0, 0))
        if kind == "own":
            return pl.BlockSpec((1,) + shape[1:], lambda k, c: (jnp.maximum(k - half, 0), 0, 0, 0))
        rest = len(shape)
        return pl.BlockSpec(shape, lambda k, c: (0,) * rest)

    in_specs = [whole(a) if kind == "full" else spec(kind, shape) for kind, shape, a in ins]
    kernel = pl.pallas_call(
        body,
        grid_spec=pltpu.PrefetchScalarGridSpec(
            num_scalar_prefetch=1,
            grid=(tiles,),
            in_specs=in_specs,
            out_specs=tuple(spec(kind, shape) for kind, shape, _, _ in outs),
            scratch_shapes=scratch,
        ),
        out_shape=tuple(jax.ShapeDtypeStruct(full, dtype) for _, _, full, dtype in outs),
        cost_estimate=cost(name),
        compiler_params=pltpu.CompilerParams(vmem_limit_bytes=VMEM_LIMIT),
        name=name,
    )
    return Order.run(kernel, [core] + [a for _, _, a in ins])


def store_grads(step, half, send_ref, own_ref, grad_in, grad_out):
    @pl.when(step < half)
    def _():
        send_ref[0, 0] = grad_in
        send_ref[0, 1] = grad_out

    @pl.when(step >= half)
    def _():
        own_ref[0, 0] = grad_in
        own_ref[0, 1] = grad_out


def ffn_both(core, hidden, upstream, gains, biases, norm_layer, w_in, b_in, w_out, b_out, layer):
    tokens, width = hidden.shape
    units = w_in.shape[2]
    tile = width
    tiles = units // tile

    def body(_, h_ref, up_ref, g_ref, b_ref, wi_ref, bi_ref, wo_ref, bo_ref,
             out_ref, grad_ref, send_ref, own_ref, dbi_ref, small_ref, n_ref, nt_ref, acc_ref, dn_ref):
        step = pl.program_id(0)

        @pl.when(step == 0)
        def _():
            normed = norm(h_ref[...], row_of(g_ref, norm_layer), row_of(b_ref, norm_layer)).astype(BF16)
            n_ref[...] = normed
            nt_ref[...] = normed.T
            acc_ref[...] = h_ref[...] + row_of(bo_ref, layer)
            dn_ref[...] = jnp.zeros_like(dn_ref)

        inner = mm(n_ref[...], wi_ref[...]) + row_of(bi_ref, layer)
        active, slope = gelu_parts(inner)
        active = active.astype(BF16)
        acc_ref[...] += mm(active, wo_ref[...])
        up = up_ref[...]
        grad_out = mm_tn(active, up).astype(BF16)
        grad_inner = (slope * mm_nt(up, wo_ref[...])).astype(BF16)
        dbi_ref[...] = jnp.sum(grad_inner.astype(F32), 0, keepdims=True)
        store_grads(step, tiles // 2, send_ref, own_ref, mm(nt_ref[...], grad_inner).astype(BF16), grad_out)
        dn_ref[...] += mm_nt(grad_inner, wi_ref[...])

        @pl.when(step == tiles - 1)
        def _():
            out_ref[...] = acc_ref[...].astype(BF16)
            top = up_ref[...].astype(F32)
            back, grad_gain, grad_bias = norm_back(h_ref[...], row_of(g_ref, norm_layer), dn_ref[...])
            grad_ref[...] = top + back
            small_ref[...] = jnp.concatenate([grad_gain, grad_bias, jnp.sum(top, 0, keepdims=True)], 0)

    ins = [
        ("full", None, hidden), ("full", None, upstream), ("full", None, gains), ("full", None, biases),
        ("w_in", (layer, (width, tile)), w_in), ("units", (b_in.shape[0], tile), b_in),
        ("w_out", (layer, (tile, width)), w_out), ("full", None, b_out),
    ]
    half = (tiles // 2, 2, width, tile)
    outs = [
        ("all", (tokens, width), (tokens, width), BF16), ("all", (tokens, width), (tokens, width), F32),
        ("send", half, half, BF16), ("own", half, half, BF16),
        ("units", (1, tile), (1, units), F32), ("all", (3, width), (3, width), F32),
    ]
    scratch = [
        pltpu.VMEM((tokens, width), BF16), pltpu.VMEM((width, tokens), BF16),
        pltpu.VMEM((tokens, width), F32), pltpu.VMEM((tokens, width), F32),
    ]
    return grad_call(body, core, ins, outs, scratch, tiles, "ffn_both")


def ffn_back(core, upstream, grad_kvs, kv_weight, memory, hidden, normed, active, slope, gains, norm_layer, w_in, w_out, layer):
    tokens, width = hidden.shape
    units = w_in.shape[2]
    tile = width
    tiles = units // tile

    def body(_, up_ref, *refs):
        (kw_ref, mem_ref, h_ref, n_in, z_ref, s_ref, g_ref, wi_ref, wo_ref, grad_ref, dkw_ref,
         send_ref, own_ref, dbi_ref, small_ref, nt_ref, top_ref, dn_ref) = refs[len(grad_kvs) :]
        step = pl.program_id(0)

        @pl.when(step == 0)
        def _():
            nt_ref[...] = n_in[...].T
            grad_kv = added(refs[: len(grad_kvs)])
            dkw_ref[...] = mm_tn(mem_ref[...], grad_kv)
            top = up_ref[...].astype(F32) + mm_nt(grad_kv, kw_ref[...])
            grad_ref[...] = top
            top_ref[...] = top.astype(BF16)
            dn_ref[...] = jnp.zeros_like(dn_ref)

        top = top_ref[...]
        grad_out = mm_tn(z_ref[...], top).astype(BF16)
        grad_inner = (s_ref[...].astype(F32) * mm_nt(top, wo_ref[...])).astype(BF16)
        dbi_ref[...] = jnp.sum(grad_inner.astype(F32), 0, keepdims=True)
        store_grads(step, tiles // 2, send_ref, own_ref, mm(nt_ref[...], grad_inner).astype(BF16), grad_out)
        dn_ref[...] += mm_nt(grad_inner, wi_ref[...])

        @pl.when(step == tiles - 1)
        def _():
            back, grad_gain, grad_bias = norm_back(h_ref[...], row_of(g_ref, norm_layer), dn_ref[...])
            grad_ref[...] += back
            grad_top = jnp.sum(top_ref[...].astype(F32), 0, keepdims=True)
            small_ref[...] = jnp.concatenate([grad_gain, grad_bias, grad_top], 0)

    ins = [("full", None, a) for a in (upstream, *grad_kvs, kv_weight, memory, hidden, normed)] + [
        ("units", (tokens, tile), active), ("units", (tokens, tile), slope), ("full", None, gains),
        ("w_in", (layer, (width, tile)), w_in), ("w_out", (layer, (tile, width)), w_out),
    ]
    half = (tiles // 2, 2, width, tile)
    outs = [
        ("all", (tokens, width), (tokens, width), F32), ("all", (width, PAIR), (width, PAIR), F32),
        ("send", half, half, BF16), ("own", half, half, BF16),
        ("units", (1, tile), (1, units), F32), ("all", (3, width), (3, width), F32),
    ]
    scratch = [
        pltpu.VMEM((width, tokens), BF16), pltpu.VMEM((tokens, width), BF16), pltpu.VMEM((tokens, width), F32),
    ]
    return grad_call(body, core, ins, outs, scratch, tiles, "ffn_back")


def digit_of(axis, count):
    if isinstance(axis, tuple):
        return (lax.axis_index(axis[0]) >> axis[1]) & (count - 1)
    return lax.axis_index(axis)


def swap(value, axis, size, mask):
    return lax.ppermute(value, axis, [(i, i ^ mask) for i in range(size)])


def every_block(value, axis, size):
    return [value] + [swap(value, axis, size, d) for d in range(1, size)]


def give_back(blocks, axis, size):
    return [blocks[0]] + [swap(blocks[d], axis, size, d) for d in range(1, size)]


def row_chunks(rows, most=256):
    return [(at, min(most, rows - at)) for at in range(0, rows, most)]


def fold(groups, merge=False, dtype=BF16, name="fold"):
    args, outs, places = [], [], []
    total = 0
    for addends, axis, count in groups:
        rows, columns = addends[0].shape
        places.append((len(args), total))
        args += list(addends)
        total += rows // count
        if not merge:
            outs += [((rows // count, columns), dtype)] * count
    if merge:
        outs = [((total, groups[0][0][0].shape[1]), dtype)] * groups[0][2]

    def body(*refs):
        out_refs = refs[len(args) :]
        at_out = 0
        for (addends, axis, count), (at, row) in zip(groups, places):
            ins = refs[at : at + len(addends)]
            rows = ins[0].shape[0] // count
            for d in range(count):
                for start, size in row_chunks(rows):
                    place = pl.ds(d * rows + start, size)
                    if axis is not None:
                        place = pl.ds(pl.multiple_of((digit_of(axis, count) ^ d) * rows + start, 16), size)
                    part = ins[0][place].astype(F32)
                    for ref in ins[1:]:
                        part = part + ref[place].astype(F32)
                    if merge:
                        out_refs[d][row + start : row + start + size] = part.astype(dtype)
                    else:
                        out_refs[at_out + d][start : start + size] = part.astype(dtype)
            at_out += count

    outs = call(body, outs, args, name=name)
    if merge:
        return list(outs)
    result, at = [], 0
    for _, _, count in groups:
        result.append(list(outs[at : at + count]))
        at += count
    return result


def unfold(groups, sizes=None, joined=None, name="unfold"):
    args, outs, places = [], [], []
    for blocks, axis, count in groups:
        rows, columns = blocks[0].shape
        parts = sizes or [rows]
        at = 0
        for many in joined or [1] * len(parts):
            base = 0
            for size in parts[at : at + many]:
                places.append((len(outs), base))
                base += size * count
            outs.append(((base, columns), BF16))
            at += many
        args += list(blocks)

    def body(*refs):
        out_refs = refs[len(args) :]
        at = at_place = 0
        for blocks, axis, count in groups:
            ins = refs[at : at + count]
            at += count
            digit = digit_of(axis, count)
            parts = sizes or [ins[0].shape[0]]
            for d in range(count):
                row = 0
                for (out, first), size in zip(places[at_place : at_place + len(parts)], parts):
                    base = first + (digit ^ d) * size
                    for start, part in row_chunks(size):
                        place = pl.ds(pl.multiple_of(base + start, 16), part)
                        out_refs[out][place] = ins[d][row + start : row + start + part]
                    row += size
            at_place += len(parts)

    return call(body, outs, args, name=name)


def place_grads(core, own, other, layer, shapes, before, name):
    pieces = [*own, *other]
    half = len(own)
    _, _, width, tile = own[0].shape

    def body(*refs):
        parts = refs[1 : 1 + 2 * half]
        in_ref, out_ref = refs[-2:]
        for k in range(2 * half):

            @pl.when(pl.program_id(0) == k)
            def _():
                in_ref[...] = parts[k][0].astype(F32)
                out_ref[...] = parts[k][1].astype(F32)

    def unit(k, core_ref):
        near = jnp.where(k < half, core_ref[0], 1 - core_ref[0])
        return near * half + lax.rem(k, half)

    kernel = pl.pallas_call(
        body,
        grid_spec=pltpu.PrefetchScalarGridSpec(
            num_scalar_prefetch=1,
            grid=(2 * half,),
            in_specs=[pl.BlockSpec((None, 2, width, tile), lambda k, c: (0, 0, 0, 0)) for _ in pieces]
            + [pl.BlockSpec(memory_space=pl.ANY) for _ in before],
            out_specs=(
                pl.BlockSpec((None, width, tile), lambda k, c: (layer, 0, unit(k, c))),
                pl.BlockSpec((None, tile, width), lambda k, c: (layer, unit(k, c), 0)),
            ),
        ),
        out_shape=tuple(jax.ShapeDtypeStruct(shape, F32) for shape in shapes),
        input_output_aliases={1 + len(pieces) + i: i for i in range(len(before))},
        cost_estimate=cost(name),
        compiler_params=pltpu.CompilerParams(vmem_limit_bytes=VMEM_LIMIT),
        name=name,
    )
    return Order.run(kernel, [core, *pieces, *before])


def place_first(core, own, other, units):
    width = own[0].shape[2]
    return place_grads(core, own, other, 1, [(2, width, units), (2, units, width)], [], "place_first")


def place_second(core, own, other, grad_in, grad_out):
    return place_grads(core, own, other, 0, [grad_in.shape, grad_out.shape], [grad_in, grad_out], "place_second")


def place_experts(core_pairs, per, width):
    args = [part for own, other, _ in core_pairs for part in (own, other)]
    subs = sum(len(layers) for _, _, layers in core_pairs)
    half = width // 2

    def body(*refs):
        out_ref = refs[-1]
        core = lax.axis_index("core")
        for k, (_, _, layers) in enumerate(core_pairs):
            for place, ref in ((core, refs[2 * k]), (1 - core, refs[2 * k + 1])):
                for i, layer in enumerate(layers):
                    for expert in range(per):
                        at = (i * per + expert) * half
                        row = pl.multiple_of(place * half, half)
                        out_ref[layer, expert, pl.ds(row, half)] = ref[at : at + half].astype(F32)

    return call(body, [((subs, per, width, PAIR), F32)], args, name="place_experts")[0]


def lanes(count):
    return [slice(c * PAIR, (c + 1) * PAIR) for c in range(count)]


def pack_small(kvs, routers, rows, in_biases):
    args = [*kvs, *routers, *rows, *in_biases]
    width = kvs[0].shape[0]
    wide = width // PAIR
    units = in_biases[0].shape[1]
    used = len(kvs) * width + len(routers) * wide * EXPERTS + sum(r.shape[0] for r in rows) * wide
    used += len(in_biases) * (units // PAIR)
    total = used + -used % 1024

    def body(*refs):
        ins, outs, buffer = refs[: len(args)], refs[len(args) : -1], refs[-1]
        at = 0
        for ref in ins[: len(kvs)]:
            buffer[at : at + width] = ref[...]
            at += width
        ins = ins[len(kvs) :]
        for ref in ins[: len(routers)]:
            for lane in lanes(wide):
                buffer[at : at + EXPERTS] = ref[:, lane]
                at += EXPERTS
        for ref in ins[len(routers) :]:
            for row in range(ref.shape[0]):
                for lane in lanes(ref.shape[1] // PAIR):
                    buffer[at : at + 1] = ref[row : row + 1, lane]
                    at += 1
        buffer[at:] = jnp.zeros((total - at, PAIR), F32)
        share = total // 2
        digit = lax.axis_index("core")
        for d in range(2):
            outs[d][...] = buffer[pl.ds(pl.multiple_of((digit ^ d) * share, share), share)].astype(BF16)

    return call(
        body, [((total // 2, PAIR), BF16)] * 2, args, scratch=[pltpu.VMEM((total, PAIR), F32)], name="pack_small"
    )


def unpack_small(parts, counts, width, units):
    share = parts[0].shape[0]
    n_kv, n_router, picks, n_bias = counts
    wide = width // PAIR
    outs = [((n_kv, width, PAIR), F32), ((n_router, EXPERTS, width), F32)]
    outs += [((len(pick), width), F32) for pick in picks] + [((n_bias, units), F32)]
    n_rows = sum(len(pick) for pick in picks)

    def body(*refs):
        ins, outs, buffer = refs[:2], refs[2:-1], refs[-1]
        digit = lax.axis_index("core")
        for d in range(2):
            buffer[pl.ds(pl.multiple_of((digit ^ d) * share, share), share)] = ins[d][...].astype(F32)
        at = 0
        for i in range(n_kv):
            outs[0][i] = buffer[at : at + width]
            at += width
        for i in range(n_router):
            for lane in lanes(wide):
                outs[1][i, :, lane] = buffer[at : at + EXPERTS]
                at += EXPERTS
        for out, pick in zip(outs[2:-1], picks):
            for k, row in enumerate(pick):
                for c, lane in enumerate(lanes(wide)):
                    place = at + row * wide + c
                    out[k : k + 1, lane] = buffer[place : place + 1]
        at += n_rows * wide
        for i in range(n_bias):
            for lane in lanes(units // PAIR):
                outs[-1][i : i + 1, lane] = buffer[at : at + 1]
                at += 1

    return call(body, outs, parts, scratch=[pltpu.VMEM((2 * share, PAIR), F32)], name="unpack_small")


def after(value, *first):
    return lax.optimization_barrier((value, first))[0]


def shards(
    sizes, enc_input, dec_input, enc_segments, dec_segments, routes, enc_out_grad, dec_out_grad,
    enc_gains, enc_biases, dec_gains, dec_biases, kv_weights, router_weights, expert_weights,
    ffn_in, ffn_in_bias, ffn_out, ffn_out_bias,
):
    n_core, n_y, n_ep, n_seq = sizes["core"], sizes["y"], sizes["ep"], sizes["seq"]
    rows, span, width = enc_input.shape
    tokens = rows * span
    per = expert_weights.shape[1]
    units = ffn_in.shape[2]
    core = lax.axis_index("core").astype(jnp.int32).reshape(1)
    Order.start()

    flat = lambda a: a.reshape(tokens, a.shape[-1])
    enc_x, dec_x = flat(enc_input), flat(dec_input)
    enc_up, dec_up = flat(enc_out_grad), flat(dec_out_grad)
    kv_w = [Layer(kv_weights, i) for i in range(3)]
    router_t = router_weights.transpose(0, 2, 1)
    routers = [Layer(router_t, i) for i in range(3)]

    n_one, kv_one, w_send = norm_kv(enc_x, enc_gains, enc_biases, kv_weights, 0, 0, expert_weights, [0])
    w_enc = [Layer(expert_weights, 0)] + every_block(w_send, "ep", n_ep)[1:]
    kvs_one = every_block(kv_one, "seq", n_seq)
    n_three, kv_three, *w_sends = norm_kv(dec_x, dec_gains, dec_biases, kv_weights, 0, 1, expert_weights, [1, 2])
    meta, q_rows = prepare(routes.transpose(0, 1, 3, 2), enc_segments, dec_segments, n_ep, n_seq, per)
    q_one, aux_one = queries(n_one, w_enc, routers[0], meta, 0)
    w_got = every_block(after(w_sends[0], q_one), "ep", n_ep)
    w_dec = [Layer(expert_weights, 1)] + w_got[1:]
    w_cross = [Layer(expert_weights, 2)] + every_block(after(w_sends[1], *w_got[1:]), "ep", n_ep)[1:]
    o_one, lse_one, enc_mid = attend(
        enc_x, q_one, aux_one, kvs_one, w_enc, meta, q_rows, 0, 0, 0, False
    )
    kvs_three = every_block(after(kv_three, q_one, *kvs_one[1:]), "seq", n_seq)
    n_two, z_two, slope_two, memory, kv_mem = ffn_forward(
        enc_mid, enc_gains, enc_biases, 1, ffn_in, ffn_in_bias, ffn_out, ffn_out_bias, 0, kv_weights[2], 4
    )
    kvs_mem = every_block(kv_mem, "seq", n_seq)
    q_three, aux_three = queries(n_three, w_dec, routers[1], meta, 1)
    o_three, lse_three, dec_mid = attend(
        dec_x, q_three, aux_three, kvs_three, w_dec, meta, q_rows, 1, 1, 1, True
    )
    n_four, q_four, aux_four = norm_queries(dec_mid, dec_gains, dec_biases, 1, w_cross, routers[2], meta, 2)
    o_four, lse_four, dec_late = attend(
        dec_mid, q_four, aux_four, kvs_mem, w_cross, meta, q_rows, 2, 1, 0, False
    )

    other_core = lambda a: swap(a, "core", n_core, 1)
    two = lambda a: a.reshape(2, a.shape[0] // 2, a.shape[1])

    near, far = (("seq", 0), 2), (("seq", 1), n_seq // 2)

    def near_swap(blocks):
        return [blocks[0], swap(blocks[1], "seq", n_seq, 1)]

    def far_swap(blocks):
        return [blocks[0]] + [swap(blocks[d], "seq", n_seq, 2 * d) for d in range(1, far[1])]

    def kv_far(keep, got, name):
        return far_swap(fold([([keep, got], None, far[1])], name=name)[0])

    def z_near(groups, name):
        return near_swap(fold([(addends, *near) for addends in groups], merge=True, name=name))

    def z_far(parts, name):
        return far_swap(fold([(parts, *far)], name=name)[0])

    def z_all(parts, name):
        ((done,),) = fold([(parts, None, 1)], name=name)
        return far_swap([done] * far[1])

    def z_back(parts, name):
        (done,) = unfold([(parts, *far)], name=name)
        return near_swap([done] * 2)

    def back_second(parts, name):
        share = parts[0].shape[0] // 2
        a, b = unfold([(parts, *near)], [share, share], name=name)
        return every_block(a, "y", n_y), every_block(b, "ep", n_ep)

    def first_parts(own, got, name):
        pairs = [[Layer(two(own), i), Layer(two(got), i)] for i in range(2)]
        a, b = fold([(pairs[0], "ep", n_ep), (pairs[1], "y", n_y)], name=name)
        return give_back(a, "ep", n_ep), give_back(b, "y", n_y)

    def second_parts(a, b, name):
        a, b = fold([(a, "y", n_y), (b, "ep", n_ep)], name=name)
        return give_back(a, "y", n_y), give_back(b, "ep", n_ep)

    def back_first(a, b, name):
        a, b = unfold([(a, "y", n_y), (b, "ep", n_ep)], name=name)
        return every_block(a, "ep", n_ep), every_block(b, "y", n_y)

    def back_core(a, b, name):
        parts = unfold([(a, "ep", n_ep), (b, "y", n_y)], name=name)
        return list(parts), [other_core(part) for part in parts]

    dec_out, grad_late, dec_send, dec_own, dbi_dec, small_dec = ffn_both(
        core, dec_late, dec_up, dec_gains, dec_biases, 2, ffn_in, ffn_in_bias, ffn_out, ffn_out_bias, 1
    )
    half = (dec_own.shape[0] * 2 * width, dec_own.shape[3])
    dec_got = other_core(dec_send.reshape(half))
    mem_keep, mem_near, dq_four, dlog_four = attend_back(
        grad_late, o_four, q_four, aux_four, lse_four, kvs_mem, w_cross, meta, q_rows, 2, 1, 0, False
    )
    mem_near = swap(mem_near, "seq", n_seq, 1)
    dec_a, dec_b = first_parts(dec_own.reshape(half), dec_got, "dec_first")
    cross_own, cross_send, dr_cross, grad_mid, small_cross = expert_back(
        grad_late, n_four, o_four, aux_four, dq_four, dlog_four, w_cross, routers[2], meta, 2,
        dec_mid, dec_gains, 1
    )
    cross_got = other_core(cross_send)
    dkv_mem = kv_far(mem_keep, mem_near, "mem_far")
    three_keep, three_near, dq_three, dlog_three = attend_back(
        grad_mid, o_three, q_three, aux_three, lse_three, kvs_three, w_dec, meta, q_rows, 1, 1, 1, True
    )
    three_near = swap(three_near, "seq", n_seq, 1)
    x_cross = give_back(fold([([cross_own, cross_got], None, n_ep)], True, name="x_cross"), "ep", n_ep)
    dec_a, dec_b = second_parts(dec_a, dec_b, "dec_second")
    grad_enc, dkw_cross, enc_send, enc_own, dbi_enc, small_enc = ffn_back(
        core, enc_up, dkv_mem, kv_w[2], memory, enc_mid, n_two, z_two, slope_two, enc_gains, 1,
        ffn_in, ffn_out, 0,
    )
    enc_got = other_core(enc_send.reshape(half))
    dkv_three = kv_far(three_keep, three_near, "three_far")
    dec_parts = z_near([dec_a, dec_b], "dec_near")
    one_keep, one_near, dq_one, dlog_one = attend_back(
        grad_enc, o_one, q_one, aux_one, lse_one, kvs_one, w_enc, meta, q_rows, 0, 0, 0, False
    )
    one_near = swap(one_near, "seq", n_seq, 1)
    enc_a, enc_b = first_parts(enc_own.reshape(half), enc_got, "enc_first")
    dec_parts = z_far(dec_parts, "dec_far")
    Order.share = LIGHT
    enc_own_x, enc_send_x, dr_enc, dn_one = expert_back(
        grad_enc, n_one, o_one, aux_one, dq_one, dlog_one, w_enc, routers[0], meta, 0
    )
    dec_own_x, dec_send_x, dr_dec, dn_three = expert_back(
        grad_mid, n_three, o_three, aux_three, dq_three, dlog_three, w_dec, routers[1], meta, 1
    )
    dkv_one = kv_far(one_keep, one_near, "one_far")
    dec_grad, dkw_dec, small_three = self_finish(
        grad_mid, dn_three, dkv_three, n_three, kv_w[1], dec_x, dec_gains, 0
    )
    enc_a, enc_b = second_parts(enc_a, enc_b, "enc_second")
    dec_got_x, enc_got_x = [other_core(after(part, enc_a[0])) for part in (dec_send_x, enc_send_x)]
    enc_grad, dkw_enc, small_one = self_finish(
        grad_enc, dn_one, dkv_one, n_one, kv_w[0], enc_x, enc_gains, 0
    )
    small_own, small_send = pack_small(
        [dkw_enc, dkw_dec, dkw_cross], [dr_enc, dr_dec, dr_cross],
        [small_one, small_enc, small_three, small_cross, small_dec], [dbi_enc, dbi_dec],
    )
    Order.share = 1.0
    small_got = other_core(small_send)
    x_dec = give_back(fold([([dec_own_x, dec_got_x], None, n_ep)], True, name="x_dec"), "ep", n_ep)
    dec_parts = z_all(dec_parts, "dec_all")
    enc_parts = z_near([enc_a, enc_b], "enc_near")
    n_x = enc_own_x.shape[0] // n_ep
    n_small = small_own.shape[0]
    halves = [([Rows(enc_own_x, n_x, d), Rows(enc_got_x, n_x, d)], "y", n_y) for d in range(n_ep)]
    x_two = give_back(fold(halves + [([small_own, small_got], "y", n_y)], True, name="x_two_y"), "y", n_y)
    enc_parts = z_far(enc_parts, "enc_far")
    x_one = give_back(fold([(x_cross, "y", n_y), (x_dec, "y", n_y)], True, name="x_one_y"), "y", n_y)
    dec_parts = z_back(dec_parts, "dec_back_far")
    n_x, n_small = n_x // n_y, n_small // n_y
    enc_rows = [Rows(part, n_ep * n_x, 0) for part in x_two]
    small_rows = [Rows(part, n_small, n_ep * n_x // n_small) for part in x_two]
    x_two = fold([(enc_rows, None, n_ep), (small_rows, "ep", n_ep)], True, name="x_two_x")
    x_two = give_back(x_two, "ep", n_ep)
    enc_parts = z_all(enc_parts, "enc_all")
    dec_a, dec_b = back_second(dec_parts, "dec_back_near")
    n_small = n_small // n_ep
    enc_rows = [Rows(part, n_x, 0) for part in x_two]
    small_rows = [Rows(part, n_small, n_x // n_small) for part in x_two]
    x_parts = z_near([x_one, enc_rows, small_rows], "x_near")
    enc_parts = z_back(enc_parts, "enc_back_far")
    dec_a, dec_b = back_first(dec_a, dec_b, "dec_back_second")
    x_parts = z_far(x_parts, "x_far")
    enc_a, enc_b = back_second(enc_parts, "enc_back_near")
    x_parts = z_all(x_parts, "x_all")
    enc_a, enc_b = back_first(enc_a, enc_b, "enc_back_second")
    x_parts = z_back(x_parts, "x_back_far")
    dec_ab, dec_other = back_core(dec_a, dec_b, "dec_back_first")
    x_part, small_part = unfold([(x_parts, *near)], [n_x, n_x // 2, n_small // 2], [2, 1], name="x_back_near")
    x_parts, small_parts = every_block(x_part, "y", n_y), every_block(small_part, "ep", n_ep)
    enc_ab, enc_other = back_core(enc_a, enc_b, "enc_back_first")
    pieces = lambda parts: [part.reshape((-1, 2, width) + dec_own.shape[3:]) for part in parts]
    grad_in, grad_out = place_first(core, pieces(dec_ab), pieces(dec_other), units)
    (small_part,) = unfold([(small_parts, "ep", n_ep)], name="small_back_x")
    small_parts = every_block(small_part, "y", n_y)
    grad_in, grad_out = place_second(core, pieces(enc_ab), pieces(enc_other), grad_in, grad_out)
    (x_half,) = unfold([(x_parts, "y", n_y)], [n_x] * 3, [3], name="x_back_y")
    x_other = other_core(x_half)
    (small_half,) = unfold([(small_parts, "y", n_y)], name="small_back_y")
    small_parts = every_block(small_half, "core", n_core)
    experts = place_experts([(x_half, x_other, (2, 1, 0))], per, width)
    picks = [[0, 2], [1, 3], [5, 7, 9], [6, 8, 10], [4, 11]]
    kv_grad, router_grad, enc_gain, enc_bias, dec_gain, dec_bias, out_bias, in_bias = unpack_small(
        small_parts, (3, 3, picks, 2), width, units
    )
    shape = enc_input.shape
    return (
        memory.reshape(shape), dec_out.reshape(shape), enc_grad.reshape(shape), dec_grad.reshape(shape),
        enc_gain, enc_bias, dec_gain, dec_bias, kv_grad, router_grad.transpose(0, 2, 1), experts,
        grad_in, in_bias, grad_out, out_bias,
    )


def solution(mesh):
    sizes = dict(mesh.shape)
    n_dp, n_ep, n_seq = sizes["dp"], sizes["ep"], sizes["seq"]
    split = jax.sharding.Mesh(mesh.devices.reshape(n_dp // 2, 2, n_ep, n_seq), ("y", "core", "ep", "seq"))
    batch = ("y", "core", "ep")
    tokens = P(batch, "seq", None)
    rows = P(batch, None)
    experts = P(None, "ep", None, None)
    return jax.shard_map(
        partial(shards, dict(split.shape)),
        mesh=split,
        in_specs=(
            tokens, tokens, rows, rows, P(None, batch, "seq", None), tokens, tokens,
            P(), P(), P(), P(), P(), P(), experts, P(), P(), P(), P(),
        ),
        out_specs=(
            tokens, tokens, tokens, tokens, P(), P(), P(), P(), P(), P(), experts, P(), P(), P(), P(),
        ),
        check_vma=False,
    )
```

```python
from functools import partial

import jax
import jax.numpy as jnp
from jax import lax
from jax.experimental import pallas as pl
from jax.experimental.pallas import tpu as pltpu
from jax.sharding import PartitionSpec as P

EXPERTS = 8
HD = 64
TOP = 2
PAIR = 2 * HD

EPS = 1e-05
SCALE = 0.125
NEG = -1e30
F32 = jnp.float32
BF16 = jnp.bfloat16
SQRT_HALF = 0.7071067811865476
INV_SQRT_2PI = 0.3989422804014327
VMEM_LIMIT = 20 * 1024 * 1024

CORE, Y, EP, SEQ = "core", "y", "ep", "seq"

ROUTE = 0
LOCAL_ROUTE = 6
KEY_SEG = 12


def mm(left, right):
    return lax.dot_general(left, right, (((1,), (0,)), ((), ())), preferred_element_type=F32)


def mm_nt(left, right):
    return lax.dot_general(left, right, (((1,), (1,)), ((), ())), preferred_element_type=F32)


def mm_tn(left, right):
    return lax.dot_general(left, right, (((0,), (0,)), ((), ())), preferred_element_type=F32)


def iota(shape, dim):
    return lax.broadcasted_iota(jnp.int32, shape, dim)


def standardize(hidden):
    centred = hidden - jnp.mean(hidden, -1, keepdims=True)
    inverse = lax.rsqrt(jnp.mean(centred * centred, -1, keepdims=True) + EPS)
    return centred * inverse, inverse


def norm(hidden, gain, bias):
    return standardize(hidden)[0] * gain + bias


def norm_back(hidden, gain, upstream):
    unit, inverse = standardize(hidden)
    grad_gain = jnp.sum(upstream * unit, 0, keepdims=True)
    grad_bias = jnp.sum(upstream, 0, keepdims=True)
    scaled = upstream * gain
    centred = scaled - jnp.mean(scaled, -1, keepdims=True)
    projected = jnp.mean(scaled * unit, -1, keepdims=True)
    return inverse * (centred - unit * projected), grad_gain, grad_bias


def widened(router):
    full = router.astype(F32)
    return jnp.concatenate([full, jnp.zeros((PAIR - full.shape[0], full.shape[1]), F32)], 0).astype(BF16)


def row_of(ref, index):
    return ref[...].astype(F32)[index : index + 1]


class Order:
    last = None
    share = 1.0

    @classmethod
    def start(cls):
        cls.last = None
        cls.share = 1.0

    @classmethod
    def run(cls, kernel, args):
        args = [operand(arg) for arg in args]
        if cls.last is not None:
            args[0], _ = lax.optimization_barrier((args[0], cls.last))
        outs = kernel(*args)
        cls.last = outs[0]
        return outs


class Layer:
    def __init__(self, array, index):
        self.array, self.index = array, index
        self.shape = array.shape[1:]

    def spec(self):
        index, rest = self.index, len(self.shape)
        return pl.BlockSpec((None,) + self.shape, lambda *_: (index,) + (0,) * rest)


class Rows:
    def __init__(self, array, rows, index):
        self.array, self.index = array, index
        self.shape = (rows, array.shape[1])

    def spec(self):
        index = self.index
        return pl.BlockSpec(self.shape, lambda *_: (index, 0))


def operand(arg):
    return arg.array if isinstance(arg, (Layer, Rows)) else arg


def whole(arg):
    if isinstance(arg, (Layer, Rows)):
        return arg.spec()
    rest = len(arg.shape)
    return pl.BlockSpec(arg.shape, lambda *_: (0,) * rest)


TIMES = {
    "norm_kv": 0.7, "prepare": 0.3, "queries": 2.0, "norm_queries": 2.3, "attend": 3.4, "ffn_forward": 6.2,
    "ffn_both": 12.0, "attend_back": 5.0, "expert_back": 3.4, "ffn_back": 8.5, "self_finish": 2.0,
    "place_first": 3.5, "place_second": 3.5, "unpack_small": 1.0,
}
PACE = 1.0
LATER = 4.0
FOLD = 0.4
LIGHT = 0.05
ROOMY = 60 * 1024 * 1024


def cost(name):
    first = ("norm_kv", "prepare", "queries", "norm_queries", "attend", "ffn_forward", "ffn_both")
    micros = TIMES.get(name, FOLD) * (PACE if name in first else LATER)
    micros *= Order.share
    return pl.CostEstimate(flops=int(micros * 1e9), bytes_accessed=int(micros * 3e6), transcendentals=0)


def call(body, outs, args, scratch=(), limit=14 * 1024 * 1024, name=None):
    shapes = [jax.ShapeDtypeStruct(s, d) for s, d in outs]
    kernel = pl.pallas_call(
        body,
        grid=(1,),
        out_shape=tuple(shapes),
        in_specs=[whole(arg) for arg in args],
        out_specs=tuple(whole(out) for out in shapes),
        scratch_shapes=list(scratch),
        cost_estimate=cost(name),
        compiler_params=pltpu.CompilerParams(vmem_limit_bytes=limit),
        name=name,
    )
    return Order.run(kernel, args)


def prepare(routes, enc_seg, dec_seg, n_ep, n_seq, per):
    subs, rows, _, span = routes.shape
    tokens = rows * span
    used = 2 * subs * TOP + 2 * n_seq

    def body(r_ref, e_ref, d_ref, meta_ref, rows_ref):
        base = lax.axis_index(EP) * per
        me = lax.axis_index(SEQ)
        lines = []
        for flip in (False, True):
            for sub in range(subs):
                for j in range(TOP):
                    line = jnp.concatenate([r_ref[sub, r, j : j + 1, :] for r in range(rows)], 1)
                    lines.append(line ^ base if flip else line)
        queries = []
        for ref in (e_ref, d_ref):
            for d in range(n_seq):
                at = pl.multiple_of((me ^ d) * span, span)
                block = ref[:, pl.ds(at, span)]
                lines.append(jnp.concatenate([block[r : r + 1] for r in range(rows)], 1))
                if d == 0:
                    queries.append(jnp.concatenate([block] * TOP, 1))
        rows_ref[...] = jnp.concatenate(queries, 0)
        lines = [line.astype(F32) for line in lines]
        lines.append(jnp.zeros((PAIR - used, tokens), F32))
        meta_ref[...] = jnp.concatenate(lines, 0).T.astype(jnp.int32)

    return call(
        body,
        [((tokens, PAIR), jnp.int32), ((2 * rows, TOP * span), jnp.int32)],
        (routes, enc_seg, dec_seg),
        name="prepare",
    )


def norm_kv(hidden, gains, biases, kv_weights, layer, index, expert_weights, copied):
    tokens, width = hidden.shape
    stack = gains.shape[0]

    def body(h_ref, g_ref, b_ref, w_ref, e_ref, n_ref, kv_ref, *rest):
        e_outs = rest[: len(copied)]
        h_in, g_in, b_in, w_in, sems = rest[len(copied) :]
        pairs = [(h_ref, h_in), (g_ref, g_in), (b_ref, b_in), (w_ref.at[index], w_in)]
        pairs += [(e_ref.at[k], out) for k, out in zip(copied, e_outs)]
        moves = [pltpu.make_async_copy(*pair, sems.at[i]) for i, pair in enumerate(pairs)]
        for move in moves:
            move.start()
        for move in moves[:3]:
            move.wait()
        normed = norm(h_in[...].astype(F32), row_of(g_in, layer), row_of(b_in, layer)).astype(BF16)
        n_ref[...] = normed
        moves[3].wait()
        kv_ref[...] = mm(normed, w_in[...]).astype(BF16)
        for move in moves[4:]:
            move.wait()

    held = pl.BlockSpec(memory_space=pltpu.HBM)
    outs = [((tokens, width), BF16), ((tokens, PAIR), BF16)] + [(expert_weights.shape[1:], BF16)] * len(copied)
    shapes = [jax.ShapeDtypeStruct(*out) for out in outs]
    kernel = pl.pallas_call(
        body,
        out_shape=tuple(shapes),
        in_specs=[held] * 5,
        out_specs=tuple(pl.BlockSpec(memory_space=pltpu.VMEM) for _ in shapes),
        scratch_shapes=[
            pltpu.VMEM((tokens, width), BF16), pltpu.VMEM((stack, width), BF16), pltpu.VMEM((stack, width), BF16),
            pltpu.VMEM(kv_weights.shape[1:], BF16), pltpu.SemaphoreType.DMA((4 + len(copied),)),
        ],
        cost_estimate=cost("norm_kv"),
        compiler_params=pltpu.CompilerParams(vmem_limit_bytes=ROOMY),
        name="norm_kv",
    )
    return Order.run(kernel, [hidden, gains, biases, kv_weights, expert_weights])


def query_part(normed, weights, router, meta_ref, sub, q_ref, aux_ref):
    tokens = normed.shape[0]
    per = weights[0].shape[0]
    lane = iota((tokens, PAIR), 1)
    local = [meta_ref[:, LOCAL_ROUTE + TOP * sub + j : LOCAL_ROUTE + TOP * sub + j + 1] for j in range(TOP)]
    route = [meta_ref[:, ROUTE + TOP * sub + j : ROUTE + TOP * sub + j + 1] for j in range(TOP)]
    picked = [jnp.zeros((tokens, PAIR), F32) for _ in range(TOP)]
    for expert in range(EXPERTS):
        every = mm(normed, weights[expert // per][expert % per])
        picked = [jnp.where(local[j] == expert, every, picked[j]) for j in range(TOP)]
    for j in range(TOP):
        rounded = picked[j].astype(BF16).astype(F32) * SCALE
        q_ref[j] = jnp.where(lane < HD, rounded, 0.0).astype(BF16)
    logits = mm_nt(normed, widened(router))
    hit = [lane == route[j] for j in range(TOP)]
    chosen = [jnp.sum(jnp.where(hit[j], logits, 0.0), -1, keepdims=True) for j in range(TOP)]
    top = jnp.maximum(chosen[0], chosen[1])
    raised = [jnp.exp(value - top) for value in chosen]
    total = raised[0] + raised[1]
    count = jnp.where(hit[0] | hit[1], 1.0, 0.0).astype(BF16)
    before = (iota((tokens, tokens), 0) > iota((tokens, tokens), 1)).astype(F32).astype(BF16)
    ranks = mm(before, count)
    capacity = tokens * TOP // EXPERTS
    aux = jnp.zeros((tokens, PAIR), F32)
    for j in range(TOP):
        rank = jnp.sum(jnp.where(hit[j], ranks, 0.0), -1, keepdims=True)
        kept = jnp.where(rank < capacity, 1.0, 0.0)
        aux = jnp.where(lane == j, raised[j] / total, aux)
        aux = jnp.where(lane == TOP + j, kept, aux)
    aux_ref[...] = aux


def queries(normed, weights, router, meta, sub):
    tokens, width = normed.shape
    count = len(weights)

    def body(*refs):
        n_ref, w_refs = refs[0], refs[1 : 1 + count]
        r_ref, meta_ref, q_ref, aux_ref = refs[1 + count :]
        query_part(n_ref[...], w_refs, r_ref[...], meta_ref, sub, q_ref, aux_ref)

    return call(
        body,
        [((TOP, tokens, PAIR), BF16), ((tokens, PAIR), F32)],
        (normed, *weights, router, meta),
        name="queries",
    )


def norm_queries(hidden, gains, biases, layer, weights, router, meta, sub):
    tokens, width = hidden.shape
    count = len(weights)

    def body(*refs):
        h_ref, g_ref, b_ref, w_refs = refs[0], refs[1], refs[2], refs[3 : 3 + count]
        r_ref, meta_ref, n_ref, q_ref, aux_ref = refs[3 + count :]
        normed = norm(h_ref[...], row_of(g_ref, layer), row_of(b_ref, layer)).astype(BF16)
        n_ref[...] = normed
        query_part(normed, w_refs, r_ref[...], meta_ref, sub, q_ref, aux_ref)

    return call(
        body,
        [((tokens, width), BF16), ((TOP, tokens, PAIR), BF16), ((tokens, PAIR), F32)],
        (hidden, gains, biases, *weights, router, meta),
        name="norm_queries",
    )


def allowed_block(meta_ref, q_row, place, rows, column, causal):
    allowed = meta_ref[rows, column : column + 1] == q_row
    if causal:
        span, wide = rows.stop - rows.start, q_row.shape[1]
        me = lax.axis_index(SEQ)
        key = iota((span, wide), 0) + ((me ^ place) - me) * span
        query = lax.rem(iota((1, wide), 1), span)
        allowed = allowed & (query >= key)
    return allowed


def mixed_slots(mixed, aux, meta_ref, sub):
    scaled = [mixed[j] * (aux[:, j : j + 1] * aux[:, TOP + j : TOP + j + 1]) for j in range(TOP)]
    local = [meta_ref[:, LOCAL_ROUTE + TOP * sub + j : LOCAL_ROUTE + TOP * sub + j + 1] for j in range(TOP)]

    def of(expert):
        part = jnp.where(local[1] == expert, scaled[1], 0.0)
        return jnp.where(local[0] == expert, scaled[0], part).astype(BF16)

    return of


def attend(hidden, query, aux, key_values, weights, meta, q_rows, sub, q_base, k_base, causal):
    tokens, width = hidden.shape
    rows = q_rows.shape[0] // 2
    span = tokens // rows
    wide = TOP * span
    blocks, owners = len(key_values), len(weights)
    per = weights[0].shape[0]

    def body(*refs):
        h_ref, q_ref, aux_ref = refs[:3]
        kv_refs = refs[3 : 3 + blocks]
        w_refs = refs[3 + blocks : 3 + blocks + owners]
        meta_ref, qr_ref, o_ref, lse_ref, out_ref, s_ref = refs[3 + blocks + owners :]
        lane = iota((wide, PAIR), 1)
        for r in range(rows):
            here = slice(r * span, (r + 1) * span)
            q_row = qr_ref[q_base * rows + r : q_base * rows + r + 1, :]
            q_all = jnp.concatenate([q_ref[j, here] for j in range(TOP)], 0)
            top = jnp.full((1, wide), NEG, F32)
            for d in range(blocks):
                scores = mm_nt(kv_refs[d][here], q_all)
                allowed = allowed_block(
                    meta_ref, q_row, d, here, KEY_SEG + k_base * blocks + d, causal
                )
                scores = jnp.where(allowed, scores, NEG)
                s_ref[d * span : (d + 1) * span] = scores
                top = jnp.maximum(top, jnp.max(scores, 0, keepdims=True))
            total = jnp.zeros((1, wide), F32)
            mixed = jnp.zeros((PAIR, wide), F32)
            for d in range(blocks):
                probs = jnp.exp(s_ref[d * span : (d + 1) * span] - top)
                total = total + jnp.sum(probs, 0, keepdims=True)
                mixed = mixed + mm_tn(kv_refs[d][here], probs.astype(BF16))
            lse_ref[r : r + 1] = top + jnp.log(total)
            mixed = jnp.where(lane < HD, 0.0, (mixed / total).T).astype(BF16)
            for j in range(TOP):
                o_ref[j, here] = mixed[j * span : (j + 1) * span]
        slot = mixed_slots([o_ref[j].astype(F32) for j in range(TOP)], aux_ref[...], meta_ref, sub)
        result = h_ref[...].astype(F32)
        for expert in range(0, EXPERTS, 2):
            part = jnp.concatenate([slot(expert), slot(expert + 1)], 1)
            weight = jnp.concatenate([w_refs[e // per][e % per] for e in (expert, expert + 1)], 1)
            result = result + mm_nt(part, weight)
        out_ref[...] = result

    args = (hidden, query, aux, *key_values, *weights, meta, q_rows)
    return call(
        body,
        [((TOP, tokens, PAIR), BF16), ((rows, wide), F32), ((tokens, width), F32)],
        args,
        scratch=[pltpu.VMEM((blocks * span, wide), F32)],
        name="attend",
    )


def attend_back(upstream, mixed, query, aux, lse, key_values, weights, meta, q_rows, sub, q_base, k_base, causal):
    tokens, width = upstream.shape
    rows = q_rows.shape[0] // 2
    span = tokens // rows
    wide = TOP * span
    blocks, owners = len(key_values), len(weights)
    per = weights[0].shape[0]

    def body(*refs):
        up_ref, o_ref, q_ref, aux_ref, lse_ref = refs[:5]
        kv_refs = refs[5 : 5 + blocks]
        w_refs = refs[5 + blocks : 5 + blocks + owners]
        meta_ref, qr_ref = refs[5 + blocks + owners : 7 + blocks + owners]
        keep_ref, near_ref, dq_ref, dlog_ref, do_ref = refs[7 + blocks + owners :]
        rounded = up_ref[...].astype(BF16)
        lane = iota((tokens, PAIR), 1)
        local = [meta_ref[:, LOCAL_ROUTE + TOP * sub + j : LOCAL_ROUTE + TOP * sub + j + 1] for j in range(TOP)]
        route = [meta_ref[:, ROUTE + TOP * sub + j : ROUTE + TOP * sub + j + 1] for j in range(TOP)]
        picked = [jnp.zeros((tokens, PAIR), F32) for _ in range(TOP)]
        for expert in range(EXPERTS):
            every = mm(rounded, w_refs[expert // per][expert % per])
            picked = [jnp.where(local[j] == expert, every, picked[j]) for j in range(TOP)]
        aux = aux_ref[...]
        gate = [aux[:, j : j + 1] for j in range(TOP)]
        kept = [aux[:, TOP + j : TOP + j + 1] for j in range(TOP)]
        grad_gate = [
            kept[j] * jnp.sum(picked[j] * o_ref[j].astype(F32), -1, keepdims=True) for j in range(TOP)
        ]
        inner = gate[0] * grad_gate[0] + gate[1] * grad_gate[1]
        dlog = jnp.zeros((tokens, PAIR), F32)
        for j in range(TOP):
            dlog = jnp.where(lane == route[j], gate[j] * (grad_gate[j] - inner), dlog)
            do_ref[j] = jnp.where(lane < HD, 0.0, picked[j] * (gate[j] * kept[j])).astype(BF16)
        dlog_ref[...] = dlog.astype(BF16)
        lane = iota((wide, PAIR), 1)
        for r in range(rows):
            here = slice(r * span, (r + 1) * span)
            q_row = qr_ref[q_base * rows + r : q_base * rows + r + 1, :]
            q_all = jnp.concatenate([q_ref[j, here] for j in range(TOP)], 0)
            do_all = jnp.concatenate([do_ref[j, here] for j in range(TOP)], 0)
            log_total = lse_ref[r : r + 1]
            inner = jnp.zeros((1, wide), F32)
            probs, grads = [], []
            for d in range(blocks):
                scores = mm_nt(kv_refs[d][here], q_all)
                allowed = allowed_block(
                    meta_ref, q_row, d, here, KEY_SEG + k_base * blocks + d, causal
                )
                prob = jnp.exp(jnp.where(allowed, scores, NEG) - log_total)
                grad = mm_nt(kv_refs[d][here], do_all)
                inner = inner + jnp.sum(prob * grad, 0, keepdims=True)
                probs.append(prob)
                grads.append(grad)
            grad_query = jnp.zeros((PAIR, wide), F32)
            for d in range(blocks):
                grad_score = (probs[d] * (grads[d] - inner)).astype(BF16)
                grad_query = grad_query + mm_tn(kv_refs[d][here], grad_score)
                grad_kv = mm(probs[d].astype(BF16), do_all) + mm(grad_score, q_all)
                place = slice(d // 2 * tokens + r * span, d // 2 * tokens + (r + 1) * span)
                (near_ref if d % 2 else keep_ref)[place] = grad_kv.astype(BF16)
            grad_query = jnp.where(lane < HD, grad_query.T * SCALE, 0.0).astype(BF16)
            for j in range(TOP):
                dq_ref[j, here] = grad_query[j * span : (j + 1) * span]

    args = (upstream, mixed, query, aux, lse, *key_values, *weights, meta, q_rows)
    return call(
        body,
        [((blocks // 2 * tokens, PAIR), BF16)] * 2 + [((TOP, tokens, PAIR), BF16), ((tokens, PAIR), BF16)],
        args,
        scratch=[pltpu.VMEM((TOP, tokens, PAIR), BF16)],
        name="attend_back",
    )


def expert_back(upstream, normed, mixed, aux, dq, dlog, weights, router, meta, sub, hidden=None, gains=None, layer=0):
    tokens, width = upstream.shape
    owners = len(weights)
    per = weights[0].shape[0]
    finish = hidden is not None

    def body(*refs):
        up_ref, n_ref, o_ref, aux_ref, dq_ref, dlog_ref = refs[:6]
        w_refs = refs[6 : 6 + owners]
        r_ref, meta_ref = refs[6 + owners : 8 + owners]
        at = 8 + owners
        if finish:
            h_ref, g_ref = refs[at : at + 2]
            at += 2
        own_ref, send_ref, dr_ref, dn_ref = refs[at : at + 4]
        low_core = lax.axis_index(CORE) == 0
        half = width // 2
        slot = mixed_slots([o_ref[j].astype(F32) for j in range(TOP)], aux_ref[...], meta_ref, sub)
        local = [meta_ref[:, LOCAL_ROUTE + TOP * sub + j : LOCAL_ROUTE + TOP * sub + j + 1] for j in range(TOP)]
        grads = [dq_ref[j].astype(F32) * aux_ref[:, TOP + j : TOP + j + 1] for j in range(TOP)]

        def query_slot(expert):
            part = jnp.where(local[1] == expert, grads[1], 0.0)
            return jnp.where(local[0] == expert, grads[0], part).astype(BF16)

        normed_t = n_ref[...].T
        up_t = up_ref[...].astype(BF16).T
        total = mm(dlog_ref[...], widened(r_ref[...]))
        for expert in range(0, EXPERTS, 2):
            both = (expert, expert + 1)
            part = jnp.concatenate([query_slot(e) for e in both], 1)
            weight = jnp.concatenate([w_refs[e // per][e % per] for e in both], 1)
            total = total + mm_nt(part, weight)
            result = jnp.concatenate([slot(e) for e in both], 1)
            grad = (mm(normed_t, part) + mm(up_t, result)).astype(BF16)
            for k, e in enumerate(both):
                low, high = [grad[at : at + half, k * PAIR : (k + 1) * PAIR] for at in (0, half)]
                place = slice(e * half, (e + 1) * half)
                own_ref[place] = jnp.where(low_core, low, high)
                send_ref[place] = jnp.where(low_core, high, low)
        dr_ref[...] = mm_tn(dlog_ref[...], n_ref[...])[:EXPERTS]
        if finish:
            back, grad_gain, grad_bias = norm_back(h_ref[...].astype(F32), row_of(g_ref, layer), total)
            dn_ref[...] = up_ref[...] + back
            refs[at + 4][...] = jnp.concatenate([grad_gain, grad_bias], 0)
        else:
            dn_ref[...] = total

    outs = [((EXPERTS * width // 2, PAIR), BF16)] * 2 + [((EXPERTS, width), F32), ((tokens, width), F32)]
    args = (upstream, normed, mixed, aux, dq, dlog, *weights, router, meta)
    if finish:
        outs = outs + [((2, width), F32)]
        args = args + (hidden, gains)
    return call(body, outs, args, name="expert_back")


def added(refs):
    total = refs[0][...].astype(F32)
    for ref in refs[1:]:
        total = total + ref[...].astype(F32)
    return total.astype(BF16)


def self_finish(upstream, grad_normed, grad_kvs, normed, kv_weight, hidden, gains, layer):
    tokens, width = upstream.shape

    def body(up_ref, dn_ref, *refs):
        n_ref, w_ref, h_ref, g_ref, out_ref, dw_ref, small_ref = refs[len(grad_kvs) :]
        grad_kv = added(refs[: len(grad_kvs)])
        total = dn_ref[...] + mm_nt(grad_kv, w_ref[...])
        dw_ref[...] = mm_tn(n_ref[...], grad_kv)
        back, grad_gain, grad_bias = norm_back(h_ref[...].astype(F32), row_of(g_ref, layer), total)
        out_ref[...] = up_ref[...] + back
        small_ref[...] = jnp.concatenate([grad_gain, grad_bias], 0)

    return call(
        body,
        [((tokens, width), F32), ((width, PAIR), F32), ((2, width), F32)],
        (upstream, grad_normed, *grad_kvs, normed, kv_weight, hidden, gains),
        name="self_finish",
    )


def gelu_parts(inner):
    cdf = 0.5 * (1.0 + lax.erf(inner * SQRT_HALF))
    density = jnp.exp(-0.5 * inner * inner) * INV_SQRT_2PI
    return inner * cdf, cdf + inner * density


def ffn_call(body, tokens, width, hidden, tiles, ins, outs, scratch, name):
    tile = hidden // tiles
    kinds = {
        "full2": lambda s: pl.BlockSpec(s, lambda k: (0, 0)),
        "win": lambda s: pl.BlockSpec((1, width, tile), lambda k: (s, 0, k)),
        "bin": lambda s: pl.BlockSpec((2, tile), lambda k: (0, k)),
        "wout": lambda s: pl.BlockSpec((1, tile, width), lambda k: (s, k, 0)),
        "act": lambda s: pl.BlockSpec((tokens, tile), lambda k: (0, k)),
    }
    kernel = pl.pallas_call(
        body,
        grid=(tiles,),
        in_specs=[kinds[kind](s) for kind, s, _ in ins],
        out_specs=tuple(kinds[kind](shape) for kind, shape, _ in outs),
        out_shape=tuple(jax.ShapeDtypeStruct(shape, dtype) for _, shape, dtype in outs),
        scratch_shapes=scratch,
        cost_estimate=cost(name),
        compiler_params=pltpu.CompilerParams(vmem_limit_bytes=VMEM_LIMIT),
        name=name,
    )
    return Order.run(kernel, [a for _, _, a in ins])


def ffn_forward(hidden, gains, biases, norm_layer, w_in, b_in, w_out, b_out, layer, kv_weight, tiles):
    tokens, width = hidden.shape
    units = w_in.shape[2]

    def body(h_ref, g_ref, b_ref, wi_ref, bi_ref, wo_ref, bo_ref, kw_ref,
             n_out, z_ref, s_ref, mem_ref, kv_ref, n_ref, acc_ref):
        step = pl.program_id(0)

        @pl.when(step == 0)
        def _():
            normed = norm(h_ref[...], row_of(g_ref, norm_layer), row_of(b_ref, norm_layer)).astype(BF16)
            n_ref[...] = normed
            n_out[...] = normed
            acc_ref[...] = h_ref[...] + row_of(bo_ref, layer)

        inner = mm(n_ref[...], wi_ref[0]) + row_of(bi_ref, layer)
        active, slope = gelu_parts(inner)
        active = active.astype(BF16)
        z_ref[...] = active
        s_ref[...] = slope.astype(BF16)
        acc_ref[...] += mm(active, wo_ref[0])

        @pl.when(step == tiles - 1)
        def _():
            memory = acc_ref[...].astype(BF16)
            mem_ref[...] = memory
            kv_ref[...] = mm(memory, kw_ref[...]).astype(BF16)

    ins = [
        ("full2", hidden.shape, hidden), ("full2", gains.shape, gains), ("full2", biases.shape, biases),
        ("win", layer, w_in), ("bin", None, b_in), ("wout", layer, w_out), ("full2", b_out.shape, b_out),
        ("full2", kv_weight.shape, kv_weight),
    ]
    outs = [
        ("full2", (tokens, width), BF16), ("act", (tokens, units), BF16), ("act", (tokens, units), BF16),
        ("full2", (tokens, width), BF16), ("full2", (tokens, PAIR), BF16),
    ]
    scratch = [pltpu.VMEM((tokens, width), BF16), pltpu.VMEM((tokens, width), F32)]
    return ffn_call(body, tokens, width, units, tiles, ins, outs, scratch, "ffn_forward")


def grad_call(body, core, ins, outs, scratch, tiles, name):
    half = tiles // 2

    def unit(k, core_ref):
        far = jnp.where(k < half, 1 - core_ref[0], core_ref[0])
        return far * half + lax.rem(k, half)

    def spec(kind, shape):
        if kind == "w_in":
            layer, (width, tile) = shape
            return pl.BlockSpec((None, width, tile), lambda k, c: (layer, 0, unit(k, c)))
        if kind == "w_out":
            layer, (tile, width) = shape
            return pl.BlockSpec((None, tile, width), lambda k, c: (layer, unit(k, c), 0))
        if kind == "units":
            rows, tile = shape
            return pl.BlockSpec((rows, tile), lambda k, c: (0, unit(k, c)))
        if kind == "send":
            return pl.BlockSpec((1,) + shape[1:], lambda k, c: (jnp.minimum(k, half - 1), 0, 0, 0))
        if kind == "own":
            return pl.BlockSpec((1,) + shape[1:], lambda k, c: (jnp.maximum(k - half, 0), 0, 0, 0))
        rest = len(shape)
        return pl.BlockSpec(shape, lambda k, c: (0,) * rest)

    in_specs = [whole(a) if kind == "full" else spec(kind, shape) for kind, shape, a in ins]
    kernel = pl.pallas_call(
        body,
        grid_spec=pltpu.PrefetchScalarGridSpec(
            num_scalar_prefetch=1,
            grid=(tiles,),
            in_specs=in_specs,
            out_specs=tuple(spec(kind, shape) for kind, shape, _, _ in outs),
            scratch_shapes=scratch,
        ),
        out_shape=tuple(jax.ShapeDtypeStruct(full, dtype) for _, _, full, dtype in outs),
        cost_estimate=cost(name),
        compiler_params=pltpu.CompilerParams(vmem_limit_bytes=VMEM_LIMIT),
        name=name,
    )
    return Order.run(kernel, [core] + [a for _, _, a in ins])


def store_grads(step, half, send_ref, own_ref, grad_in, grad_out):
    @pl.when(step < half)
    def _():
        send_ref[0, 0] = grad_in
        send_ref[0, 1] = grad_out

    @pl.when(step >= half)
    def _():
        own_ref[0, 0] = grad_in
        own_ref[0, 1] = grad_out


def ffn_both(core, hidden, upstream, gains, biases, norm_layer, w_in, b_in, w_out, b_out, layer):
    tokens, width = hidden.shape
    units = w_in.shape[2]
    tile = width
    tiles = units // tile

    def body(_, h_ref, up_ref, g_ref, b_ref, wi_ref, bi_ref, wo_ref, bo_ref,
             out_ref, grad_ref, send_ref, own_ref, dbi_ref, small_ref, n_ref, nt_ref, acc_ref, dn_ref):
        step = pl.program_id(0)

        @pl.when(step == 0)
        def _():
            normed = norm(h_ref[...], row_of(g_ref, norm_layer), row_of(b_ref, norm_layer)).astype(BF16)
            n_ref[...] = normed
            nt_ref[...] = normed.T
            acc_ref[...] = h_ref[...] + row_of(bo_ref, layer)
            dn_ref[...] = jnp.zeros_like(dn_ref)

        inner = mm(n_ref[...], wi_ref[...]) + row_of(bi_ref, layer)
        active, slope = gelu_parts(inner)
        active = active.astype(BF16)
        acc_ref[...] += mm(active, wo_ref[...])
        up = up_ref[...]
        grad_out = mm_tn(active, up).astype(BF16)
        grad_inner = (slope * mm_nt(up, wo_ref[...])).astype(BF16)
        dbi_ref[...] = jnp.sum(grad_inner.astype(F32), 0, keepdims=True)
        store_grads(step, tiles // 2, send_ref, own_ref, mm(nt_ref[...], grad_inner).astype(BF16), grad_out)
        dn_ref[...] += mm_nt(grad_inner, wi_ref[...])

        @pl.when(step == tiles - 1)
        def _():
            out_ref[...] = acc_ref[...].astype(BF16)
            top = up_ref[...].astype(F32)
            back, grad_gain, grad_bias = norm_back(h_ref[...], row_of(g_ref, norm_layer), dn_ref[...])
            grad_ref[...] = top + back
            small_ref[...] = jnp.concatenate([grad_gain, grad_bias, jnp.sum(top, 0, keepdims=True)], 0)

    ins = [
        ("full", None, hidden), ("full", None, upstream), ("full", None, gains), ("full", None, biases),
        ("w_in", (layer, (width, tile)), w_in), ("units", (b_in.shape[0], tile), b_in),
        ("w_out", (layer, (tile, width)), w_out), ("full", None, b_out),
    ]
    half = (tiles // 2, 2, width, tile)
    outs = [
        ("all", (tokens, width), (tokens, width), BF16), ("all", (tokens, width), (tokens, width), F32),
        ("send", half, half, BF16), ("own", half, half, BF16),
        ("units", (1, tile), (1, units), F32), ("all", (3, width), (3, width), F32),
    ]
    scratch = [
        pltpu.VMEM((tokens, width), BF16), pltpu.VMEM((width, tokens), BF16),
        pltpu.VMEM((tokens, width), F32), pltpu.VMEM((tokens, width), F32),
    ]
    return grad_call(body, core, ins, outs, scratch, tiles, "ffn_both")


def ffn_back(core, upstream, grad_kvs, kv_weight, memory, hidden, normed, active, slope, gains, norm_layer, w_in, w_out, layer):
    tokens, width = hidden.shape
    units = w_in.shape[2]
    tile = width
    tiles = units // tile

    def body(_, up_ref, *refs):
        (kw_ref, mem_ref, h_ref, n_in, z_ref, s_ref, g_ref, wi_ref, wo_ref, grad_ref, dkw_ref,
         send_ref, own_ref, dbi_ref, small_ref, nt_ref, top_ref, dn_ref) = refs[len(grad_kvs) :]
        step = pl.program_id(0)

        @pl.when(step == 0)
        def _():
            nt_ref[...] = n_in[...].T
            grad_kv = added(refs[: len(grad_kvs)])
            dkw_ref[...] = mm_tn(mem_ref[...], grad_kv)
            top = up_ref[...].astype(F32) + mm_nt(grad_kv, kw_ref[...])
            grad_ref[...] = top
            top_ref[...] = top.astype(BF16)
            dn_ref[...] = jnp.zeros_like(dn_ref)

        top = top_ref[...]
        grad_out = mm_tn(z_ref[...], top).astype(BF16)
        grad_inner = (s_ref[...].astype(F32) * mm_nt(top, wo_ref[...])).astype(BF16)
        dbi_ref[...] = jnp.sum(grad_inner.astype(F32), 0, keepdims=True)
        store_grads(step, tiles // 2, send_ref, own_ref, mm(nt_ref[...], grad_inner).astype(BF16), grad_out)
        dn_ref[...] += mm_nt(grad_inner, wi_ref[...])

        @pl.when(step == tiles - 1)
        def _():
            back, grad_gain, grad_bias = norm_back(h_ref[...], row_of(g_ref, norm_layer), dn_ref[...])
            grad_ref[...] += back
            grad_top = jnp.sum(top_ref[...].astype(F32), 0, keepdims=True)
            small_ref[...] = jnp.concatenate([grad_gain, grad_bias, grad_top], 0)

    ins = [("full", None, a) for a in (upstream, *grad_kvs, kv_weight, memory, hidden, normed)] + [
        ("units", (tokens, tile), active), ("units", (tokens, tile), slope), ("full", None, gains),
        ("w_in", (layer, (width, tile)), w_in), ("w_out", (layer, (tile, width)), w_out),
    ]
    half = (tiles // 2, 2, width, tile)
    outs = [
        ("all", (tokens, width), (tokens, width), F32), ("all", (width, PAIR), (width, PAIR), F32),
        ("send", half, half, BF16), ("own", half, half, BF16),
        ("units", (1, tile), (1, units), F32), ("all", (3, width), (3, width), F32),
    ]
    scratch = [
        pltpu.VMEM((width, tokens), BF16), pltpu.VMEM((tokens, width), BF16), pltpu.VMEM((tokens, width), F32),
    ]
    return grad_call(body, core, ins, outs, scratch, tiles, "ffn_back")


def digit_of(axis, count):
    if isinstance(axis, tuple):
        return (lax.axis_index(axis[0]) >> axis[1]) & (count - 1)
    return lax.axis_index(axis)


def swap(value, axis, size, mask):
    return lax.ppermute(value, axis, [(i, i ^ mask) for i in range(size)])


def every_block(value, axis, size):
    return [value] + [swap(value, axis, size, d) for d in range(1, size)]


def give_back(blocks, axis, size):
    return [blocks[0]] + [swap(blocks[d], axis, size, d) for d in range(1, size)]


def row_chunks(rows, most=256):
    return [(at, min(most, rows - at)) for at in range(0, rows, most)]


def fold(groups, merge=False, dtype=BF16, name="fold"):
    args, outs, places = [], [], []
    total = 0
    for addends, axis, count in groups:
        rows, columns = addends[0].shape
        places.append((len(args), total))
        args += list(addends)
        total += rows // count
        if not merge:
            outs += [((rows // count, columns), dtype)] * count
    if merge:
        outs = [((total, groups[0][0][0].shape[1]), dtype)] * groups[0][2]

    def body(*refs):
        out_refs = refs[len(args) :]
        at_out = 0
        for (addends, axis, count), (at, row) in zip(groups, places):
            ins = refs[at : at + len(addends)]
            rows = ins[0].shape[0] // count
            for d in range(count):
                for start, size in row_chunks(rows):
                    place = pl.ds(d * rows + start, size)
                    if axis is not None:
                        place = pl.ds(pl.multiple_of((digit_of(axis, count) ^ d) * rows + start, 16), size)
                    part = ins[0][place].astype(F32)
                    for ref in ins[1:]:
                        part = part + ref[place].astype(F32)
                    if merge:
                        out_refs[d][row + start : row + start + size] = part.astype(dtype)
                    else:
                        out_refs[at_out + d][start : start + size] = part.astype(dtype)
            at_out += count

    outs = call(body, outs, args, name=name)
    if merge:
        return list(outs)
    result, at = [], 0
    for _, _, count in groups:
        result.append(list(outs[at : at + count]))
        at += count
    return result


def unfold(groups, sizes=None, joined=None, name="unfold"):
    args, outs, places = [], [], []
    for blocks, axis, count in groups:
        rows, columns = blocks[0].shape
        parts = sizes or [rows]
        at = 0
        for many in joined or [1] * len(parts):
            base = 0
            for size in parts[at : at + many]:
                places.append((len(outs), base))
                base += size * count
            outs.append(((base, columns), BF16))
            at += many
        args += list(blocks)

    def body(*refs):
        out_refs = refs[len(args) :]
        at = at_place = 0
        for blocks, axis, count in groups:
            ins = refs[at : at + count]
            at += count
            digit = digit_of(axis, count)
            parts = sizes or [ins[0].shape[0]]
            for d in range(count):
                row = 0
                for (out, first), size in zip(places[at_place : at_place + len(parts)], parts):
                    base = first + (digit ^ d) * size
                    for start, part in row_chunks(size):
                        place = pl.ds(pl.multiple_of(base + start, 16), part)
                        out_refs[out][place] = ins[d][row + start : row + start + part]
                    row += size
            at_place += len(parts)

    return call(body, outs, args, name=name)


def place_grads(core, own, other, layer, shapes, before, name):
    pieces = [*own, *other]
    half = len(own)
    _, _, width, tile = own[0].shape

    def body(*refs):
        parts = refs[1 : 1 + 2 * half]
        in_ref, out_ref = refs[-2:]
        for k in range(2 * half):

            @pl.when(pl.program_id(0) == k)
            def _():
                in_ref[...] = parts[k][0].astype(F32)
                out_ref[...] = parts[k][1].astype(F32)

    def unit(k, core_ref):
        near = jnp.where(k < half, core_ref[0], 1 - core_ref[0])
        return near * half + lax.rem(k, half)

    kernel = pl.pallas_call(
        body,
        grid_spec=pltpu.PrefetchScalarGridSpec(
            num_scalar_prefetch=1,
            grid=(2 * half,),
            in_specs=[pl.BlockSpec((None, 2, width, tile), lambda k, c: (0, 0, 0, 0)) for _ in pieces]
            + [pl.BlockSpec(memory_space=pl.ANY) for _ in before],
            out_specs=(
                pl.BlockSpec((None, width, tile), lambda k, c: (layer, 0, unit(k, c))),
                pl.BlockSpec((None, tile, width), lambda k, c: (layer, unit(k, c), 0)),
            ),
        ),
        out_shape=tuple(jax.ShapeDtypeStruct(shape, F32) for shape in shapes),
        input_output_aliases={1 + len(pieces) + i: i for i in range(len(before))},
        cost_estimate=cost(name),
        compiler_params=pltpu.CompilerParams(vmem_limit_bytes=VMEM_LIMIT),
        name=name,
    )
    return Order.run(kernel, [core, *pieces, *before])


def place_first(core, own, other, units):
    width = own[0].shape[2]
    return place_grads(core, own, other, 1, [(2, width, units), (2, units, width)], [], "place_first")


def place_second(core, own, other, grad_in, grad_out):
    return place_grads(core, own, other, 0, [grad_in.shape, grad_out.shape], [grad_in, grad_out], "place_second")


def place_experts(core_pairs, per, width):
    args = [part for own, other, _ in core_pairs for part in (own, other)]
    subs = sum(len(layers) for _, _, layers in core_pairs)
    half = width // 2

    def body(*refs):
        out_ref = refs[-1]
        core = lax.axis_index(CORE)
        for k, (_, _, layers) in enumerate(core_pairs):
            for place, ref in ((core, refs[2 * k]), (1 - core, refs[2 * k + 1])):
                for i, layer in enumerate(layers):
                    for expert in range(per):
                        at = (i * per + expert) * half
                        row = pl.multiple_of(place * half, half)
                        out_ref[layer, expert, pl.ds(row, half)] = ref[at : at + half].astype(F32)

    return call(body, [((subs, per, width, PAIR), F32)], args, name="place_experts")[0]


def lanes(count):
    return [slice(c * PAIR, (c + 1) * PAIR) for c in range(count)]


def pack_small(kvs, routers, rows, in_biases):
    args = [*kvs, *routers, *rows, *in_biases]
    width = kvs[0].shape[0]
    wide = width // PAIR
    units = in_biases[0].shape[1]
    used = len(kvs) * width + len(routers) * wide * EXPERTS + sum(r.shape[0] for r in rows) * wide
    used += len(in_biases) * (units // PAIR)
    total = used + -used % 1024

    def body(*refs):
        ins, outs, buffer = refs[: len(args)], refs[len(args) : -1], refs[-1]
        at = 0
        for ref in ins[: len(kvs)]:
            buffer[at : at + width] = ref[...]
            at += width
        ins = ins[len(kvs) :]
        for ref in ins[: len(routers)]:
            for lane in lanes(wide):
                buffer[at : at + EXPERTS] = ref[:, lane]
                at += EXPERTS
        for ref in ins[len(routers) :]:
            for row in range(ref.shape[0]):
                for lane in lanes(ref.shape[1] // PAIR):
                    buffer[at : at + 1] = ref[row : row + 1, lane]
                    at += 1
        buffer[at:] = jnp.zeros((total - at, PAIR), F32)
        share = total // 2
        digit = lax.axis_index(CORE)
        for d in range(2):
            outs[d][...] = buffer[pl.ds(pl.multiple_of((digit ^ d) * share, share), share)].astype(BF16)

    return call(
        body, [((total // 2, PAIR), BF16)] * 2, args, scratch=[pltpu.VMEM((total, PAIR), F32)], name="pack_small"
    )


def unpack_small(parts, counts, width, units):
    share = parts[0].shape[0]
    n_kv, n_router, picks, n_bias = counts
    wide = width // PAIR
    outs = [((n_kv, width, PAIR), F32), ((n_router, EXPERTS, width), F32)]
    outs += [((len(pick), width), F32) for pick in picks] + [((n_bias, units), F32)]
    n_rows = sum(len(pick) for pick in picks)

    def body(*refs):
        ins, outs, buffer = refs[:2], refs[2:-1], refs[-1]
        digit = lax.axis_index(CORE)
        for d in range(2):
            buffer[pl.ds(pl.multiple_of((digit ^ d) * share, share), share)] = ins[d][...].astype(F32)
        at = 0
        for i in range(n_kv):
            outs[0][i] = buffer[at : at + width]
            at += width
        for i in range(n_router):
            for lane in lanes(wide):
                outs[1][i, :, lane] = buffer[at : at + EXPERTS]
                at += EXPERTS
        for out, pick in zip(outs[2:-1], picks):
            for k, row in enumerate(pick):
                for c, lane in enumerate(lanes(wide)):
                    place = at + row * wide + c
                    out[k : k + 1, lane] = buffer[place : place + 1]
        at += n_rows * wide
        for i in range(n_bias):
            for lane in lanes(units // PAIR):
                outs[-1][i : i + 1, lane] = buffer[at : at + 1]
                at += 1

    return call(body, outs, parts, scratch=[pltpu.VMEM((2 * share, PAIR), F32)], name="unpack_small")


def after(value, *first):
    return lax.optimization_barrier((value, first))[0]


def shards(
    sizes, enc_input, dec_input, enc_segments, dec_segments, routes, enc_out_grad, dec_out_grad,
    enc_gains, enc_biases, dec_gains, dec_biases, kv_weights, router_weights, expert_weights,
    ffn_in, ffn_in_bias, ffn_out, ffn_out_bias,
):
    n_core, n_y, n_ep, n_seq = sizes[CORE], sizes[Y], sizes[EP], sizes[SEQ]
    rows, span, width = enc_input.shape
    tokens = rows * span
    per = expert_weights.shape[1]
    units = ffn_in.shape[2]
    core = lax.axis_index(CORE).astype(jnp.int32).reshape(1)
    Order.start()

    flat = lambda a: a.reshape(tokens, a.shape[-1])
    enc_x, dec_x = flat(enc_input), flat(dec_input)
    enc_up, dec_up = flat(enc_out_grad), flat(dec_out_grad)
    kv_w = [Layer(kv_weights, i) for i in range(3)]
    router_t = router_weights.transpose(0, 2, 1)
    routers = [Layer(router_t, i) for i in range(3)]

    n_one, kv_one, w_send = norm_kv(enc_x, enc_gains, enc_biases, kv_weights, 0, 0, expert_weights, [0])
    w_enc = [Layer(expert_weights, 0)] + every_block(w_send, EP, n_ep)[1:]
    kvs_one = every_block(kv_one, SEQ, n_seq)
    n_three, kv_three, *w_sends = norm_kv(dec_x, dec_gains, dec_biases, kv_weights, 0, 1, expert_weights, [1, 2])
    kv_near = swap(kv_three, SEQ, n_seq, 1)
    meta, q_rows = prepare(routes.transpose(0, 1, 3, 2), enc_segments, dec_segments, n_ep, n_seq, per)
    q_one, aux_one = queries(n_one, w_enc, routers[0], meta, 0)
    w_got = every_block(after(w_sends[0], q_one), EP, n_ep)
    w_dec = [Layer(expert_weights, 1)] + w_got[1:]
    o_one, lse_one, enc_mid = attend(
        enc_x, q_one, aux_one, kvs_one, w_enc, meta, q_rows, 0, 0, 0, False
    )
    w_cross = [Layer(expert_weights, 2)] + every_block(after(w_sends[1], o_one), EP, n_ep)[1:]
    kv_pair = jnp.concatenate([kv_three, after(kv_near, o_one)])
    kv_far_got = [swap(kv_pair, SEQ, n_seq, 2 * d) for d in range(1, n_seq // 2)]
    kvs_three = [kv_three, kv_near] + [Rows(got, tokens, i) for got in kv_far_got for i in range(2)]
    n_two, z_two, slope_two, memory, kv_mem = ffn_forward(
        enc_mid, enc_gains, enc_biases, 1, ffn_in, ffn_in_bias, ffn_out, ffn_out_bias, 0, kv_weights[2], 4
    )
    kvs_mem = every_block(kv_mem, SEQ, n_seq)
    q_three, aux_three = queries(n_three, w_dec, routers[1], meta, 1)
    o_three, lse_three, dec_mid = attend(
        dec_x, q_three, aux_three, kvs_three, w_dec, meta, q_rows, 1, 1, 1, True
    )
    n_four, q_four, aux_four = norm_queries(dec_mid, dec_gains, dec_biases, 1, w_cross, routers[2], meta, 2)
    o_four, lse_four, dec_late = attend(
        dec_mid, q_four, aux_four, kvs_mem, w_cross, meta, q_rows, 2, 1, 0, False
    )

    other_core = lambda a: swap(a, CORE, n_core, 1)
    two = lambda a: a.reshape(2, a.shape[0] // 2, a.shape[1])

    near, far = ((SEQ, 0), 2), ((SEQ, 1), n_seq // 2)

    def near_swap(blocks):
        return [blocks[0], swap(blocks[1], SEQ, n_seq, 1)]

    def far_swap(blocks):
        return [blocks[0]] + [swap(blocks[d], SEQ, n_seq, 2 * d) for d in range(1, far[1])]

    def kv_far(keep, got):
        return far_swap(fold([([keep, got], None, far[1])])[0])

    def z_near(groups):
        return near_swap(fold([(addends, *near) for addends in groups], merge=True))

    def z_far(parts):
        return far_swap(fold([(parts, *far)])[0])

    def z_all(parts):
        ((done,),) = fold([(parts, None, 1)])
        return far_swap([done] * far[1])

    def z_back(parts):
        (done,) = unfold([(parts, *far)])
        return near_swap([done] * 2)

    def back_second(parts):
        share = parts[0].shape[0] // 2
        a, b = unfold([(parts, *near)], [share, share])
        return every_block(a, Y, n_y), every_block(b, EP, n_ep)

    def first_parts(own, got):
        pairs = [[Layer(two(own), i), Layer(two(got), i)] for i in range(2)]
        a, b = fold([(pairs[0], EP, n_ep), (pairs[1], Y, n_y)])
        return give_back(a, EP, n_ep), give_back(b, Y, n_y)

    def second_parts(a, b):
        a, b = fold([(a, Y, n_y), (b, EP, n_ep)])
        return give_back(a, Y, n_y), give_back(b, EP, n_ep)

    def back_first(a, b):
        a, b = unfold([(a, Y, n_y), (b, EP, n_ep)])
        return every_block(a, EP, n_ep), every_block(b, Y, n_y)

    def back_core(a, b):
        parts = unfold([(a, EP, n_ep), (b, Y, n_y)])
        return list(parts), [other_core(part) for part in parts]

    dec_out, grad_late, dec_send, dec_own, dbi_dec, small_dec = ffn_both(
        core, dec_late, dec_up, dec_gains, dec_biases, 2, ffn_in, ffn_in_bias, ffn_out, ffn_out_bias, 1
    )
    half = (dec_own.shape[0] * 2 * width, dec_own.shape[3])
    dec_got = other_core(dec_send.reshape(half))
    mem_keep, mem_near, dq_four, dlog_four = attend_back(
        grad_late, o_four, q_four, aux_four, lse_four, kvs_mem, w_cross, meta, q_rows, 2, 1, 0, False
    )
    mem_near = swap(mem_near, SEQ, n_seq, 1)
    dec_a, dec_b = first_parts(dec_own.reshape(half), dec_got)
    cross_own, cross_send, dr_cross, grad_mid, small_cross = expert_back(
        grad_late, n_four, o_four, aux_four, dq_four, dlog_four, w_cross, routers[2], meta, 2,
        dec_mid, dec_gains, 1
    )
    cross_got = other_core(cross_send)
    dkv_mem = kv_far(mem_keep, mem_near)
    three_keep, three_near, dq_three, dlog_three = attend_back(
        grad_mid, o_three, q_three, aux_three, lse_three, kvs_three, w_dec, meta, q_rows, 1, 1, 1, True
    )
    three_near = swap(three_near, SEQ, n_seq, 1)
    x_cross = give_back(fold([([cross_own, cross_got], None, n_ep)], True), EP, n_ep)
    dec_a, dec_b = second_parts(dec_a, dec_b)
    grad_enc, dkw_cross, enc_send, enc_own, dbi_enc, small_enc = ffn_back(
        core, enc_up, dkv_mem, kv_w[2], memory, enc_mid, n_two, z_two, slope_two, enc_gains, 1,
        ffn_in, ffn_out, 0,
    )
    enc_got = other_core(enc_send.reshape(half))
    dkv_three = kv_far(three_keep, three_near)
    dec_parts = z_near([dec_a, dec_b])
    one_keep, one_near, dq_one, dlog_one = attend_back(
        grad_enc, o_one, q_one, aux_one, lse_one, kvs_one, w_enc, meta, q_rows, 0, 0, 0, False
    )
    one_near = swap(one_near, SEQ, n_seq, 1)
    enc_a, enc_b = first_parts(enc_own.reshape(half), enc_got)
    Order.share = LIGHT
    enc_own_x, enc_send_x, dr_enc, dn_one = expert_back(
        grad_enc, n_one, o_one, aux_one, dq_one, dlog_one, w_enc, routers[0], meta, 0
    )
    dec_own_x, dec_send_x, dr_dec, dn_three = expert_back(
        grad_mid, n_three, o_three, aux_three, dq_three, dlog_three, w_dec, routers[1], meta, 1
    )
    dkv_one = kv_far(one_keep, one_near)
    dec_parts = z_far(dec_parts)
    dec_grad, dkw_dec, small_three = self_finish(
        grad_mid, dn_three, dkv_three, n_three, kv_w[1], dec_x, dec_gains, 0
    )
    enc_grad, dkw_enc, small_one = self_finish(
        grad_enc, dn_one, dkv_one, n_one, kv_w[0], enc_x, enc_gains, 0
    )
    small_own, small_send = pack_small(
        [dkw_enc, dkw_dec, dkw_cross], [dr_enc, dr_dec, dr_cross],
        [small_one, small_enc, small_three, small_cross, small_dec], [dbi_enc, dbi_dec],
    )
    enc_a, enc_b = second_parts(enc_a, enc_b)
    dec_got_x, enc_got_x = [other_core(after(part, enc_a[0])) for part in (dec_send_x, enc_send_x)]
    Order.share = 1.0
    small_got = other_core(small_send)
    x_dec = give_back(fold([([dec_own_x, dec_got_x], None, n_ep)], True), EP, n_ep)
    dec_parts = z_all(dec_parts)
    enc_parts = z_near([enc_a, enc_b])
    n_x = enc_own_x.shape[0] // n_ep
    n_small = small_own.shape[0]
    halves = [([Rows(enc_own_x, n_x, d), Rows(enc_got_x, n_x, d)], Y, n_y) for d in range(n_ep)]
    x_two = give_back(fold(halves + [([small_own, small_got], Y, n_y)], True), Y, n_y)
    enc_parts = z_far(enc_parts)
    x_one = give_back(fold([(x_cross, Y, n_y), (x_dec, Y, n_y)], True), Y, n_y)
    dec_parts = z_back(dec_parts)
    n_x, n_small = n_x // n_y, n_small // n_y
    enc_rows = [Rows(part, n_ep * n_x, 0) for part in x_two]
    small_rows = [Rows(part, n_small, n_ep * n_x // n_small) for part in x_two]
    x_two = fold([(enc_rows, None, n_ep), (small_rows, EP, n_ep)], True)
    x_two = give_back(x_two, EP, n_ep)
    enc_parts = z_all(enc_parts)
    dec_a, dec_b = back_second(dec_parts)
    n_small = n_small // n_ep
    enc_rows = [Rows(part, n_x, 0) for part in x_two]
    small_rows = [Rows(part, n_small, n_x // n_small) for part in x_two]
    x_parts = z_near([x_one, enc_rows, small_rows])
    enc_parts = z_back(enc_parts)
    dec_a, dec_b = back_first(dec_a, dec_b)
    x_parts = z_far(x_parts)
    enc_a, enc_b = back_second(enc_parts)
    x_parts = z_all(x_parts)
    enc_a, enc_b = back_first(enc_a, enc_b)
    x_parts = z_back(x_parts)
    x_part, small_part = unfold([(x_parts, *near)], [n_x, n_x // 2, n_small // 2], [2, 1])
    x_parts, small_parts = every_block(x_part, Y, n_y), every_block(small_part, EP, n_ep)
    dec_ab, dec_other = back_core(dec_a, dec_b)
    enc_ab, enc_other = back_core(enc_a, enc_b)
    pieces = lambda parts: [part.reshape((-1, 2, width) + dec_own.shape[3:]) for part in parts]
    grad_in, grad_out = place_first(core, pieces(dec_ab), pieces(dec_other), units)
    (small_part,) = unfold([(small_parts, EP, n_ep)])
    small_parts = every_block(small_part, Y, n_y)
    (x_half,) = unfold([(x_parts, Y, n_y)], [n_x] * 3, [3])
    x_other = other_core(x_half)
    grad_in, grad_out = place_second(core, pieces(enc_ab), pieces(enc_other), grad_in, grad_out)
    (small_half,) = unfold([(small_parts, Y, n_y)])
    small_parts = every_block(small_half, CORE, n_core)
    experts = place_experts([(x_half, x_other, (2, 1, 0))], per, width)
    picks = [[0, 2], [1, 3], [5, 7, 9], [6, 8, 10], [4, 11]]
    kv_grad, router_grad, enc_gain, enc_bias, dec_gain, dec_bias, out_bias, in_bias = unpack_small(
        small_parts, (3, 3, picks, 2), width, units
    )
    shape = enc_input.shape
    return (
        memory.reshape(shape), dec_out.reshape(shape), enc_grad.reshape(shape), dec_grad.reshape(shape),
        enc_gain, enc_bias, dec_gain, dec_bias, kv_grad, router_grad.transpose(0, 2, 1), experts,
        grad_in, in_bias, grad_out, out_bias,
    )


def solution(mesh):
    sizes = dict(mesh.shape)
    n_dp, n_ep, n_seq = sizes["dp"], sizes[EP], sizes[SEQ]
    split = jax.sharding.Mesh(mesh.devices.reshape(n_dp // 2, 2, n_ep, n_seq), (Y, CORE, EP, SEQ))
    batch = (Y, CORE, EP)
    tokens = P(batch, SEQ, None)
    rows = P(batch, None)
    experts = P(None, EP, None, None)
    return jax.shard_map(
        partial(shards, dict(split.shape)),
        mesh=split,
        in_specs=(
            tokens, tokens, rows, rows, P(None, batch, SEQ, None), tokens, tokens,
            P(), P(), P(), P(), P(), P(), experts, P(), P(), P(), P(),
        ),
        out_specs=(
            tokens, tokens, tokens, tokens, P(), P(), P(), P(), P(), P(), experts, P(), P(), P(), P(),
        ),
        check_vma=False,
    )
```

```python
from functools import partial

import jax
import jax.numpy as jnp
from jax import lax
from jax.experimental import pallas as pl
from jax.experimental.pallas import tpu as pltpu
from jax.sharding import PartitionSpec as P

EXPERTS = 8
HD = 64
TOP = 2
PAIR = 2 * HD

EPS = 1e-05
SCALE = 0.125
NEG = -1e30
F32 = jnp.float32
BF16 = jnp.bfloat16
SQRT_HALF = 0.7071067811865476
INV_SQRT_2PI = 0.3989422804014327
VMEM_LIMIT = 20 * 1024 * 1024

CORE, Y, EP, SEQ = "core", "y", "ep", "seq"

ROUTE = 0
LOCAL_ROUTE = 6
KEY_SEG = 12


def mm(left, right):
    return lax.dot_general(left, right, (((1,), (0,)), ((), ())), preferred_element_type=F32)


def mm_nt(left, right):
    return lax.dot_general(left, right, (((1,), (1,)), ((), ())), preferred_element_type=F32)


def mm_tn(left, right):
    return lax.dot_general(left, right, (((0,), (0,)), ((), ())), preferred_element_type=F32)


def iota(shape, dim):
    return lax.broadcasted_iota(jnp.int32, shape, dim)


def standardize(hidden):
    centred = hidden - jnp.mean(hidden, -1, keepdims=True)
    inverse = lax.rsqrt(jnp.mean(centred * centred, -1, keepdims=True) + EPS)
    return centred * inverse, inverse


def norm(hidden, gain, bias):
    return standardize(hidden)[0] * gain + bias


def norm_back(hidden, gain, upstream):
    unit, inverse = standardize(hidden)
    grad_gain = jnp.sum(upstream * unit, 0, keepdims=True)
    grad_bias = jnp.sum(upstream, 0, keepdims=True)
    scaled = upstream * gain
    centred = scaled - jnp.mean(scaled, -1, keepdims=True)
    projected = jnp.mean(scaled * unit, -1, keepdims=True)
    return inverse * (centred - unit * projected), grad_gain, grad_bias


def widened(router):
    full = router.astype(F32)
    return jnp.concatenate([full, jnp.zeros((PAIR - full.shape[0], full.shape[1]), F32)], 0).astype(BF16)


def row_of(ref, index):
    return ref[...].astype(F32)[index : index + 1]


class Order:
    last = None
    share = 1.0

    @classmethod
    def start(cls):
        cls.last = None
        cls.share = 1.0

    @classmethod
    def run(cls, kernel, args):
        args = [operand(arg) for arg in args]
        if cls.last is not None:
            args[0], _ = lax.optimization_barrier((args[0], cls.last))
        outs = kernel(*args)
        cls.last = outs[0]
        return outs


class Layer:
    def __init__(self, array, index):
        self.array, self.index = array, index
        self.shape = array.shape[1:]

    def spec(self):
        index, rest = self.index, len(self.shape)
        return pl.BlockSpec((None,) + self.shape, lambda *_: (index,) + (0,) * rest)


class Rows:
    def __init__(self, array, rows, index):
        self.array, self.index = array, index
        self.shape = (rows, array.shape[1])

    def spec(self):
        index = self.index
        return pl.BlockSpec(self.shape, lambda *_: (index, 0))


def operand(arg):
    return arg.array if isinstance(arg, (Layer, Rows)) else arg


def whole(arg):
    if isinstance(arg, (Layer, Rows)):
        return arg.spec()
    rest = len(arg.shape)
    return pl.BlockSpec(arg.shape, lambda *_: (0,) * rest)


TIMES = {
    "norm_kv": 0.7, "prepare": 0.3, "queries": 2.0, "norm_queries": 2.3, "attend": 3.4, "ffn_forward": 6.2,
    "ffn_both": 12.0, "attend_back": 5.0, "expert_back": 3.4, "ffn_back": 8.5, "self_finish": 2.0,
    "place_first": 3.5, "place_second": 3.5, "unpack_small": 1.0,
}
PACE = 1.0
LATER = 4.0
FOLD = 0.4
LIGHT = 0.05
ROOMY = 60 * 1024 * 1024


def cost(name):
    first = ("norm_kv", "prepare", "queries", "norm_queries", "attend", "ffn_forward", "ffn_both")
    micros = TIMES.get(name, FOLD) * (PACE if name in first else LATER)
    micros *= Order.share
    return pl.CostEstimate(flops=int(micros * 1e9), bytes_accessed=int(micros * 3e6), transcendentals=0)


def call(body, outs, args, scratch=(), limit=14 * 1024 * 1024, name=None):
    shapes = [jax.ShapeDtypeStruct(s, d) for s, d in outs]
    kernel = pl.pallas_call(
        body,
        grid=(1,),
        out_shape=tuple(shapes),
        in_specs=[whole(arg) for arg in args],
        out_specs=tuple(whole(out) for out in shapes),
        scratch_shapes=list(scratch),
        cost_estimate=cost(name),
        compiler_params=pltpu.CompilerParams(vmem_limit_bytes=limit),
        name=name,
    )
    return Order.run(kernel, args)


def prepare(routes, enc_seg, dec_seg, n_ep, n_seq, per):
    subs, rows, _, span = routes.shape
    tokens = rows * span
    used = 2 * subs * TOP + 2 * n_seq

    def body(r_ref, e_ref, d_ref, meta_ref, rows_ref):
        base = lax.axis_index(EP) * per
        me = lax.axis_index(SEQ)
        lines = []
        for flip in (False, True):
            for sub in range(subs):
                for j in range(TOP):
                    line = jnp.concatenate([r_ref[sub, r, j : j + 1, :] for r in range(rows)], 1)
                    lines.append(line ^ base if flip else line)
        queries = []
        for ref in (e_ref, d_ref):
            for d in range(n_seq):
                at = pl.multiple_of((me ^ d) * span, span)
                block = ref[:, pl.ds(at, span)]
                lines.append(jnp.concatenate([block[r : r + 1] for r in range(rows)], 1))
                if d == 0:
                    queries.append(jnp.concatenate([block] * TOP, 1))
        rows_ref[...] = jnp.concatenate(queries, 0)
        lines = [line.astype(F32) for line in lines]
        lines.append(jnp.zeros((PAIR - used, tokens), F32))
        meta_ref[...] = jnp.concatenate(lines, 0).T.astype(jnp.int32)

    return call(
        body,
        [((tokens, PAIR), jnp.int32), ((2 * rows, TOP * span), jnp.int32)],
        (routes, enc_seg, dec_seg),
        name="prepare",
    )


def norm_kv(hidden, gains, biases, kv_weights, layer, index, expert_weights, copied):
    tokens, width = hidden.shape
    stack = gains.shape[0]

    def body(h_ref, g_ref, b_ref, w_ref, e_ref, n_ref, kv_ref, *rest):
        e_outs = rest[: len(copied)]
        h_in, g_in, b_in, w_in, sems = rest[len(copied) :]
        pairs = [(h_ref, h_in), (g_ref, g_in), (b_ref, b_in), (w_ref.at[index], w_in)]
        pairs += [(e_ref.at[k], out) for k, out in zip(copied, e_outs)]
        moves = [pltpu.make_async_copy(*pair, sems.at[i]) for i, pair in enumerate(pairs)]
        for move in moves:
            move.start()
        for move in moves[:3]:
            move.wait()
        normed = norm(h_in[...].astype(F32), row_of(g_in, layer), row_of(b_in, layer)).astype(BF16)
        n_ref[...] = normed
        moves[3].wait()
        kv_ref[...] = mm(normed, w_in[...]).astype(BF16)
        for move in moves[4:]:
            move.wait()

    held = pl.BlockSpec(memory_space=pltpu.HBM)
    outs = [((tokens, width), BF16), ((tokens, PAIR), BF16)] + [(expert_weights.shape[1:], BF16)] * len(copied)
    shapes = [jax.ShapeDtypeStruct(*out) for out in outs]
    kernel = pl.pallas_call(
        body,
        out_shape=tuple(shapes),
        in_specs=[held] * 5,
        out_specs=tuple(pl.BlockSpec(memory_space=pltpu.VMEM) for _ in shapes),
        scratch_shapes=[
            pltpu.VMEM((tokens, width), BF16), pltpu.VMEM((stack, width), BF16), pltpu.VMEM((stack, width), BF16),
            pltpu.VMEM(kv_weights.shape[1:], BF16), pltpu.SemaphoreType.DMA((4 + len(copied),)),
        ],
        cost_estimate=cost("norm_kv"),
        compiler_params=pltpu.CompilerParams(vmem_limit_bytes=ROOMY),
        name="norm_kv",
    )
    return Order.run(kernel, [hidden, gains, biases, kv_weights, expert_weights])


def query_part(normed, weights, router, meta_ref, sub, q_ref, aux_ref):
    tokens = normed.shape[0]
    per = weights[0].shape[0]
    lane = iota((tokens, PAIR), 1)
    local = [meta_ref[:, LOCAL_ROUTE + TOP * sub + j : LOCAL_ROUTE + TOP * sub + j + 1] for j in range(TOP)]
    route = [meta_ref[:, ROUTE + TOP * sub + j : ROUTE + TOP * sub + j + 1] for j in range(TOP)]
    picked = [jnp.zeros((tokens, PAIR), F32) for _ in range(TOP)]
    for expert in range(EXPERTS):
        every = mm(normed, weights[expert // per][expert % per])
        picked = [jnp.where(local[j] == expert, every, picked[j]) for j in range(TOP)]
    for j in range(TOP):
        rounded = picked[j].astype(BF16).astype(F32) * SCALE
        q_ref[j] = jnp.where(lane < HD, rounded, 0.0).astype(BF16)
    logits = mm_nt(normed, widened(router))
    hit = [lane == route[j] for j in range(TOP)]
    chosen = [jnp.sum(jnp.where(hit[j], logits, 0.0), -1, keepdims=True) for j in range(TOP)]
    top = jnp.maximum(chosen[0], chosen[1])
    raised = [jnp.exp(value - top) for value in chosen]
    total = raised[0] + raised[1]
    count = jnp.where(hit[0] | hit[1], 1.0, 0.0).astype(BF16)
    before = (iota((tokens, tokens), 0) > iota((tokens, tokens), 1)).astype(F32).astype(BF16)
    ranks = mm(before, count)
    capacity = tokens * TOP // EXPERTS
    aux = jnp.zeros((tokens, PAIR), F32)
    for j in range(TOP):
        rank = jnp.sum(jnp.where(hit[j], ranks, 0.0), -1, keepdims=True)
        kept = jnp.where(rank < capacity, 1.0, 0.0)
        aux = jnp.where(lane == j, raised[j] / total, aux)
        aux = jnp.where(lane == TOP + j, kept, aux)
    aux_ref[...] = aux


def queries(normed, weights, router, meta, sub):
    tokens, width = normed.shape
    count = len(weights)

    def body(*refs):
        n_ref, w_refs = refs[0], refs[1 : 1 + count]
        r_ref, meta_ref, q_ref, aux_ref = refs[1 + count :]
        query_part(n_ref[...], w_refs, r_ref[...], meta_ref, sub, q_ref, aux_ref)

    return call(
        body,
        [((TOP, tokens, PAIR), BF16), ((tokens, PAIR), F32)],
        (normed, *weights, router, meta),
        name="queries",
    )


def norm_queries(hidden, gains, biases, layer, weights, router, meta, sub):
    tokens, width = hidden.shape
    count = len(weights)

    def body(*refs):
        h_ref, g_ref, b_ref, w_refs = refs[0], refs[1], refs[2], refs[3 : 3 + count]
        r_ref, meta_ref, n_ref, q_ref, aux_ref = refs[3 + count :]
        normed = norm(h_ref[...], row_of(g_ref, layer), row_of(b_ref, layer)).astype(BF16)
        n_ref[...] = normed
        query_part(normed, w_refs, r_ref[...], meta_ref, sub, q_ref, aux_ref)

    return call(
        body,
        [((tokens, width), BF16), ((TOP, tokens, PAIR), BF16), ((tokens, PAIR), F32)],
        (hidden, gains, biases, *weights, router, meta),
        name="norm_queries",
    )


def allowed_block(meta_ref, q_row, place, rows, column, causal):
    allowed = meta_ref[rows, column : column + 1] == q_row
    if causal:
        span, wide = rows.stop - rows.start, q_row.shape[1]
        me = lax.axis_index(SEQ)
        key = iota((span, wide), 0) + ((me ^ place) - me) * span
        query = lax.rem(iota((1, wide), 1), span)
        allowed = allowed & (query >= key)
    return allowed


def mixed_slots(mixed, aux, meta_ref, sub):
    scaled = [mixed[j] * (aux[:, j : j + 1] * aux[:, TOP + j : TOP + j + 1]) for j in range(TOP)]
    local = [meta_ref[:, LOCAL_ROUTE + TOP * sub + j : LOCAL_ROUTE + TOP * sub + j + 1] for j in range(TOP)]

    def of(expert):
        part = jnp.where(local[1] == expert, scaled[1], 0.0)
        return jnp.where(local[0] == expert, scaled[0], part).astype(BF16)

    return of


def attend(hidden, query, aux, key_values, weights, meta, q_rows, sub, q_base, k_base, causal):
    tokens, width = hidden.shape
    rows = q_rows.shape[0] // 2
    span = tokens // rows
    wide = TOP * span
    blocks, owners = len(key_values), len(weights)
    per = weights[0].shape[0]

    def body(*refs):
        h_ref, q_ref, aux_ref = refs[:3]
        kv_refs = refs[3 : 3 + blocks]
        w_refs = refs[3 + blocks : 3 + blocks + owners]
        meta_ref, qr_ref, o_ref, lse_ref, out_ref, s_ref = refs[3 + blocks + owners :]
        lane = iota((wide, PAIR), 1)
        for r in range(rows):
            here = slice(r * span, (r + 1) * span)
            q_row = qr_ref[q_base * rows + r : q_base * rows + r + 1, :]
            q_all = jnp.concatenate([q_ref[j, here] for j in range(TOP)], 0)
            top = jnp.full((1, wide), NEG, F32)
            for d in range(blocks):
                scores = mm_nt(kv_refs[d][here], q_all)
                allowed = allowed_block(
                    meta_ref, q_row, d, here, KEY_SEG + k_base * blocks + d, causal
                )
                scores = jnp.where(allowed, scores, NEG)
                s_ref[d * span : (d + 1) * span] = scores
                top = jnp.maximum(top, jnp.max(scores, 0, keepdims=True))
            total = jnp.zeros((1, wide), F32)
            mixed = jnp.zeros((PAIR, wide), F32)
            for d in range(blocks):
                probs = jnp.exp(s_ref[d * span : (d + 1) * span] - top)
                total = total + jnp.sum(probs, 0, keepdims=True)
                mixed = mixed + mm_tn(kv_refs[d][here], probs.astype(BF16))
            lse_ref[r : r + 1] = top + jnp.log(total)
            mixed = jnp.where(lane < HD, 0.0, (mixed / total).T).astype(BF16)
            for j in range(TOP):
                o_ref[j, here] = mixed[j * span : (j + 1) * span]
        slot = mixed_slots([o_ref[j].astype(F32) for j in range(TOP)], aux_ref[...], meta_ref, sub)
        result = h_ref[...].astype(F32)
        for expert in range(0, EXPERTS, 2):
            part = jnp.concatenate([slot(expert), slot(expert + 1)], 1)
            weight = jnp.concatenate([w_refs[e // per][e % per] for e in (expert, expert + 1)], 1)
            result = result + mm_nt(part, weight)
        out_ref[...] = result

    args = (hidden, query, aux, *key_values, *weights, meta, q_rows)
    return call(
        body,
        [((TOP, tokens, PAIR), BF16), ((rows, wide), F32), ((tokens, width), F32)],
        args,
        scratch=[pltpu.VMEM((blocks * span, wide), F32)],
        name="attend",
    )


def attend_back(upstream, mixed, query, aux, lse, key_values, weights, meta, q_rows, sub, q_base, k_base, causal):
    tokens, width = upstream.shape
    rows = q_rows.shape[0] // 2
    span = tokens // rows
    wide = TOP * span
    blocks, owners = len(key_values), len(weights)
    per = weights[0].shape[0]

    def body(*refs):
        up_ref, o_ref, q_ref, aux_ref, lse_ref = refs[:5]
        kv_refs = refs[5 : 5 + blocks]
        w_refs = refs[5 + blocks : 5 + blocks + owners]
        meta_ref, qr_ref = refs[5 + blocks + owners : 7 + blocks + owners]
        keep_ref, near_ref, dq_ref, dlog_ref, do_ref = refs[7 + blocks + owners :]
        rounded = up_ref[...].astype(BF16)
        lane = iota((tokens, PAIR), 1)
        local = [meta_ref[:, LOCAL_ROUTE + TOP * sub + j : LOCAL_ROUTE + TOP * sub + j + 1] for j in range(TOP)]
        route = [meta_ref[:, ROUTE + TOP * sub + j : ROUTE + TOP * sub + j + 1] for j in range(TOP)]
        picked = [jnp.zeros((tokens, PAIR), F32) for _ in range(TOP)]
        for expert in range(EXPERTS):
            every = mm(rounded, w_refs[expert // per][expert % per])
            picked = [jnp.where(local[j] == expert, every, picked[j]) for j in range(TOP)]
        aux = aux_ref[...]
        gate = [aux[:, j : j + 1] for j in range(TOP)]
        kept = [aux[:, TOP + j : TOP + j + 1] for j in range(TOP)]
        grad_gate = [
            kept[j] * jnp.sum(picked[j] * o_ref[j].astype(F32), -1, keepdims=True) for j in range(TOP)
        ]
        inner = gate[0] * grad_gate[0] + gate[1] * grad_gate[1]
        dlog = jnp.zeros((tokens, PAIR), F32)
        for j in range(TOP):
            dlog = jnp.where(lane == route[j], gate[j] * (grad_gate[j] - inner), dlog)
            do_ref[j] = jnp.where(lane < HD, 0.0, picked[j] * (gate[j] * kept[j])).astype(BF16)
        dlog_ref[...] = dlog.astype(BF16)
        lane = iota((wide, PAIR), 1)
        for r in range(rows):
            here = slice(r * span, (r + 1) * span)
            q_row = qr_ref[q_base * rows + r : q_base * rows + r + 1, :]
            q_all = jnp.concatenate([q_ref[j, here] for j in range(TOP)], 0)
            do_all = jnp.concatenate([do_ref[j, here] for j in range(TOP)], 0)
            log_total = lse_ref[r : r + 1]
            inner = jnp.zeros((1, wide), F32)
            probs, grads = [], []
            for d in range(blocks):
                scores = mm_nt(kv_refs[d][here], q_all)
                allowed = allowed_block(
                    meta_ref, q_row, d, here, KEY_SEG + k_base * blocks + d, causal
                )
                prob = jnp.exp(jnp.where(allowed, scores, NEG) - log_total)
                grad = mm_nt(kv_refs[d][here], do_all)
                inner = inner + jnp.sum(prob * grad, 0, keepdims=True)
                probs.append(prob)
                grads.append(grad)
            grad_query = jnp.zeros((PAIR, wide), F32)
            for d in range(blocks):
                grad_score = (probs[d] * (grads[d] - inner)).astype(BF16)
                grad_query = grad_query + mm_tn(kv_refs[d][here], grad_score)
                grad_kv = mm(probs[d].astype(BF16), do_all) + mm(grad_score, q_all)
                place = slice(d // 2 * tokens + r * span, d // 2 * tokens + (r + 1) * span)
                (near_ref if d % 2 else keep_ref)[place] = grad_kv.astype(BF16)
            grad_query = jnp.where(lane < HD, grad_query.T * SCALE, 0.0).astype(BF16)
            for j in range(TOP):
                dq_ref[j, here] = grad_query[j * span : (j + 1) * span]

    args = (upstream, mixed, query, aux, lse, *key_values, *weights, meta, q_rows)
    return call(
        body,
        [((blocks // 2 * tokens, PAIR), BF16)] * 2 + [((TOP, tokens, PAIR), BF16), ((tokens, PAIR), BF16)],
        args,
        scratch=[pltpu.VMEM((TOP, tokens, PAIR), BF16)],
        name="attend_back",
    )


def expert_back(upstream, normed, mixed, aux, dq, dlog, weights, router, meta, sub, hidden=None, gains=None, layer=0):
    tokens, width = upstream.shape
    owners = len(weights)
    per = weights[0].shape[0]
    finish = hidden is not None

    def body(*refs):
        up_ref, n_ref, o_ref, aux_ref, dq_ref, dlog_ref = refs[:6]
        w_refs = refs[6 : 6 + owners]
        r_ref, meta_ref = refs[6 + owners : 8 + owners]
        at = 8 + owners
        if finish:
            h_ref, g_ref = refs[at : at + 2]
            at += 2
        own_ref, send_ref, dr_ref, dn_ref = refs[at : at + 4]
        low_core = lax.axis_index(CORE) == 0
        half = width // 2
        slot = mixed_slots([o_ref[j].astype(F32) for j in range(TOP)], aux_ref[...], meta_ref, sub)
        local = [meta_ref[:, LOCAL_ROUTE + TOP * sub + j : LOCAL_ROUTE + TOP * sub + j + 1] for j in range(TOP)]
        grads = [dq_ref[j].astype(F32) * aux_ref[:, TOP + j : TOP + j + 1] for j in range(TOP)]

        def query_slot(expert):
            part = jnp.where(local[1] == expert, grads[1], 0.0)
            return jnp.where(local[0] == expert, grads[0], part).astype(BF16)

        normed_t = n_ref[...].T
        up_t = up_ref[...].astype(BF16).T
        total = mm(dlog_ref[...], widened(r_ref[...]))
        for expert in range(0, EXPERTS, 2):
            both = (expert, expert + 1)
            part = jnp.concatenate([query_slot(e) for e in both], 1)
            weight = jnp.concatenate([w_refs[e // per][e % per] for e in both], 1)
            total = total + mm_nt(part, weight)
            result = jnp.concatenate([slot(e) for e in both], 1)
            grad = (mm(normed_t, part) + mm(up_t, result)).astype(BF16)
            for k, e in enumerate(both):
                low, high = [grad[at : at + half, k * PAIR : (k + 1) * PAIR] for at in (0, half)]
                place = slice(e * half, (e + 1) * half)
                own_ref[place] = jnp.where(low_core, low, high)
                send_ref[place] = jnp.where(low_core, high, low)
        dr_ref[...] = mm_tn(dlog_ref[...], n_ref[...])[:EXPERTS]
        if finish:
            back, grad_gain, grad_bias = norm_back(h_ref[...].astype(F32), row_of(g_ref, layer), total)
            dn_ref[...] = up_ref[...] + back
            refs[at + 4][...] = jnp.concatenate([grad_gain, grad_bias], 0)
        else:
            dn_ref[...] = total

    outs = [((EXPERTS * width // 2, PAIR), BF16)] * 2 + [((EXPERTS, width), F32), ((tokens, width), F32)]
    args = (upstream, normed, mixed, aux, dq, dlog, *weights, router, meta)
    if finish:
        outs = outs + [((2, width), F32)]
        args = args + (hidden, gains)
    return call(body, outs, args, name="expert_back")


def added(refs):
    total = refs[0][...].astype(F32)
    for ref in refs[1:]:
        total = total + ref[...].astype(F32)
    return total.astype(BF16)


def self_finish(upstream, grad_normed, grad_kvs, normed, kv_weight, hidden, gains, layer):
    tokens, width = upstream.shape

    def body(up_ref, dn_ref, *refs):
        n_ref, w_ref, h_ref, g_ref, out_ref, dw_ref, small_ref = refs[len(grad_kvs) :]
        grad_kv = added(refs[: len(grad_kvs)])
        total = dn_ref[...] + mm_nt(grad_kv, w_ref[...])
        dw_ref[...] = mm_tn(n_ref[...], grad_kv)
        back, grad_gain, grad_bias = norm_back(h_ref[...].astype(F32), row_of(g_ref, layer), total)
        out_ref[...] = up_ref[...] + back
        small_ref[...] = jnp.concatenate([grad_gain, grad_bias], 0)

    return call(
        body,
        [((tokens, width), F32), ((width, PAIR), F32), ((2, width), F32)],
        (upstream, grad_normed, *grad_kvs, normed, kv_weight, hidden, gains),
        name="self_finish",
    )


def gelu_parts(inner):
    cdf = 0.5 * (1.0 + lax.erf(inner * SQRT_HALF))
    density = jnp.exp(-0.5 * inner * inner) * INV_SQRT_2PI
    return inner * cdf, cdf + inner * density


def ffn_call(body, tokens, width, hidden, tiles, ins, outs, scratch, name):
    tile = hidden // tiles
    kinds = {
        "full2": lambda s: pl.BlockSpec(s, lambda k: (0, 0)),
        "win": lambda s: pl.BlockSpec((1, width, tile), lambda k: (s, 0, k)),
        "bin": lambda s: pl.BlockSpec((2, tile), lambda k: (0, k)),
        "wout": lambda s: pl.BlockSpec((1, tile, width), lambda k: (s, k, 0)),
        "act": lambda s: pl.BlockSpec((tokens, tile), lambda k: (0, k)),
    }
    kernel = pl.pallas_call(
        body,
        grid=(tiles,),
        in_specs=[kinds[kind](s) for kind, s, _ in ins],
        out_specs=tuple(kinds[kind](shape) for kind, shape, _ in outs),
        out_shape=tuple(jax.ShapeDtypeStruct(shape, dtype) for _, shape, dtype in outs),
        scratch_shapes=scratch,
        cost_estimate=cost(name),
        compiler_params=pltpu.CompilerParams(vmem_limit_bytes=VMEM_LIMIT),
        name=name,
    )
    return Order.run(kernel, [a for _, _, a in ins])


def ffn_forward(hidden, gains, biases, norm_layer, w_in, b_in, w_out, b_out, layer, kv_weight, tiles):
    tokens, width = hidden.shape
    units = w_in.shape[2]

    def body(h_ref, g_ref, b_ref, wi_ref, bi_ref, wo_ref, bo_ref, kw_ref,
             n_out, z_ref, s_ref, mem_ref, kv_ref, n_ref, acc_ref):
        step = pl.program_id(0)

        @pl.when(step == 0)
        def _():
            normed = norm(h_ref[...], row_of(g_ref, norm_layer), row_of(b_ref, norm_layer)).astype(BF16)
            n_ref[...] = normed
            n_out[...] = normed
            acc_ref[...] = h_ref[...] + row_of(bo_ref, layer)

        inner = mm(n_ref[...], wi_ref[0]) + row_of(bi_ref, layer)
        active, slope = gelu_parts(inner)
        active = active.astype(BF16)
        z_ref[...] = active
        s_ref[...] = slope.astype(BF16)
        acc_ref[...] += mm(active, wo_ref[0])

        @pl.when(step == tiles - 1)
        def _():
            memory = acc_ref[...].astype(BF16)
            mem_ref[...] = memory
            kv_ref[...] = mm(memory, kw_ref[...]).astype(BF16)

    ins = [
        ("full2", hidden.shape, hidden), ("full2", gains.shape, gains), ("full2", biases.shape, biases),
        ("win", layer, w_in), ("bin", None, b_in), ("wout", layer, w_out), ("full2", b_out.shape, b_out),
        ("full2", kv_weight.shape, kv_weight),
    ]
    outs = [
        ("full2", (tokens, width), BF16), ("act", (tokens, units), BF16), ("act", (tokens, units), BF16),
        ("full2", (tokens, width), BF16), ("full2", (tokens, PAIR), BF16),
    ]
    scratch = [pltpu.VMEM((tokens, width), BF16), pltpu.VMEM((tokens, width), F32)]
    return ffn_call(body, tokens, width, units, tiles, ins, outs, scratch, "ffn_forward")


def grad_call(body, core, ins, outs, scratch, tiles, name):
    half = tiles // 2

    def unit(k, core_ref):
        far = jnp.where(k < half, 1 - core_ref[0], core_ref[0])
        return far * half + lax.rem(k, half)

    def spec(kind, shape):
        if kind == "w_in":
            layer, (width, tile) = shape
            return pl.BlockSpec((None, width, tile), lambda k, c: (layer, 0, unit(k, c)))
        if kind == "w_out":
            layer, (tile, width) = shape
            return pl.BlockSpec((None, tile, width), lambda k, c: (layer, unit(k, c), 0))
        if kind == "units":
            rows, tile = shape
            return pl.BlockSpec((rows, tile), lambda k, c: (0, unit(k, c)))
        if kind == "send":
            return pl.BlockSpec((1,) + shape[1:], lambda k, c: (jnp.minimum(k, half - 1), 0, 0, 0))
        if kind == "own":
            return pl.BlockSpec((1,) + shape[1:], lambda k, c: (jnp.maximum(k - half, 0), 0, 0, 0))
        rest = len(shape)
        return pl.BlockSpec(shape, lambda k, c: (0,) * rest)

    in_specs = [whole(a) if kind == "full" else spec(kind, shape) for kind, shape, a in ins]
    kernel = pl.pallas_call(
        body,
        grid_spec=pltpu.PrefetchScalarGridSpec(
            num_scalar_prefetch=1,
            grid=(tiles,),
            in_specs=in_specs,
            out_specs=tuple(spec(kind, shape) for kind, shape, _, _ in outs),
            scratch_shapes=scratch,
        ),
        out_shape=tuple(jax.ShapeDtypeStruct(full, dtype) for _, _, full, dtype in outs),
        cost_estimate=cost(name),
        compiler_params=pltpu.CompilerParams(vmem_limit_bytes=VMEM_LIMIT),
        name=name,
    )
    return Order.run(kernel, [core] + [a for _, _, a in ins])


def store_grads(step, half, send_ref, own_ref, grad_in, grad_out):
    @pl.when(step < half)
    def _():
        send_ref[0, 0] = grad_in
        send_ref[0, 1] = grad_out

    @pl.when(step >= half)
    def _():
        own_ref[0, 0] = grad_in
        own_ref[0, 1] = grad_out


def ffn_both(core, hidden, upstream, gains, biases, norm_layer, w_in, b_in, w_out, b_out, layer):
    tokens, width = hidden.shape
    units = w_in.shape[2]
    tile = width
    tiles = units // tile

    def body(_, h_ref, up_ref, g_ref, b_ref, wi_ref, bi_ref, wo_ref, bo_ref,
             out_ref, grad_ref, send_ref, own_ref, dbi_ref, small_ref, n_ref, nt_ref, acc_ref, dn_ref):
        step = pl.program_id(0)

        @pl.when(step == 0)
        def _():
            normed = norm(h_ref[...], row_of(g_ref, norm_layer), row_of(b_ref, norm_layer)).astype(BF16)
            n_ref[...] = normed
            nt_ref[...] = normed.T
            acc_ref[...] = h_ref[...] + row_of(bo_ref, layer)
            dn_ref[...] = jnp.zeros_like(dn_ref)

        inner = mm(n_ref[...], wi_ref[...]) + row_of(bi_ref, layer)
        active, slope = gelu_parts(inner)
        active = active.astype(BF16)
        acc_ref[...] += mm(active, wo_ref[...])
        up = up_ref[...]
        grad_out = mm_tn(active, up).astype(BF16)
        grad_inner = (slope * mm_nt(up, wo_ref[...])).astype(BF16)
        dbi_ref[...] = jnp.sum(grad_inner.astype(F32), 0, keepdims=True)
        store_grads(step, tiles // 2, send_ref, own_ref, mm(nt_ref[...], grad_inner).astype(BF16), grad_out)
        dn_ref[...] += mm_nt(grad_inner, wi_ref[...])

        @pl.when(step == tiles - 1)
        def _():
            out_ref[...] = acc_ref[...].astype(BF16)
            top = up_ref[...].astype(F32)
            back, grad_gain, grad_bias = norm_back(h_ref[...], row_of(g_ref, norm_layer), dn_ref[...])
            grad_ref[...] = top + back
            small_ref[...] = jnp.concatenate([grad_gain, grad_bias, jnp.sum(top, 0, keepdims=True)], 0)

    ins = [
        ("full", None, hidden), ("full", None, upstream), ("full", None, gains), ("full", None, biases),
        ("w_in", (layer, (width, tile)), w_in), ("units", (b_in.shape[0], tile), b_in),
        ("w_out", (layer, (tile, width)), w_out), ("full", None, b_out),
    ]
    half = (tiles // 2, 2, width, tile)
    outs = [
        ("all", (tokens, width), (tokens, width), BF16), ("all", (tokens, width), (tokens, width), F32),
        ("send", half, half, BF16), ("own", half, half, BF16),
        ("units", (1, tile), (1, units), F32), ("all", (3, width), (3, width), F32),
    ]
    scratch = [
        pltpu.VMEM((tokens, width), BF16), pltpu.VMEM((width, tokens), BF16),
        pltpu.VMEM((tokens, width), F32), pltpu.VMEM((tokens, width), F32),
    ]
    return grad_call(body, core, ins, outs, scratch, tiles, "ffn_both")


def ffn_back(core, upstream, grad_kvs, kv_weight, memory, hidden, normed, active, slope, gains, norm_layer, w_in, w_out, layer):
    tokens, width = hidden.shape
    units = w_in.shape[2]
    tile = width
    tiles = units // tile

    def body(_, up_ref, *refs):
        (kw_ref, mem_ref, h_ref, n_in, z_ref, s_ref, g_ref, wi_ref, wo_ref, grad_ref, dkw_ref,
         send_ref, own_ref, dbi_ref, small_ref, nt_ref, top_ref, dn_ref) = refs[len(grad_kvs) :]
        step = pl.program_id(0)

        @pl.when(step == 0)
        def _():
            nt_ref[...] = n_in[...].T
            grad_kv = added(refs[: len(grad_kvs)])
            dkw_ref[...] = mm_tn(mem_ref[...], grad_kv)
            top = up_ref[...].astype(F32) + mm_nt(grad_kv, kw_ref[...])
            grad_ref[...] = top
            top_ref[...] = top.astype(BF16)
            dn_ref[...] = jnp.zeros_like(dn_ref)

        top = top_ref[...]
        grad_out = mm_tn(z_ref[...], top).astype(BF16)
        grad_inner = (s_ref[...].astype(F32) * mm_nt(top, wo_ref[...])).astype(BF16)
        dbi_ref[...] = jnp.sum(grad_inner.astype(F32), 0, keepdims=True)
        store_grads(step, tiles // 2, send_ref, own_ref, mm(nt_ref[...], grad_inner).astype(BF16), grad_out)
        dn_ref[...] += mm_nt(grad_inner, wi_ref[...])

        @pl.when(step == tiles - 1)
        def _():
            back, grad_gain, grad_bias = norm_back(h_ref[...], row_of(g_ref, norm_layer), dn_ref[...])
            grad_ref[...] += back
            grad_top = jnp.sum(top_ref[...].astype(F32), 0, keepdims=True)
            small_ref[...] = jnp.concatenate([grad_gain, grad_bias, grad_top], 0)

    ins = [("full", None, a) for a in (upstream, *grad_kvs, kv_weight, memory, hidden, normed)] + [
        ("units", (tokens, tile), active), ("units", (tokens, tile), slope), ("full", None, gains),
        ("w_in", (layer, (width, tile)), w_in), ("w_out", (layer, (tile, width)), w_out),
    ]
    half = (tiles // 2, 2, width, tile)
    outs = [
        ("all", (tokens, width), (tokens, width), F32), ("all", (width, PAIR), (width, PAIR), F32),
        ("send", half, half, BF16), ("own", half, half, BF16),
        ("units", (1, tile), (1, units), F32), ("all", (3, width), (3, width), F32),
    ]
    scratch = [
        pltpu.VMEM((width, tokens), BF16), pltpu.VMEM((tokens, width), BF16), pltpu.VMEM((tokens, width), F32),
    ]
    return grad_call(body, core, ins, outs, scratch, tiles, "ffn_back")


def digit_of(axis, count):
    if isinstance(axis, tuple):
        return (lax.axis_index(axis[0]) >> axis[1]) & (count - 1)
    return lax.axis_index(axis)


def swap(value, axis, size, mask):
    return lax.ppermute(value, axis, [(i, i ^ mask) for i in range(size)])


def every_block(value, axis, size):
    return [value] + [swap(value, axis, size, d) for d in range(1, size)]


def give_back(blocks, axis, size):
    return [blocks[0]] + [swap(blocks[d], axis, size, d) for d in range(1, size)]


def row_chunks(rows, most=256):
    return [(at, min(most, rows - at)) for at in range(0, rows, most)]


def fold(groups, merge=False, dtype=BF16, name="fold"):
    args, outs, places = [], [], []
    total = 0
    for addends, axis, count in groups:
        rows, columns = addends[0].shape
        places.append((len(args), total))
        args += list(addends)
        total += rows // count
        if not merge:
            outs += [((rows // count, columns), dtype)] * count
    if merge:
        outs = [((total, groups[0][0][0].shape[1]), dtype)] * groups[0][2]

    def body(*refs):
        out_refs = refs[len(args) :]
        at_out = 0
        for (addends, axis, count), (at, row) in zip(groups, places):
            ins = refs[at : at + len(addends)]
            rows = ins[0].shape[0] // count
            for d in range(count):
                for start, size in row_chunks(rows):
                    place = pl.ds(d * rows + start, size)
                    if axis is not None:
                        place = pl.ds(pl.multiple_of((digit_of(axis, count) ^ d) * rows + start, 16), size)
                    part = ins[0][place].astype(F32)
                    for ref in ins[1:]:
                        part = part + ref[place].astype(F32)
                    if merge:
                        out_refs[d][row + start : row + start + size] = part.astype(dtype)
                    else:
                        out_refs[at_out + d][start : start + size] = part.astype(dtype)
            at_out += count

    outs = call(body, outs, args, name=name)
    if merge:
        return list(outs)
    result, at = [], 0
    for _, _, count in groups:
        result.append(list(outs[at : at + count]))
        at += count
    return result


def unfold(groups, sizes=None, joined=None, name="unfold"):
    args, outs, places = [], [], []
    for blocks, axis, count in groups:
        rows, columns = blocks[0].shape
        parts = sizes or [rows]
        at = 0
        for many in joined or [1] * len(parts):
            base = 0
            for size in parts[at : at + many]:
                places.append((len(outs), base))
                base += size * count
            outs.append(((base, columns), BF16))
            at += many
        args += list(blocks)

    def body(*refs):
        out_refs = refs[len(args) :]
        at = at_place = 0
        for blocks, axis, count in groups:
            ins = refs[at : at + count]
            at += count
            digit = digit_of(axis, count)
            parts = sizes or [ins[0].shape[0]]
            for d in range(count):
                row = 0
                for (out, first), size in zip(places[at_place : at_place + len(parts)], parts):
                    base = first + (digit ^ d) * size
                    for start, part in row_chunks(size):
                        place = pl.ds(pl.multiple_of(base + start, 16), part)
                        out_refs[out][place] = ins[d][row + start : row + start + part]
                    row += size
            at_place += len(parts)

    return call(body, outs, args, name=name)


def place_grads(core, own, other, layer, shapes, before, name):
    pieces = [*own, *other]
    half = len(own)
    _, _, width, tile = own[0].shape

    def body(*refs):
        parts = refs[1 : 1 + 2 * half]
        in_ref, out_ref = refs[-2:]
        for k in range(2 * half):

            @pl.when(pl.program_id(0) == k)
            def _():
                in_ref[...] = parts[k][0].astype(F32)
                out_ref[...] = parts[k][1].astype(F32)

    def unit(k, core_ref):
        near = jnp.where(k < half, core_ref[0], 1 - core_ref[0])
        return near * half + lax.rem(k, half)

    kernel = pl.pallas_call(
        body,
        grid_spec=pltpu.PrefetchScalarGridSpec(
            num_scalar_prefetch=1,
            grid=(2 * half,),
            in_specs=[pl.BlockSpec((None, 2, width, tile), lambda k, c: (0, 0, 0, 0)) for _ in pieces]
            + [pl.BlockSpec(memory_space=pl.ANY) for _ in before],
            out_specs=(
                pl.BlockSpec((None, width, tile), lambda k, c: (layer, 0, unit(k, c))),
                pl.BlockSpec((None, tile, width), lambda k, c: (layer, unit(k, c), 0)),
            ),
        ),
        out_shape=tuple(jax.ShapeDtypeStruct(shape, F32) for shape in shapes),
        input_output_aliases={1 + len(pieces) + i: i for i in range(len(before))},
        cost_estimate=cost(name),
        compiler_params=pltpu.CompilerParams(vmem_limit_bytes=VMEM_LIMIT),
        name=name,
    )
    return Order.run(kernel, [core, *pieces, *before])


def place_first(core, own, other, units):
    width = own[0].shape[2]
    return place_grads(core, own, other, 1, [(2, width, units), (2, units, width)], [], "place_first")


def place_second(core, own, other, grad_in, grad_out):
    return place_grads(core, own, other, 0, [grad_in.shape, grad_out.shape], [grad_in, grad_out], "place_second")


def place_experts(core_pairs, per, width):
    args = [part for own, other, _ in core_pairs for part in (own, other)]
    subs = sum(len(layers) for _, _, layers in core_pairs)
    half = width // 2

    def body(*refs):
        out_ref = refs[-1]
        core = lax.axis_index(CORE)
        for k, (_, _, layers) in enumerate(core_pairs):
            for place, ref in ((core, refs[2 * k]), (1 - core, refs[2 * k + 1])):
                for i, layer in enumerate(layers):
                    for expert in range(per):
                        at = (i * per + expert) * half
                        row = pl.multiple_of(place * half, half)
                        out_ref[layer, expert, pl.ds(row, half)] = ref[at : at + half].astype(F32)

    return call(body, [((subs, per, width, PAIR), F32)], args, name="place_experts")[0]


def lanes(count):
    return [slice(c * PAIR, (c + 1) * PAIR) for c in range(count)]


def pack_small(kvs, routers, rows, in_biases):
    args = [*kvs, *routers, *rows, *in_biases]
    width = kvs[0].shape[0]
    wide = width // PAIR
    units = in_biases[0].shape[1]
    used = len(kvs) * width + len(routers) * wide * EXPERTS + sum(r.shape[0] for r in rows) * wide
    used += len(in_biases) * (units // PAIR)
    total = used + -used % 1024

    def body(*refs):
        ins, outs, buffer = refs[: len(args)], refs[len(args) : -1], refs[-1]
        at = 0
        for ref in ins[: len(kvs)]:
            buffer[at : at + width] = ref[...]
            at += width
        ins = ins[len(kvs) :]
        for ref in ins[: len(routers)]:
            for lane in lanes(wide):
                buffer[at : at + EXPERTS] = ref[:, lane]
                at += EXPERTS
        for ref in ins[len(routers) :]:
            for row in range(ref.shape[0]):
                for lane in lanes(ref.shape[1] // PAIR):
                    buffer[at : at + 1] = ref[row : row + 1, lane]
                    at += 1
        buffer[at:] = jnp.zeros((total - at, PAIR), F32)
        share = total // 2
        digit = lax.axis_index(CORE)
        for d in range(2):
            outs[d][...] = buffer[pl.ds(pl.multiple_of((digit ^ d) * share, share), share)].astype(BF16)

    return call(
        body, [((total // 2, PAIR), BF16)] * 2, args, scratch=[pltpu.VMEM((total, PAIR), F32)], name="pack_small"
    )


def unpack_small(parts, counts, width, units):
    share = parts[0].shape[0]
    n_kv, n_router, picks, n_bias = counts
    wide = width // PAIR
    outs = [((n_kv, width, PAIR), F32), ((n_router, EXPERTS, width), F32)]
    outs += [((len(pick), width), F32) for pick in picks] + [((n_bias, units), F32)]
    n_rows = sum(len(pick) for pick in picks)

    def body(*refs):
        ins, outs, buffer = refs[:2], refs[2:-1], refs[-1]
        digit = lax.axis_index(CORE)
        for d in range(2):
            buffer[pl.ds(pl.multiple_of((digit ^ d) * share, share), share)] = ins[d][...].astype(F32)
        at = 0
        for i in range(n_kv):
            outs[0][i] = buffer[at : at + width]
            at += width
        for i in range(n_router):
            for lane in lanes(wide):
                outs[1][i, :, lane] = buffer[at : at + EXPERTS]
                at += EXPERTS
        for out, pick in zip(outs[2:-1], picks):
            for k, row in enumerate(pick):
                for c, lane in enumerate(lanes(wide)):
                    place = at + row * wide + c
                    out[k : k + 1, lane] = buffer[place : place + 1]
        at += n_rows * wide
        for i in range(n_bias):
            for lane in lanes(units // PAIR):
                outs[-1][i : i + 1, lane] = buffer[at : at + 1]
                at += 1

    return call(body, outs, parts, scratch=[pltpu.VMEM((2 * share, PAIR), F32)], name="unpack_small")


def after(value, *first):
    return lax.optimization_barrier((value, first))[0]


def shards(
    sizes, enc_input, dec_input, enc_segments, dec_segments, routes, enc_out_grad, dec_out_grad,
    enc_gains, enc_biases, dec_gains, dec_biases, kv_weights, router_weights, expert_weights,
    ffn_in, ffn_in_bias, ffn_out, ffn_out_bias,
):
    n_core, n_y, n_ep, n_seq = sizes[CORE], sizes[Y], sizes[EP], sizes[SEQ]
    rows, span, width = enc_input.shape
    tokens = rows * span
    per = expert_weights.shape[1]
    units = ffn_in.shape[2]
    core = lax.axis_index(CORE).astype(jnp.int32).reshape(1)
    Order.start()

    flat = lambda a: a.reshape(tokens, a.shape[-1])
    enc_x, dec_x = flat(enc_input), flat(dec_input)
    enc_up, dec_up = flat(enc_out_grad), flat(dec_out_grad)
    kv_w = [Layer(kv_weights, i) for i in range(3)]
    router_t = router_weights.transpose(0, 2, 1)
    routers = [Layer(router_t, i) for i in range(3)]

    n_one, kv_one, w_send = norm_kv(enc_x, enc_gains, enc_biases, kv_weights, 0, 0, expert_weights, [0])
    w_enc = [Layer(expert_weights, 0)] + every_block(w_send, EP, n_ep)[1:]
    kvs_one = every_block(kv_one, SEQ, n_seq)
    n_three, kv_three, *w_sends = norm_kv(dec_x, dec_gains, dec_biases, kv_weights, 0, 1, expert_weights, [1, 2])
    kv_near = swap(kv_three, SEQ, n_seq, 1)
    meta, q_rows = prepare(routes.transpose(0, 1, 3, 2), enc_segments, dec_segments, n_ep, n_seq, per)
    q_one, aux_one = queries(n_one, w_enc, routers[0], meta, 0)
    w_got = every_block(w_sends[0], EP, n_ep)
    w_dec = [Layer(expert_weights, 1)] + w_got[1:]
    o_one, lse_one, enc_mid = attend(
        enc_x, q_one, aux_one, kvs_one, w_enc, meta, q_rows, 0, 0, 0, False
    )
    w_cross = [Layer(expert_weights, 2)] + every_block(after(w_sends[1], o_one), EP, n_ep)[1:]
    kv_pair = jnp.concatenate([kv_three, after(kv_near, o_one)])
    kv_far_got = [swap(kv_pair, SEQ, n_seq, 2 * d) for d in range(1, n_seq // 2)]
    kvs_three = [kv_three, kv_near] + [Rows(got, tokens, i) for got in kv_far_got for i in range(2)]
    n_two, z_two, slope_two, memory, kv_mem = ffn_forward(
        enc_mid, enc_gains, enc_biases, 1, ffn_in, ffn_in_bias, ffn_out, ffn_out_bias, 0, kv_weights[2], 4
    )
    kvs_mem = every_block(kv_mem, SEQ, n_seq)
    q_three, aux_three = queries(n_three, w_dec, routers[1], meta, 1)
    o_three, lse_three, dec_mid = attend(
        dec_x, q_three, aux_three, kvs_three, w_dec, meta, q_rows, 1, 1, 1, True
    )
    n_four, q_four, aux_four = norm_queries(dec_mid, dec_gains, dec_biases, 1, w_cross, routers[2], meta, 2)
    o_four, lse_four, dec_late = attend(
        dec_mid, q_four, aux_four, kvs_mem, w_cross, meta, q_rows, 2, 1, 0, False
    )

    other_core = lambda a: swap(a, CORE, n_core, 1)
    two = lambda a: a.reshape(2, a.shape[0] // 2, a.shape[1])

    near, far = ((SEQ, 0), 2), ((SEQ, 1), n_seq // 2)

    def near_swap(blocks):
        return [blocks[0], swap(blocks[1], SEQ, n_seq, 1)]

    def far_swap(blocks):
        return [blocks[0]] + [swap(blocks[d], SEQ, n_seq, 2 * d) for d in range(1, far[1])]

    def kv_far(keep, got):
        return far_swap(fold([([keep, got], None, far[1])])[0])

    def z_near(groups):
        return near_swap(fold([(addends, *near) for addends in groups], merge=True))

    def z_far(parts):
        return far_swap(fold([(parts, *far)])[0])

    def z_all(parts):
        ((done,),) = fold([(parts, None, 1)])
        return far_swap([done] * far[1])

    def z_back(parts):
        (done,) = unfold([(parts, *far)])
        return near_swap([done] * 2)

    def back_second(parts):
        share = parts[0].shape[0] // 2
        a, b = unfold([(parts, *near)], [share, share])
        return every_block(a, Y, n_y), every_block(b, EP, n_ep)

    def first_parts(own, got):
        pairs = [[Layer(two(own), i), Layer(two(got), i)] for i in range(2)]
        a, b = fold([(pairs[0], EP, n_ep), (pairs[1], Y, n_y)])
        return give_back(a, EP, n_ep), give_back(b, Y, n_y)

    def second_parts(a, b):
        a, b = fold([(a, Y, n_y), (b, EP, n_ep)])
        return give_back(a, Y, n_y), give_back(b, EP, n_ep)

    def back_first(a, b):
        a, b = unfold([(a, Y, n_y), (b, EP, n_ep)])
        return every_block(a, EP, n_ep), every_block(b, Y, n_y)

    def back_core(a, b):
        parts = unfold([(a, EP, n_ep), (b, Y, n_y)])
        return list(parts), [other_core(part) for part in parts]

    dec_out, grad_late, dec_send, dec_own, dbi_dec, small_dec = ffn_both(
        core, dec_late, dec_up, dec_gains, dec_biases, 2, ffn_in, ffn_in_bias, ffn_out, ffn_out_bias, 1
    )
    half = (dec_own.shape[0] * 2 * width, dec_own.shape[3])
    dec_got = other_core(dec_send.reshape(half))
    mem_keep, mem_near, dq_four, dlog_four = attend_back(
        grad_late, o_four, q_four, aux_four, lse_four, kvs_mem, w_cross, meta, q_rows, 2, 1, 0, False
    )
    mem_near = swap(mem_near, SEQ, n_seq, 1)
    dec_a, dec_b = first_parts(dec_own.reshape(half), dec_got)
    cross_own, cross_send, dr_cross, grad_mid, small_cross = expert_back(
        grad_late, n_four, o_four, aux_four, dq_four, dlog_four, w_cross, routers[2], meta, 2,
        dec_mid, dec_gains, 1
    )
    cross_got = other_core(cross_send)
    dkv_mem = kv_far(mem_keep, mem_near)
    three_keep, three_near, dq_three, dlog_three = attend_back(
        grad_mid, o_three, q_three, aux_three, lse_three, kvs_three, w_dec, meta, q_rows, 1, 1, 1, True
    )
    three_near = swap(three_near, SEQ, n_seq, 1)
    x_cross = give_back(fold([([cross_own, cross_got], None, n_ep)], True), EP, n_ep)
    dec_a, dec_b = second_parts(dec_a, dec_b)
    grad_enc, dkw_cross, enc_send, enc_own, dbi_enc, small_enc = ffn_back(
        core, enc_up, dkv_mem, kv_w[2], memory, enc_mid, n_two, z_two, slope_two, enc_gains, 1,
        ffn_in, ffn_out, 0,
    )
    enc_got = other_core(enc_send.reshape(half))
    dkv_three = kv_far(three_keep, three_near)
    dec_parts = z_near([dec_a, dec_b])
    one_keep, one_near, dq_one, dlog_one = attend_back(
        grad_enc, o_one, q_one, aux_one, lse_one, kvs_one, w_enc, meta, q_rows, 0, 0, 0, False
    )
    one_near = swap(one_near, SEQ, n_seq, 1)
    enc_a, enc_b = first_parts(enc_own.reshape(half), enc_got)
    Order.share = LIGHT
    enc_own_x, enc_send_x, dr_enc, dn_one = expert_back(
        grad_enc, n_one, o_one, aux_one, dq_one, dlog_one, w_enc, routers[0], meta, 0
    )
    dec_own_x, dec_send_x, dr_dec, dn_three = expert_back(
        grad_mid, n_three, o_three, aux_three, dq_three, dlog_three, w_dec, routers[1], meta, 1
    )
    dkv_one = kv_far(one_keep, one_near)
    dec_parts = z_far(dec_parts)
    dec_grad, dkw_dec, small_three = self_finish(
        grad_mid, dn_three, dkv_three, n_three, kv_w[1], dec_x, dec_gains, 0
    )
    enc_grad, dkw_enc, small_one = self_finish(
        grad_enc, dn_one, dkv_one, n_one, kv_w[0], enc_x, enc_gains, 0
    )
    small_own, small_send = pack_small(
        [dkw_enc, dkw_dec, dkw_cross], [dr_enc, dr_dec, dr_cross],
        [small_one, small_enc, small_three, small_cross, small_dec], [dbi_enc, dbi_dec],
    )
    enc_a, enc_b = second_parts(enc_a, enc_b)
    dec_got_x, enc_got_x = [other_core(after(part, enc_a[0])) for part in (dec_send_x, enc_send_x)]
    Order.share = 1.0
    small_got = other_core(small_send)
    x_dec = give_back(fold([([dec_own_x, dec_got_x], None, n_ep)], True), EP, n_ep)
    dec_parts = z_all(dec_parts)
    enc_parts = z_near([enc_a, enc_b])
    n_x = enc_own_x.shape[0] // n_ep
    n_small = small_own.shape[0]
    halves = [([Rows(enc_own_x, n_x, d), Rows(enc_got_x, n_x, d)], Y, n_y) for d in range(n_ep)]
    x_two = give_back(fold(halves + [([small_own, small_got], Y, n_y)], True), Y, n_y)
    enc_parts = z_far(enc_parts)
    x_one = give_back(fold([(x_cross, Y, n_y), (x_dec, Y, n_y)], True), Y, n_y)
    dec_parts = z_back(dec_parts)
    n_x, n_small = n_x // n_y, n_small // n_y
    enc_rows = [Rows(part, n_ep * n_x, 0) for part in x_two]
    small_rows = [Rows(part, n_small, n_ep * n_x // n_small) for part in x_two]
    x_two = fold([(enc_rows, None, n_ep), (small_rows, EP, n_ep)], True)
    x_two = give_back(x_two, EP, n_ep)
    enc_parts = z_all(enc_parts)
    dec_a, dec_b = back_second(dec_parts)
    n_small = n_small // n_ep
    enc_rows = [Rows(part, n_x, 0) for part in x_two]
    small_rows = [Rows(part, n_small, n_x // n_small) for part in x_two]
    x_parts = z_near([x_one, enc_rows, small_rows])
    enc_parts = z_back(enc_parts)
    dec_a, dec_b = back_first(dec_a, dec_b)
    x_parts = z_far(x_parts)
    enc_a, enc_b = back_second(enc_parts)
    x_parts = z_all(x_parts)
    enc_a, enc_b = back_first(enc_a, enc_b)
    x_parts = z_back(x_parts)
    x_part, small_part = unfold([(x_parts, *near)], [n_x, n_x // 2, n_small // 2], [2, 1])
    x_parts, small_parts = every_block(x_part, Y, n_y), every_block(small_part, EP, n_ep)
    dec_ab, dec_other = back_core(dec_a, dec_b)
    enc_ab, enc_other = back_core(enc_a, enc_b)
    pieces = lambda parts: [part.reshape((-1, 2, width) + dec_own.shape[3:]) for part in parts]
    grad_in, grad_out = place_first(core, pieces(dec_ab), pieces(dec_other), units)
    (small_part,) = unfold([(small_parts, EP, n_ep)])
    small_parts = every_block(small_part, Y, n_y)
    (x_half,) = unfold([(x_parts, Y, n_y)], [n_x] * 3, [3])
    x_other = other_core(x_half)
    grad_in, grad_out = place_second(core, pieces(enc_ab), pieces(enc_other), grad_in, grad_out)
    (small_half,) = unfold([(small_parts, Y, n_y)])
    small_parts = every_block(small_half, CORE, n_core)
    experts = place_experts([(x_half, x_other, (2, 1, 0))], per, width)
    picks = [[0, 2], [1, 3], [5, 7, 9], [6, 8, 10], [4, 11]]
    kv_grad, router_grad, enc_gain, enc_bias, dec_gain, dec_bias, out_bias, in_bias = unpack_small(
        small_parts, (3, 3, picks, 2), width, units
    )
    shape = enc_input.shape
    return (
        memory.reshape(shape), dec_out.reshape(shape), enc_grad.reshape(shape), dec_grad.reshape(shape),
        enc_gain, enc_bias, dec_gain, dec_bias, kv_grad, router_grad.transpose(0, 2, 1), experts,
        grad_in, in_bias, grad_out, out_bias,
    )


def solution(mesh):
    sizes = dict(mesh.shape)
    n_dp, n_ep, n_seq = sizes["dp"], sizes[EP], sizes[SEQ]
    split = jax.sharding.Mesh(mesh.devices.reshape(n_dp // 2, 2, n_ep, n_seq), (Y, CORE, EP, SEQ))
    batch = (Y, CORE, EP)
    tokens = P(batch, SEQ, None)
    rows = P(batch, None)
    experts = P(None, EP, None, None)
    return jax.shard_map(
        partial(shards, dict(split.shape)),
        mesh=split,
        in_specs=(
            tokens, tokens, rows, rows, P(None, batch, SEQ, None), tokens, tokens,
            P(), P(), P(), P(), P(), P(), experts, P(), P(), P(), P(),
        ),
        out_specs=(
            tokens, tokens, tokens, tokens, P(), P(), P(), P(), P(), P(), experts, P(), P(), P(), P(),
        ),
        check_vma=False,
    )
```
